128 devices in a mesh: pat: 16 (over z_hi, y, core), code: 8 (over z_lo, x).
Axes of the slice: x: 4, y: 4, z: 4 (z_hi: 2, z_lo: 2; z = z_hi * 2 + z_lo), core: 2. Of those that a mesh axis runs over, the one named last changes fastest.
Arguments:
- tile_data: bfloat16 [16, 8, 16, 128, 512], P('pat', 'code'), may hold values from 0 to 7, as said below
- tile_list: int32 [16, 8, 3, 16], P('pat', 'code'), may hold values from 0 to 31, as said below
- tile_count: int32 [16, 8], P('pat', 'code'), may hold values from 8 to 16, as said below
- visit_counts: int32 [512], P('pat'), may hold values from 1 to 256, as said below
- code_factor_t: float32 [64, 65536], P(None, 'code'), may hold values from 0.004 to 0.33, as said below
- visit_mix: float32 [64, 64], replicated, may hold values from -0.15 to 1.2
- patient_weight: float32 [512, 64], P('pat'), may hold values from 0.5 to 30, as said below
Outputs:
- code_factor_new: float32 [64, 65536], P(None, 'code')
- mix_new: float32 [64, 64], replicated
- patient_weight_new: float32 [512, 64], P(('pat', 'code'))
The draws below stay inside these ranges and needn't reach their ends.
Inputs may be any that keep to these rules, and one draw needn't show every extreme that they name: `tile_list`: for device (p, c) and slot t: entry 0 is a patient of pat index p (0 to 31), entry 1 a visit block below that patient's visits divided by 128 and rounded up, entry 2 a code block of code index c (0 to 15). A triple may repeat; such tiles add. `tile_count`: slots at or past a device's count are not in use; some device uses all slots. `visit_counts`: some patient has 256 visits. `tile_data`: Whole-number counts. Rows past the patient's visit count and slots not in use hold left-over values that are not part of the data. `code_factor_t`: Positive. `patient_weight`: Positive.
All inputs are finite; a program needn't handle non-finite values.
Results may differ from the reference program's by a relative error of at most 0.0073.
Values may be sent and summed in bfloat16 or wider, within the bound.
No kernel may reach another device: no remote copies, remote signals or barrier semaphores. Data moves between devices by JAX's collectives and lax.ppermute only.
A program may use at most 64 MiB of HBM per device.

```python
import jax
import jax.numpy as jnp
from jax import lax

RANK = 64
CODES = 65536
TILE_V = 128
TILE_C = 512
VBLOCKS = 2
NS_STEPS = 8
TILES_DEV = 16
PAT_ROW = 32
PATIENTS = 512
CB_DEV = 16
VMAX = 256
N_PAT = 16
N_CODE = 8


def visit_helper(key):
    base_counts = jax.random.randint(jax.random.fold_in(key, 11), (PATIENTS,), 1, VMAX + 1)
    chosen = jax.random.randint(jax.random.fold_in(key, 12), (), 0, PATIENTS)
    return jnp.where(jnp.arange(PATIENTS) == chosen, VMAX, base_counts).astype(jnp.int32)


def draw_visit_counts(key, part):
    return visit_helper(key)


def draw_tile_list(key, part):
    visits = visit_helper(key)
    shape_all = (N_PAT, N_CODE, TILES_DEV)
    owners = jax.random.randint(jax.random.fold_in(key, 21), shape_all, 0, PAT_ROW)
    global_owner = owners + (jnp.arange(N_PAT) * PAT_ROW)[:, None, None]
    block_limit = (visits[global_owner] + TILE_V - 1) // TILE_V
    visit_block = jax.random.randint(jax.random.fold_in(key, 22), shape_all, 0, block_limit)
    code_block = jax.random.randint(jax.random.fold_in(key, 23), shape_all, 0, CB_DEV)
    return jnp.stack([owners, visit_block, code_block], axis=2).astype(jnp.int32)


def draw_tile_count(key, part):
    counts = jax.random.randint(jax.random.fold_in(key, 31), (N_PAT, N_CODE), TILES_DEV // 2, TILES_DEV + 1)
    chosen = jax.random.randint(jax.random.fold_in(key, 32), (), 0, N_PAT * N_CODE)
    flat_index = jnp.arange(N_PAT * N_CODE).reshape(N_PAT, N_CODE)
    return jnp.where(flat_index == chosen, TILES_DEV, counts).astype(jnp.int32)


def draw_tile_data(key, part):
    shape_all = (N_PAT, N_CODE, TILES_DEV, TILE_V, TILE_C)
    values = jax.random.randint(jax.random.fold_in(key, 41), shape_all, 0, 4)
    present = jax.random.randint(jax.random.fold_in(key, 42), shape_all, 0, 2) == 0
    return jnp.where(present, values, 0).astype(jnp.float32).astype(jnp.bfloat16)


def draw_code_factor_t(key, part):
    position = jnp.arange(CODES, dtype=jnp.float32) / CODES
    growth = 3.0 ** position
    base_values = jax.random.uniform(jax.random.fold_in(key, 51), (RANK, CODES), jnp.float32, 0.5, 1.5)
    return 0.02 * base_values * growth[None, :]


def draw_visit_mix(key, part):
    eye_mat = jnp.eye(RANK, dtype=jnp.float32)
    offdiag = jax.random.uniform(jax.random.fold_in(key, 61), (RANK, RANK), jnp.float32, -0.15, 0.15)
    diag_values = jax.random.uniform(jax.random.fold_in(key, 62), (RANK,), jnp.float32, 0.95, 1.05)
    return offdiag * (1.0 - eye_mat) + eye_mat * diag_values[None, :]


def draw_patient_weight(key, part):
    position = jnp.arange(PATIENTS, dtype=jnp.float32) / PATIENTS
    growth = 3.0 ** position
    base_values = jax.random.uniform(jax.random.fold_in(key, 71), (PATIENTS, RANK), jnp.float32, 0.5, 1.5)
    return base_values * growth[:, None]


def setup_inputs(seed: int = 0) -> dict:
    key_list = jax.random.split(jax.random.key(seed), 8)
    return {
        "tile_data": draw_tile_data(jax.random.fold_in(key_list[7], 71), 0),
        "tile_list": draw_tile_list(jax.random.fold_in(key_list[7], 71), 0),
        "tile_count": draw_tile_count(jax.random.fold_in(key_list[7], 71), 0),
        "visit_counts": draw_visit_counts(jax.random.fold_in(key_list[7], 71), 0),
        "code_factor_t": draw_code_factor_t(jax.random.fold_in(key_list[7], 71), 0),
        "visit_mix": draw_visit_mix(jax.random.fold_in(key_list[7], 71), 0),
        "patient_weight": draw_patient_weight(jax.random.fold_in(key_list[7], 71), 0),
    }


highest = lax.Precision.HIGHEST
damping = 0.1
epsilon = 1e-06

def damped_solve(gram, right):
    eye_mat = jnp.eye(gram.shape[0], dtype=gram.dtype)
    shifted = gram + damping * jnp.mean(jnp.diagonal(gram)) * eye_mat
    return jnp.linalg.solve(shifted, right)

def newton_schulz(target):
    norm_sq = lax.optimization_barrier(jnp.sum(target * target, axis=(1, 2, 3), keepdims=True))
    iterate = target / jnp.sqrt(norm_sq + epsilon)
    for step_number in range(NS_STEPS):
        inner_gram = jnp.einsum('kbrv,kbsv->krs', iterate, iterate, precision=highest)
        iterate = 1.5 * iterate - 0.5 * jnp.einsum('krs,kbsv->kbrv', inner_gram, iterate, precision=highest)
    return iterate

def keep_rows(owners, visit_block, live_count, visits_row, slot_total, tile_rows):
    match = owners[:, None] == jnp.arange(visits_row.shape[0], dtype=jnp.int32)[None, :]
    own_visits = lax.optimization_barrier(jnp.sum(jnp.where(match, visits_row[None, :], 0), axis=1))
    row_index = visit_block[:, None] * tile_rows + jnp.arange(tile_rows, dtype=jnp.int32)[None, :]
    in_use = jnp.arange(slot_total, dtype=jnp.int32) < live_count
    return (row_index < own_visits[:, None]) & in_use[:, None]

def reference(tile_data, tile_list, tile_count, visit_counts, code_factor_t, visit_mix, patient_weight):
    code_blocks = code_factor_t.astype(jnp.bfloat16).reshape(RANK, N_CODE * CB_DEV, TILE_C).astype(jnp.float32)
    segment_total = PAT_ROW * VBLOCKS

    def load_device(device_id):
        pat_at = device_id // N_CODE
        code_at = device_id % N_CODE
        tile_slab = tile_data[pat_at, code_at]
        listing = tile_list[pat_at, code_at]
        visits_row = lax.dynamic_slice_in_dim(visit_counts, pat_at * PAT_ROW, PAT_ROW, 0)
        keep_mask = keep_rows(listing[0], listing[1], tile_count[pat_at, code_at], visits_row, TILES_DEV, TILE_V)
        masked = jnp.where(keep_mask[:, :, None], tile_slab, jnp.zeros((), tile_slab.dtype)).astype(jnp.float32)
        return (pat_at, code_at, listing, masked)

    def gather_products(running, device_id):
        pat_at, code_at, listing, masked = load_device(device_id)
        picked = jnp.take(code_blocks, code_at * CB_DEV + listing[2], axis=1)
        contrib = jnp.einsum('rtc,tvc->trv', picked, masked, precision=highest)
        partial_value = jax.ops.segment_sum(contrib, listing[0] * VBLOCKS + listing[1], num_segments=segment_total)
        offset = pat_at * segment_total
        updated = lax.dynamic_slice_in_dim(running, offset, segment_total, 0) + partial_value
        return (lax.dynamic_update_slice_in_dim(running, updated, offset, 0), None)
    device_ids = jnp.arange(N_PAT * N_CODE, dtype=jnp.int32)
    flat_products, unused = lax.scan(gather_products, jnp.zeros((PATIENTS * VBLOCKS, RANK, TILE_V), jnp.float32), device_ids)
    products = flat_products.reshape(PATIENTS, VBLOCKS, RANK, TILE_V)
    code_gram = jnp.dot(code_factor_t, code_factor_t.T, precision=highest)
    target = jnp.einsum('rs,ks,kbsv->kbrv', visit_mix, patient_weight, products, precision=highest)
    polar_factor = newton_schulz(target)
    projected = jnp.einsum('kbrv,kbsv->krs', polar_factor, products, precision=highest)
    mix_numer = jnp.einsum('kis,ks->is', projected, patient_weight, precision=highest)
    weight_gram = jnp.dot(patient_weight.T, patient_weight, precision=highest)
    mix_new = damped_solve(code_gram * weight_gram, mix_numer.T).T
    mix_gram = jnp.dot(mix_new.T, mix_new, precision=highest)
    diag_terms = jnp.einsum('is,kis->ks', mix_new, projected, precision=highest)
    weight_new = jnp.maximum(damped_solve(mix_gram * code_gram, diag_terms.T).T, 0.0)
    spread = (jnp.einsum('is,kbiv->kbsv', mix_new, polar_factor, precision=highest) * weight_new[:, None, :, None]).astype(jnp.bfloat16)
    spread_flat = spread.reshape(PATIENTS * VBLOCKS, RANK, TILE_V).astype(jnp.float32)

    def gather_numer(running, device_id):
        pat_at, code_at, listing, masked = load_device(device_id)
        rows_used = (pat_at * PAT_ROW + listing[0]) * VBLOCKS + listing[1]
        picked = jnp.take(spread_flat, rows_used, axis=0)
        contrib = jnp.einsum('trv,tvc->trc', picked, masked, precision=highest)
        partial_value = jax.ops.segment_sum(contrib, listing[2], num_segments=CB_DEV)
        offset = code_at * CB_DEV
        updated = lax.dynamic_slice_in_dim(running, offset, CB_DEV, 1) + jnp.transpose(partial_value, (1, 0, 2))
        return (lax.dynamic_update_slice_in_dim(running, updated, offset, 1), None)
    numer_sums, unused = lax.scan(gather_numer, jnp.zeros((RANK, N_CODE * CB_DEV, TILE_C), jnp.float32), device_ids)
    weight_gram_new = jnp.dot(weight_new.T, weight_new, precision=highest)
    code_new = jnp.maximum(damped_solve(mix_gram * weight_gram_new, numer_sums.reshape(RANK, CODES)), 0.0)
    return (code_new, mix_new, weight_new)
```

```python
import jax
import jax.numpy as jnp
from jax import lax
from jax.experimental import pallas as pl
from jax.experimental.pallas import tpu as pltpu
from jax.sharding import PartitionSpec as P

VBLOCKS = 2
NS_STEPS = 8
damping = 0.1
epsilon = 1e-06
F32, BF16, F16 = jnp.float32, jnp.bfloat16, jnp.float16
VM = pl.BlockSpec(memory_space=pltpu.VMEM)
SM = pl.BlockSpec(memory_space=pltpu.SMEM)
PARAMS = pltpu.CompilerParams(vmem_limit_bytes=48 * 1024 * 1024)


def mm(a, b, dims=((1,), (0,))):
    return lax.dot_general(
        a, b, (dims, ((), ())), precision=lax.Precision.HIGHEST, preferred_element_type=F32
    )


def mm16(a, b, dims=((1,), (0,))):
    return lax.dot_general(a, b, (dims, ((), ())), preferred_element_type=F32)


NT = ((1,), (1,))
TN = ((0,), (0,))


def split(x):
    high = x.astype(BF16)
    return high, (x - high.astype(F32)).astype(BF16)


def fold(x):
    half = x.shape[1] // 2
    return x[:, :half] + x[:, half:]


def damped_inverse(gram):
    size = gram.shape[0]
    eye = lax.broadcasted_iota(jnp.int32, (size, size), 0) == lax.broadcasted_iota(
        jnp.int32, (size, size), 1
    )
    mean = jnp.sum(jnp.where(eye, gram, 0.0), keepdims=True) / size
    work = jnp.concatenate(
        [gram + jnp.where(eye, damping * mean, 0.0), eye.astype(F32)], axis=1
    )
    row_at = lax.broadcasted_iota(jnp.int32, work.shape, 0)
    for j in range(size):
        row = work[j : j + 1, :]
        row = row / row[:, j : j + 1]
        work = jnp.where(row_at == j, row, work - work[:, j : j + 1] * row)
    return work[:, size:]


def live_rows(t, list_ref, count_ref, visits_ref, tile_rows):
    k, b, g = list_ref[0, t], list_ref[1, t], list_ref[2, t]
    kept = jnp.where(t < count_ref[0, 0], visits_ref[k] - tile_rows * b, 0)
    return k, b, g, kept


def products_kernel(list_ref, count_ref, visits_ref, tile_ref, code_ref, out_ref):
    slots, rows, cols = tile_ref.shape
    rank = code_ref.shape[0]
    out_ref[...] = jnp.zeros(out_ref.shape, F32)
    lane = lax.broadcasted_iota(jnp.int32, (rank, rows), 1)
    for t in range(slots):
        k, b, g, kept = live_rows(t, list_ref, count_ref, visits_ref, rows)
        codes = code_ref[:, pl.ds(pl.multiple_of(g * cols, cols), cols)].astype(BF16)
        part = mm16(codes, tile_ref[t], NT)
        out_ref[k * VBLOCKS + b] += jnp.where(lane < kept, part, 0.0)


def gram_kernel(code_ref, out_ref):
    high, low = split(code_ref[...])
    cross = mm16(high, low, NT)
    high, low = split(mm16(high, high, NT) + cross + cross.T)
    out_ref[...] = jnp.concatenate([high, low], axis=1)


def polar_kernel(at_ref, prod_ref, mix_ref, weight_ref, gram_ref, out_ref):
    dests = out_ref.shape[0]
    segs, rank, rows = prod_ref.shape
    own = segs // VBLOCKS
    prods = [
        jnp.concatenate([prod_ref[VBLOCKS * j + b] for b in range(VBLOCKS)], axis=1)
        for j in range(own)
    ]
    zs = []
    for j in range(own):
        weight = weight_ref[pl.ds(at_ref[0] * own + j, 1), :]
        target = mm(mix_ref[...] * weight, prods[j])
        zs.append(target / jnp.sqrt(jnp.sum(target * target, keepdims=True) + epsilon))
    for _ in range(NS_STEPS):
        grams = [mm(z, z, NT) for z in zs]
        zs = [1.5 * z - 0.5 * mm(g, z) for g, z in zip(grams, zs)]
    pieces = []
    for z in zs:
        z = z.astype(BF16)
        pieces += [z[:, b * rows : (b + 1) * rows] for b in range(VBLOCKS)]
    for z, p in zip(zs, prods):
        pieces.append(jnp.concatenate(split(mm(z, p, NT)), axis=1))
    pieces.append(gram_ref[...])
    for d in range(dests):
        for i, piece in enumerate(pieces):
            out_ref[d, i * rank : (i + 1) * rank, :] = piece


def numer_kernel(got_ref, weight_ref, out_ref):
    sources = got_ref.shape[0]
    rank = out_ref.shape[0]
    own = weight_ref.shape[0] // sources
    first = own * VBLOCKS * rank
    weight = weight_ref[...]
    twice = jnp.concatenate([weight, weight], axis=1)
    total = jnp.zeros(out_ref.shape, F32)
    for d in range(sources):
        for j in range(own):
            at = first + j * rank
            k = d * own + j
            total += got_ref[d, at : at + rank, :].astype(F32) * twice[k : k + 1, :]
    out_ref[...] = jnp.concatenate([fold(total), mm(weight, weight, TN)], axis=1)


def update_kernel(
    place_ref, list_ref, count_ref, visits_ref, sum_a, sum_b, got_ref, tile_ref,
    keep_ref, send_ref, wgram_ref, mix_ref, mgram_ref, own_ref, acc_ref, all_ref,
):
    sources = got_ref.shape[0]
    slots, rows, cols = tile_ref.shape
    rank = mix_ref.shape[0]
    patients = all_ref.shape[0]
    own = patients // sources
    first = own * VBLOCKS * rank
    last = first + own * rank
    sums = sum_a[...] + sum_b[...]
    code_gram = got_ref[0, last : last + rank, :].astype(F32)
    for d in range(1, sources):
        code_gram += got_ref[d, last : last + rank, :].astype(F32)
    code_gram = fold(code_gram)
    mix = mm(sums[:, :rank], damped_inverse(code_gram * sums[:, rank:]))
    mix_ref[...] = mix
    mix_gram = mm(mix, mix, TN)
    mgram_ref[...] = mix_gram
    inverse = damped_inverse(mix_gram * code_gram)
    twice = jnp.concatenate([mix, mix], axis=1)
    terms = []
    for d in range(sources):
        for j in range(own):
            at = first + j * rank
            terms.append(
                jnp.sum(got_ref[d, at : at + rank, :].astype(F32) * twice, axis=0, keepdims=True)
            )
    weight = jnp.maximum(mm(fold(jnp.concatenate(terms, axis=0)), inverse), 0.0)
    all_ref[...] = weight
    for j in range(own):
        own_ref[j : j + 1, :] = all_ref[pl.ds(place_ref[0] * own + j, 1), :]
    gram = mm(weight, weight, TN)
    wgram_ref[...] = jnp.concatenate([gram, jnp.zeros_like(gram)], axis=1)
    acc_ref[...] = jnp.zeros(acc_ref.shape, F32)
    lane = lax.broadcasted_iota(jnp.int32, (rank, rows), 1)
    for t in range(slots):
        k, b, g, kept = live_rows(t, list_ref, count_ref, visits_ref, rows)
        high, low = split(mix * all_ref[pl.ds(k, 1), :])
        at = pl.multiple_of((lax.rem(k, own) * VBLOCKS + b) * rank, rank)
        polar = got_ref[lax.div(k, own), pl.ds(at, rank), :]
        spread = mm16(high, polar, TN) + mm16(low, polar, TN)
        spread = jnp.where(lane < kept, spread, 0.0).astype(BF16)
        acc_ref[g] += mm16(spread, tile_ref[t])
    parity = place_ref[1]
    for j in range(keep_ref.shape[0]):
        keep_ref[j] = acc_ref[2 * j + parity]
        send_ref[j] = acc_ref[2 * j + 1 - parity]


def pair_kernel(keep_ref, came_ref, gram_a, gram_b, out_ref):
    lanes = gram_a.shape[1]
    slabs = keep_ref.shape[2] // lanes
    rank = gram_a.shape[0]
    high, low = split(gram_a[...] + gram_b[...])
    piece = jnp.concatenate([high[:, :rank], low[:, :rank]], axis=1)
    for j in range(keep_ref.shape[0]):
        both = (keep_ref[j] + came_ref[j]).astype(BF16)
        for i in range(slabs):
            out_ref[j, i] = both[:, i * lanes : (i + 1) * lanes]
        out_ref[j, slabs] = piece


def factor_kernel(got_ref, mgram_ref, out_ref):
    sources, slabs = got_ref.shape[0], got_ref.shape[1] - 1
    sums = []
    for i in range(slabs + 1):
        total = got_ref[0, i].astype(F32)
        for d in range(1, sources):
            total += got_ref[d, i].astype(F32)
        sums.append(total)
    inverse = damped_inverse(mgram_ref[...] * fold(sums[slabs]))
    code = jnp.maximum(mm(inverse, jnp.concatenate(sums[:slabs], axis=1)), 0.0).astype(BF16)
    for d in range(sources):
        out_ref[d] = code


def place_kernel(place_ref, mine_ref, came_ref, out_ref):
    parity = place_ref[1]
    cols = mine_ref.shape[2]
    for j in range(mine_ref.shape[0]):
        at = pl.multiple_of((2 * j + parity) * cols, cols)
        out_ref[:, pl.ds(at, cols)] = mine_ref[j].astype(F32)
        at = pl.multiple_of((2 * j + 1 - parity) * cols, cols)
        out_ref[:, pl.ds(at, cols)] = came_ref[j].astype(F32)


def call(kernel, outs, specs, args, scratch=()):
    many = isinstance(outs, tuple)
    return pl.pallas_call(
        kernel,
        out_shape=outs,
        in_specs=specs,
        out_specs=(VM,) * len(outs) if many else VM,
        scratch_shapes=scratch,
        compiler_params=PARAMS,
    )(*args)


def body(tile_data, tile_list, tile_count, visit_counts, code_factor_t, visit_mix, patient_weight):
    tiles = tile_data[0, 0]
    listing = tile_list[0, 0]
    slots, rows, cols = tiles.shape
    rank = visit_mix.shape[0]
    patients = visit_counts.shape[0]
    n_code, n_pat = lax.axis_size("code"), lax.axis_size("pat")
    half = n_pat // 2
    own = patients // n_code
    code_at, pat_at = lax.axis_index("code"), lax.axis_index("pat")
    place = jnp.stack([code_at, lax.rem(pat_at, 2)]).astype(jnp.int32)
    shape = jax.ShapeDtypeStruct

    partial = call(
        products_kernel, shape((patients * VBLOCKS, rank, rows), F32),
        [SM, SM, SM, VM, VM], (listing, tile_count, visit_counts, tiles, code_factor_t),
    )
    sent = partial.astype(F16).reshape(n_code, own * VBLOCKS * rank, rows)
    got = lax.all_to_all(sent, "code", 0, 0, tiled=True)
    gram = call(gram_kernel, shape((rank, 2 * rank), BF16), [VM], (code_factor_t,))
    products = jnp.sum(got.astype(F32), axis=0).reshape(own * VBLOCKS, rank, rows)

    length = (own * VBLOCKS + own + 1) * rank
    message = call(
        polar_kernel, shape((n_code, length, rows), BF16),
        [SM, VM, VM, VM, VM], (place, products, visit_mix, patient_weight, gram),
    )
    shared = lax.all_to_all(message, "code", 0, 0, tiled=True)
    sums = call(numer_kernel, shape((rank, 2 * rank), F32), [VM, VM], (shared, patient_weight))

    def swap(x, bit):
        return lax.ppermute(x, "pat", [(i, i ^ bit) for i in range(n_pat)])

    around = [swap(sums, bit) for bit in (2, 4, 6)]
    sums = sums + around[0] + around[1] + around[2]
    sums = sums + swap(sums, 8)
    other = swap(sums, 1)
    keep, send, wgram, mix_new, mix_gram, weight_new = call(
        update_kernel,
        (
            shape((half, rank, cols), F32), shape((half, rank, cols), F32),
            shape((rank, 2 * rank), F32), shape((rank, rank), F32),
            shape((rank, rank), F32), shape((own, rank), F32),
        ),
        [SM, SM, SM, SM, VM, VM, VM, VM],
        (place, listing, tile_count, visit_counts, sums, other, shared, tiles),
        [pltpu.VMEM((n_pat, rank, cols), F32), pltpu.VMEM((patients, rank), F32)],
    )
    came, wgram_came = swap(send, 1), swap(wgram, 1)
    lanes = 2 * rank
    packed = call(
        pair_kernel, shape((half, cols // lanes + 1, rank, lanes), BF16),
        [VM] * 4, (keep, came, wgram, wgram_came),
    )
    groups = [[core + 2 * i for i in range(half)] for core in (0, 1)]

    def exchange(x):
        return lax.all_to_all(x, "pat", 0, 0, axis_index_groups=groups, tiled=True)

    code = call(
        factor_kernel, shape((half, rank, cols), BF16), [VM, VM], (exchange(packed), mix_gram)
    )
    mine = exchange(code)
    code_new = call(
        place_kernel, shape((rank, n_pat * cols), F32), [SM, VM, VM], (place, mine, swap(mine, 1))
    )
    return (code_new, mix_new, weight_new)


def solution(mesh):
    placed = (
        P("pat", "code", None, None, None),
        P("pat", "code", None, None),
        P("pat", "code"),
        P("pat"),
        P(None, "code"),
        P(),
        P("pat", None),
    )
    return jax.shard_map(
        body,
        mesh=mesh,
        in_specs=placed,
        out_specs=(P(None, "code"), P(), P(("pat", "code"), None)),
        check_vma=False,
    )
```

```python
import jax
import jax.numpy as jnp
from jax import lax
from jax.experimental import pallas as pl
from jax.experimental.pallas import tpu as pltpu
from jax.sharding import PartitionSpec as P

VBLOCKS = 2
NS_STEPS = 8
damping = 0.1
epsilon = 1e-06
F32, BF16, F16 = jnp.float32, jnp.bfloat16, jnp.float16
VM = pl.BlockSpec(memory_space=pltpu.VMEM)
SM = pl.BlockSpec(memory_space=pltpu.SMEM)
PARAMS = pltpu.CompilerParams(vmem_limit_bytes=48 * 1024 * 1024)


def mm(a, b, dims=((1,), (0,))):
    return lax.dot_general(
        a, b, (dims, ((), ())), precision=lax.Precision.HIGHEST, preferred_element_type=F32
    )


def mm16(a, b, dims=((1,), (0,))):
    return lax.dot_general(a, b, (dims, ((), ())), preferred_element_type=F32)


NT = ((1,), (1,))
TN = ((0,), (0,))


def split(x):
    high = x.astype(BF16)
    return high, (x - high.astype(F32)).astype(BF16)


def fold(x):
    half = x.shape[1] // 2
    return x[:, :half] + x[:, half:]


def times2(x, y):
    return [[x[i][0] * y[0][j] + x[i][1] * y[1][j] for j in (0, 1)] for i in (0, 1)]


def flip2(x):
    return [[x[0][0], x[1][0]], [x[0][1], x[1][1]]]


def inverse2(x):
    r = 1.0 / (x[0][0] * x[1][1] - x[0][1] * x[1][0])
    return [[x[1][1] * r, -x[0][1] * r], [-x[1][0] * r, x[0][0] * r]]


def inverse4(p):
    a = [[p[0][0], p[0][1]], [p[0][1], p[1][1]]]
    b = [[p[0][2], p[0][3]], [p[1][2], p[1][3]]]
    ai = inverse2(a)
    t = times2(ai, b)
    bt = times2(flip2(b), t)
    si = inverse2([[p[2][2] - bt[0][0], p[2][3] - bt[0][1]], [p[2][3] - bt[1][0], p[3][3] - bt[1][1]]])
    r = times2(t, si)
    u = times2(r, flip2(t))
    return [
        [ai[0][0] + u[0][0], ai[0][1] + u[0][1], -r[0][0], -r[0][1]],
        [ai[1][0] + u[1][0], ai[1][1] + u[1][1], -r[1][0], -r[1][1]],
        [-r[0][0], -r[1][0], si[0][0], si[0][1]],
        [-r[0][1], -r[1][1], si[1][0], si[1][1]],
    ]


def damped_inverse(gram):
    size = gram.shape[0]
    eye = lax.broadcasted_iota(jnp.int32, (size, size), 0) == lax.broadcasted_iota(
        jnp.int32, (size, size), 1
    )
    mean = jnp.sum(jnp.where(eye, gram, 0.0), keepdims=True) / size
    work = jnp.concatenate(
        [gram + jnp.where(eye, damping * mean, 0.0), eye.astype(F32)], axis=1
    )
    lanes = 2 * size
    blocks = [work[i : i + 8] for i in range(0, size, 8)]
    row_at = lax.broadcasted_iota(jnp.int32, (8, lanes), 0)
    for j in range(0, size, 4):
        owner, at = j // 8, j % 8
        rows = [blocks[owner][at + i : at + i + 1] for i in range(4)]
        pivot = [
            [jnp.broadcast_to(row[:, j + k : j + k + 1], (1, lanes)) for k in range(4)]
            for row in rows
        ]
        inverse = inverse4(pivot)
        fresh = []
        for i in range(4):
            total = inverse[i][0] * rows[0]
            for k in range(1, 4):
                total = total + inverse[i][k] * rows[k]
            fresh.append(total)
        after = []
        for m, block in enumerate(blocks):
            value = block
            for k in range(4):
                value = value - block[:, j + k : j + k + 1] * fresh[k]
            if m == owner:
                for k in range(4):
                    value = jnp.where(row_at == at + k, fresh[k], value)
            after.append(value)
        blocks = after
    return jnp.concatenate(blocks, axis=0)[:, size:]


def live_rows(t, list_ref, count_ref, visits_ref, tile_rows):
    k, b, g = list_ref[0, t], list_ref[1, t], list_ref[2, t]
    kept = jnp.where(t < count_ref[0, 0], visits_ref[k] - tile_rows * b, 0)
    return k, b, g, kept


def products_kernel(list_ref, count_ref, visits_ref, tile_ref, code_ref, out_ref):
    slots, rows, cols = tile_ref.shape
    rank = code_ref.shape[0]
    out_ref[...] = jnp.zeros(out_ref.shape, F32)
    lane = lax.broadcasted_iota(jnp.int32, (rank, rows), 1)
    for t in range(slots):
        k, b, g, kept = live_rows(t, list_ref, count_ref, visits_ref, rows)
        codes = code_ref[:, pl.ds(pl.multiple_of(g * cols, cols), cols)].astype(BF16)
        part = mm16(codes, tile_ref[t], NT)
        out_ref[k * VBLOCKS + b] += jnp.where(lane < kept, part, 0.0)


def gram_kernel(code_ref, weight_ref, code_gram_ref, weight_gram_ref):
    high, low = split(code_ref[...])
    cross = mm16(high, low, NT)
    code_gram_ref[...] = mm16(high, high, NT) + cross + cross.T
    weight = weight_ref[...]
    weight_gram_ref[...] = mm(weight, weight, TN)


def inverse_kernel(a_ref, b_ref, out_ref):
    out_ref[...] = damped_inverse(a_ref[...] * b_ref[...])


def polar_kernel(at_ref, prod_ref, mix_ref, weight_ref, numer_ref, out_ref):
    dests = out_ref.shape[0]
    segs, rank, rows = prod_ref.shape
    own = segs // VBLOCKS
    prods = [
        jnp.concatenate([prod_ref[VBLOCKS * j + b] for b in range(VBLOCKS)], axis=1)
        for j in range(own)
    ]
    weights = [weight_ref[pl.ds(at_ref[0] * own + j, 1), :] for j in range(own)]
    zs = []
    for j in range(own):
        target = mm(mix_ref[...] * weights[j], prods[j])
        zs.append(target / jnp.sqrt(jnp.sum(target * target, keepdims=True) + epsilon))
    for _ in range(NS_STEPS):
        grams = [mm(z, z, NT) for z in zs]
        zs = [1.5 * z - 0.5 * mm(g, z) for g, z in zip(grams, zs)]
    pieces = []
    for z in zs:
        z = z.astype(BF16)
        pieces += [z[:, b * rows : (b + 1) * rows] for b in range(VBLOCKS)]
    numer = jnp.zeros((rank, rank), F32)
    for z, p, weight in zip(zs, prods, weights):
        projected = mm(z, p, NT)
        numer += projected * weight
        pieces.append(jnp.concatenate(split(projected), axis=1))
    numer_ref[...] = jnp.concatenate([numer[: rank // 2], numer[rank // 2 :]], axis=1)
    for d in range(dests):
        for i, piece in enumerate(pieces):
            out_ref[d, i * rank : (i + 1) * rank, :] = piece


def mix_kernel(sum_a, sum_b, inverse_ref, code_gram_ref, mix_ref, mgram_ref, out_ref):
    sums = sum_a[...] + sum_b[...]
    rank = mix_ref.shape[0]
    numer = jnp.concatenate([sums[:, :rank], sums[:, rank:]], axis=0)
    mix = mm(numer, inverse_ref[...])
    mix_ref[...] = mix
    mix_gram = mm(mix, mix, TN)
    mgram_ref[...] = mix_gram
    out_ref[...] = damped_inverse(mix_gram * code_gram_ref[...])


def weight_kernel(place_ref, got_ref, mix_ref, inverse_ref, weight_ref, wgram_ref, own_ref):
    sources = got_ref.shape[0]
    rank = mix_ref.shape[0]
    own = own_ref.shape[0]
    first = own * VBLOCKS * rank
    mix = mix_ref[...]
    twice = jnp.concatenate([mix, mix], axis=1)
    terms = []
    for d in range(sources):
        for j in range(own):
            at = first + j * rank
            terms.append(
                jnp.sum(got_ref[d, at : at + rank, :].astype(F32) * twice, axis=0, keepdims=True)
            )
    weight = jnp.maximum(mm(fold(jnp.concatenate(terms, axis=0)), inverse_ref[...]), 0.0)
    weight_ref[...] = weight
    for j in range(own):
        own_ref[j : j + 1, :] = weight_ref[pl.ds(place_ref[0] * own + j, 1), :]
    wgram_ref[...] = mm(weight, weight, TN)


def numer_kernel(
    place_ref, list_ref, count_ref, visits_ref, got_ref, mix_ref, weight_ref, tile_ref,
    keep_ref, send_ref, acc_ref,
):
    slots, rows, cols = tile_ref.shape
    rank = mix_ref.shape[0]
    own = weight_ref.shape[0] // got_ref.shape[0]
    mix = mix_ref[...]
    acc_ref[...] = jnp.zeros(acc_ref.shape, F32)
    lane = lax.broadcasted_iota(jnp.int32, (rank, rows), 1)
    for t in range(slots):
        k, b, g, kept = live_rows(t, list_ref, count_ref, visits_ref, rows)
        high, low = split(mix * weight_ref[pl.ds(k, 1), :])
        at = pl.multiple_of((lax.rem(k, own) * VBLOCKS + b) * rank, rank)
        polar = got_ref[lax.div(k, own), pl.ds(at, rank), :]
        spread = mm16(high, polar, TN) + mm16(low, polar, TN)
        spread = jnp.where(lane < kept, spread, 0.0).astype(BF16)
        acc_ref[g] += mm16(spread, tile_ref[t])
    parity = place_ref[1]
    for j in range(keep_ref.shape[0]):
        keep_ref[j] = acc_ref[2 * j + parity]
        send_ref[j] = acc_ref[2 * j + 1 - parity]


def factor_kernel(got_ref, inverse_ref, out_ref):
    sources = got_ref.shape[0]
    total = got_ref[0].astype(F32)
    for d in range(1, sources):
        total += got_ref[d].astype(F32)
    code = jnp.maximum(mm(inverse_ref[...], total), 0.0).astype(BF16)
    for d in range(sources):
        out_ref[d] = code


def place_kernel(place_ref, mine_ref, came_ref, out_ref):
    parity = place_ref[1]
    cols = mine_ref.shape[2]
    for j in range(mine_ref.shape[0]):
        at = pl.multiple_of((2 * j + parity) * cols, cols)
        out_ref[:, pl.ds(at, cols)] = mine_ref[j].astype(F32)
        at = pl.multiple_of((2 * j + 1 - parity) * cols, cols)
        out_ref[:, pl.ds(at, cols)] = came_ref[j].astype(F32)


def call(kernel, outs, specs, args, scratch=(), flops=1e9):
    many = isinstance(outs, tuple)
    return pl.pallas_call(
        kernel,
        out_shape=outs,
        in_specs=specs,
        out_specs=(VM,) * len(outs) if many else VM,
        scratch_shapes=scratch,
        compiler_params=PARAMS,
        cost_estimate=pl.CostEstimate(flops=int(flops), bytes_accessed=65536, transcendentals=0),
    )(*args)


def swap(x, axis, bit):
    size = lax.axis_size(axis)
    return lax.ppermute(x, axis, [(i, i ^ bit) for i in range(size)])


def swap_z(x, high, low):
    n_pat, n_code = lax.axis_size("pat"), lax.axis_size("code")
    pairs = [
        (p * n_code + c, (p ^ (high * n_pat // 2)) * n_code + (c ^ (low * n_code // 2)))
        for p in range(n_pat)
        for c in range(n_code)
    ]
    return lax.ppermute(x, ("pat", "code"), pairs)


def plus(x, parts):
    for part in parts:
        x = x + part
    return x


def sum_pat(x):
    x = plus(x, [swap(x, "pat", bit) for bit in (2, 4, 6)])
    x = x + swap(x, "pat", 8)
    return x + swap(x, "pat", 1)


def body(tile_data, tile_list, tile_count, visit_counts, code_factor_t, visit_mix, patient_weight):
    tiles = tile_data[0, 0]
    listing = tile_list[0, 0]
    slots, rows, cols = tiles.shape
    rank = visit_mix.shape[0]
    patients = visit_counts.shape[0]
    n_code, n_pat = lax.axis_size("code"), lax.axis_size("pat")
    half = n_pat // 2
    own = patients // n_code
    code_at, pat_at = lax.axis_index("code"), lax.axis_index("pat")
    place = jnp.stack([code_at, lax.rem(pat_at, 2)]).astype(jnp.int32)
    shape = jax.ShapeDtypeStruct
    square = shape((rank, rank), F32)

    partial = call(
        products_kernel, shape((patients * VBLOCKS, rank, rows), F32),
        [SM, SM, SM, VM, VM], (listing, tile_count, visit_counts, tiles, code_factor_t),
    )
    sent = partial.astype(F16).reshape(n_code, own * VBLOCKS * rank, rows)
    got = lax.all_to_all(sent, "code", 0, 0, tiled=True)
    code_gram, weight_gram = call(
        gram_kernel, (square, square), [VM, VM], (code_factor_t, patient_weight)
    )
    code_gram = plus(code_gram, [swap(code_gram, "code", bit) for bit in (1, 2, 3)])
    code_gram = code_gram + swap(code_gram, "code", 4)
    inverse_mix = call(
        inverse_kernel, square, [VM, VM], (code_gram, sum_pat(weight_gram)), flops=4e9
    )
    products = jnp.sum(got.astype(F32), axis=0).reshape(own * VBLOCKS, rank, rows)

    length = (own * VBLOCKS + own) * rank
    sums, message = call(
        polar_kernel,
        (shape((rank // 2, 2 * rank), F32), shape((n_code, length, rows), BF16)),
        [SM, VM, VM, VM], (place, products, visit_mix, patient_weight), flops=5e9,
    )
    shared = lax.all_to_all(message, "code", 0, 0, tiled=True)
    sums = plus(sums, [swap(sums, "code", bit) for bit in (1, 2, 3)])
    sums = plus(sums, [swap_z(sums, high, low) for high, low in ((0, 1), (1, 0), (1, 1))])
    sums = plus(sums, [swap(sums, "pat", bit) for bit in (2, 4, 6)])
    mix_new, mix_gram, inverse_weight = call(
        mix_kernel, (square,) * 3, [VM] * 4,
        (sums, swap(sums, "pat", 1), inverse_mix, code_gram), flops=4e9,
    )
    weights, wgram, weight_new = call(
        weight_kernel, (shape((patients, rank), F32), square, shape((own, rank), F32)),
        [SM, VM, VM, VM], (place, shared, mix_new, inverse_weight),
    )
    block = shape((half, rank, cols), F32)
    keep, send = call(
        numer_kernel, (block, block), [SM, SM, SM, SM, VM, VM, VM, VM],
        (place, listing, tile_count, visit_counts, shared, mix_new, weights, tiles),
        [pltpu.VMEM((n_pat, rank, cols), F32)], flops=4e9,
    )
    groups = [[core + 2 * i for i in range(half)] for core in (0, 1)]

    def exchange(x):
        return lax.all_to_all(x, "pat", 0, 0, axis_index_groups=groups, tiled=True)

    summed = exchange((keep + swap(send, "pat", 1)).astype(BF16))
    inverse_code = call(inverse_kernel, square, [VM, VM], (mix_gram, sum_pat(wgram)), flops=4e9)
    code = call(
        factor_kernel, shape((half, rank, cols), BF16), [VM, VM], (summed, inverse_code)
    )
    mine = exchange(code)
    code_new = call(
        place_kernel, shape((rank, n_pat * cols), F32),
        [SM, VM, VM], (place, mine, swap(mine, "pat", 1)),
    )
    return (code_new, mix_new, weight_new)


def solution(mesh):
    placed = (
        P("pat", "code", None, None, None),
        P("pat", "code", None, None),
        P("pat", "code"),
        P("pat"),
        P(None, "code"),
        P(),
        P("pat", None),
    )
    return jax.shard_map(
        body,
        mesh=mesh,
        in_specs=placed,
        out_specs=(P(None, "code"), P(), P(("pat", "code"), None)),
        check_vma=False,
    )
```

```python
import jax
import jax.numpy as jnp
from jax import lax
from jax.experimental import pallas as pl
from jax.experimental.pallas import tpu as pltpu
from jax.sharding import PartitionSpec as P

VBLOCKS = 2
NS_STEPS = 8
damping = 0.1
epsilon = 1e-06
F32, BF16, F16 = jnp.float32, jnp.bfloat16, jnp.float16
VM = pl.BlockSpec(memory_space=pltpu.VMEM)
SM = pl.BlockSpec(memory_space=pltpu.SMEM)
PARAMS = pltpu.CompilerParams(vmem_limit_bytes=48 * 1024 * 1024)


def mm(a, b, dims=((1,), (0,))):
    return lax.dot_general(
        a, b, (dims, ((), ())), precision=lax.Precision.HIGHEST, preferred_element_type=F32
    )


def mm16(a, b, dims=((1,), (0,))):
    return lax.dot_general(a, b, (dims, ((), ())), preferred_element_type=F32)


NT = ((1,), (1,))
TN = ((0,), (0,))


def split(x):
    high = x.astype(BF16)
    return high, (x - high.astype(F32)).astype(BF16)


def fold(x):
    half = x.shape[1] // 2
    return x[:, :half] + x[:, half:]


def times2(x, y):
    return [[x[i][0] * y[0][j] + x[i][1] * y[1][j] for j in (0, 1)] for i in (0, 1)]


def flip2(x):
    return [[x[0][0], x[1][0]], [x[0][1], x[1][1]]]


def inverse2(x):
    r = 1.0 / (x[0][0] * x[1][1] - x[0][1] * x[1][0])
    return [[x[1][1] * r, -x[0][1] * r], [-x[1][0] * r, x[0][0] * r]]


def inverse4(p):
    a = [[p[0][0], p[0][1]], [p[0][1], p[1][1]]]
    b = [[p[0][2], p[0][3]], [p[1][2], p[1][3]]]
    ai = inverse2(a)
    t = times2(ai, b)
    bt = times2(flip2(b), t)
    si = inverse2([[p[2][2] - bt[0][0], p[2][3] - bt[0][1]], [p[2][3] - bt[1][0], p[3][3] - bt[1][1]]])
    r = times2(t, si)
    u = times2(r, flip2(t))
    return [
        [ai[0][0] + u[0][0], ai[0][1] + u[0][1], -r[0][0], -r[0][1]],
        [ai[1][0] + u[1][0], ai[1][1] + u[1][1], -r[1][0], -r[1][1]],
        [-r[0][0], -r[1][0], si[0][0], si[0][1]],
        [-r[0][1], -r[1][1], si[1][0], si[1][1]],
    ]


def halves(x):
    low = x.shape[0] // 2
    return jnp.concatenate([x[:low], x[low:]], axis=1)


def damped_inverse(gram):
    size = gram.shape[0]
    eye = lax.broadcasted_iota(jnp.int32, (size, size), 0) == lax.broadcasted_iota(
        jnp.int32, (size, size), 1
    )
    mean = jnp.sum(jnp.where(eye, gram, 0.0), keepdims=True) / size
    work = jnp.concatenate(
        [gram + jnp.where(eye, damping * mean, 0.0), eye.astype(F32)], axis=1
    )
    lanes = 2 * size
    blocks = [work[i : i + 8] for i in range(0, size, 8)]
    row_at = lax.broadcasted_iota(jnp.int32, (8, lanes), 0)
    for j in range(0, size, 4):
        owner, at = j // 8, j % 8
        rows = [blocks[owner][at + i : at + i + 1] for i in range(4)]
        pivot = [
            [jnp.broadcast_to(row[:, j + k : j + k + 1], (1, lanes)) for k in range(4)]
            for row in rows
        ]
        inverse = inverse4(pivot)
        fresh = []
        for i in range(4):
            total = inverse[i][0] * rows[0]
            for k in range(1, 4):
                total = total + inverse[i][k] * rows[k]
            fresh.append(total)
        after = []
        for m, block in enumerate(blocks):
            value = block
            for k in range(4):
                value = value - block[:, j + k : j + k + 1] * fresh[k]
            if m == owner:
                for k in range(4):
                    value = jnp.where(row_at == at + k, fresh[k], value)
            after.append(value)
        blocks = after
    return jnp.concatenate(blocks, axis=0)[:, size:]


def live_rows(t, list_ref, count_ref, visits_ref, tile_rows):
    k, b, g = list_ref[0, t], list_ref[1, t], list_ref[2, t]
    kept = jnp.where(t < count_ref[0, 0], visits_ref[k] - tile_rows * b, 0)
    return k, b, g, kept


def products_kernel(list_ref, count_ref, visits_ref, tile_ref, code_ref, out_ref):
    slots, rows, cols = tile_ref.shape
    rank = code_ref.shape[0]
    out_ref[...] = jnp.zeros(out_ref.shape, F32)
    lane = lax.broadcasted_iota(jnp.int32, (rank, rows), 1)
    for t in range(slots):
        k, b, g, kept = live_rows(t, list_ref, count_ref, visits_ref, rows)
        codes = code_ref[:, pl.ds(pl.multiple_of(g * cols, cols), cols)].astype(BF16)
        part = mm16(codes, tile_ref[t], NT)
        out_ref[k * VBLOCKS + b] += jnp.where(lane < kept, part, 0.0)


def gram_kernel(code_ref, weight_ref, code_gram_ref, weight_gram_ref):
    high, low = split(code_ref[...])
    cross = mm16(high, low, NT)
    code_gram_ref[...] = mm16(high, high, NT) + cross + cross.T
    weight = weight_ref[...]
    weight_gram_ref[...] = mm(weight, weight, TN)


def inverse_kernel(a_ref, b_ref, out_ref):
    out_ref[...] = damped_inverse(a_ref[...] * b_ref[...])


def polar_kernel(at_ref, prod_ref, mix_ref, weight_ref, proj_ref, polar_ref):
    dests = polar_ref.shape[0]
    segs, rank, rows = prod_ref.shape
    own = segs // VBLOCKS
    prods = [
        jnp.concatenate([prod_ref[VBLOCKS * j + b] for b in range(VBLOCKS)], axis=1)
        for j in range(own)
    ]
    zs = []
    for j in range(own):
        weight = weight_ref[pl.ds(at_ref[0] * own + j, 1), :]
        target = mm(mix_ref[...] * weight, prods[j])
        zs.append(target / jnp.sqrt(jnp.sum(target * target, keepdims=True) + epsilon))
    for _ in range(NS_STEPS):
        grams = [mm(z, z, NT) for z in zs]
        zs = [1.5 * z - 0.5 * mm(g, z) for g, z in zip(grams, zs)]
    projected = [halves(mm(z, p, NT)) for z, p in zip(zs, prods)]
    polar = [z.astype(BF16) for z in zs]
    low = rank // 2
    for d in range(dests):
        for j in range(own):
            proj_ref[d, j * low : (j + 1) * low, :] = projected[j]
            for b in range(VBLOCKS):
                at = (VBLOCKS * j + b) * rank
                polar_ref[d, at : at + rank, :] = polar[j][:, b * rows : (b + 1) * rows]


def partial_kernel(got_ref, weight_ref, out_ref):
    sources = got_ref.shape[0]
    low = out_ref.shape[0]
    weight = weight_ref[...]
    twice = jnp.concatenate([weight, weight], axis=1)
    own = weight.shape[0] // sources
    total = jnp.zeros(out_ref.shape, F32)
    for d in range(sources):
        for j in range(own):
            k = d * own + j
            total += got_ref[d, j * low : (j + 1) * low, :] * twice[k : k + 1, :]
    out_ref[...] = total


def mix_kernel(
    place_ref, sum_a, sum_b, inverse_ref, code_gram_ref, got_ref,
    mix_ref, mgram_ref, weight_ref, wgram_ref, own_ref,
):
    sources = got_ref.shape[0]
    rank = mix_ref.shape[0]
    own = own_ref.shape[0]
    low = rank // 2
    sums = sum_a[...] + sum_b[...]
    numer = jnp.concatenate([sums[:, :rank], sums[:, rank:]], axis=0)
    mix = mm(numer, inverse_ref[...])
    mix_ref[...] = mix
    mix_gram = mm(mix, mix, TN)
    mgram_ref[...] = mix_gram
    inverse = damped_inverse(mix_gram * code_gram_ref[...])
    beside = halves(mix)
    terms = []
    for d in range(sources):
        for j in range(own):
            part = got_ref[d, j * low : (j + 1) * low, :] * beside
            terms.append(jnp.sum(part, axis=0, keepdims=True))
    weight = jnp.maximum(mm(fold(jnp.concatenate(terms, axis=0)), inverse), 0.0)
    weight_ref[...] = weight
    for j in range(own):
        own_ref[j : j + 1, :] = weight_ref[pl.ds(place_ref[0] * own + j, 1), :]
    wgram_ref[...] = halves(mm(weight, weight, TN))


def numer_kernel(
    place_ref, list_ref, count_ref, visits_ref, got_ref, mix_ref, weight_ref, tile_ref,
    keep_ref, send_ref, acc_ref,
):
    slots, rows, cols = tile_ref.shape
    rank = mix_ref.shape[0]
    own = weight_ref.shape[0] // got_ref.shape[0]
    mix = mix_ref[...]
    acc_ref[...] = jnp.zeros(acc_ref.shape, F32)
    lane = lax.broadcasted_iota(jnp.int32, (rank, rows), 1)
    for t in range(slots):
        k, b, g, kept = live_rows(t, list_ref, count_ref, visits_ref, rows)
        high, low = split(mix * weight_ref[pl.ds(k, 1), :])
        at = pl.multiple_of((lax.rem(k, own) * VBLOCKS + b) * rank, rank)
        polar = got_ref[lax.div(k, own), pl.ds(at, rank), :]
        spread = mm16(high, polar, TN) + mm16(low, polar, TN)
        spread = jnp.where(lane < kept, spread, 0.0).astype(BF16)
        acc_ref[g] += mm16(spread, tile_ref[t])
    parity = place_ref[1]
    for j in range(keep_ref.shape[0]):
        keep_ref[j] = acc_ref[2 * j + parity]
        send_ref[j] = acc_ref[2 * j + 1 - parity]


def pair_kernel(keep_ref, came_ref, gram_a, gram_b, out_ref):
    low, lanes = gram_a.shape
    slabs = keep_ref.shape[2] // lanes
    piece = jnp.concatenate(split(gram_a[...] + gram_b[...]), axis=0)
    for j in range(keep_ref.shape[0]):
        both = (keep_ref[j] + came_ref[j]).astype(BF16)
        for i in range(slabs):
            out_ref[j, i] = both[:, i * lanes : (i + 1) * lanes]
        out_ref[j, slabs] = piece


def factor_kernel(got_ref, mgram_ref, out_ref):
    sources, slabs = got_ref.shape[0], got_ref.shape[1] - 1
    sums = []
    for i in range(slabs + 1):
        total = got_ref[0, i].astype(F32)
        for d in range(1, sources):
            total += got_ref[d, i].astype(F32)
        sums.append(total)
    low = sums[slabs].shape[0] // 2
    gram = sums[slabs][:low] + sums[slabs][low:]
    rank = mgram_ref.shape[0]
    gram = jnp.concatenate([gram[:, :rank], gram[:, rank:]], axis=0)
    inverse = damped_inverse(mgram_ref[...] * gram)
    code = jnp.maximum(mm(inverse, jnp.concatenate(sums[:slabs], axis=1)), 0.0).astype(BF16)
    for d in range(sources):
        out_ref[d] = code


def place_kernel(place_ref, mine_ref, came_ref, out_ref):
    parity = place_ref[1]
    cols = mine_ref.shape[2]
    for j in range(mine_ref.shape[0]):
        at = pl.multiple_of((2 * j + parity) * cols, cols)
        out_ref[:, pl.ds(at, cols)] = mine_ref[j].astype(F32)
        at = pl.multiple_of((2 * j + 1 - parity) * cols, cols)
        out_ref[:, pl.ds(at, cols)] = came_ref[j].astype(F32)


def call(kernel, outs, specs, args, scratch=(), flops=1e9):
    many = isinstance(outs, tuple)
    return pl.pallas_call(
        kernel,
        out_shape=outs,
        in_specs=specs,
        out_specs=(VM,) * len(outs) if many else VM,
        scratch_shapes=scratch,
        compiler_params=PARAMS,
        cost_estimate=pl.CostEstimate(flops=int(flops), bytes_accessed=65536, transcendentals=0),
    )(*args)


def swap(x, axis, bit):
    size = lax.axis_size(axis)
    return lax.ppermute(x, axis, [(i, i ^ bit) for i in range(size)])


def plus(x, parts):
    for part in parts:
        x = x + part
    return x


def sum_pat(x):
    x = plus(x, [swap(x, "pat", bit) for bit in (2, 4, 6)])
    x = x + swap(x, "pat", 8)
    return x + swap(x, "pat", 1)


def body(tile_data, tile_list, tile_count, visit_counts, code_factor_t, visit_mix, patient_weight):
    tiles = tile_data[0, 0]
    listing = tile_list[0, 0]
    slots, rows, cols = tiles.shape
    rank = visit_mix.shape[0]
    patients = visit_counts.shape[0]
    n_code, n_pat = lax.axis_size("code"), lax.axis_size("pat")
    half = n_pat // 2
    own = patients // n_code
    code_at, pat_at = lax.axis_index("code"), lax.axis_index("pat")
    place = jnp.stack([code_at, lax.rem(pat_at, 2)]).astype(jnp.int32)
    shape = jax.ShapeDtypeStruct
    square = shape((rank, rank), F32)

    partial = call(
        products_kernel, shape((patients * VBLOCKS, rank, rows), F32),
        [SM, SM, SM, VM, VM], (listing, tile_count, visit_counts, tiles, code_factor_t),
    )
    sent = partial.astype(F16).reshape(n_code, own * VBLOCKS * rank, rows)
    sent, weight_after = lax.optimization_barrier((sent, patient_weight))
    got = lax.all_to_all(sent, "code", 0, 0, tiled=True)
    code_gram, weight_gram = call(
        gram_kernel, (square, square), [VM, VM], (code_factor_t, weight_after)
    )
    code_gram = plus(code_gram, [swap(code_gram, "code", bit) for bit in (1, 2, 3)])
    code_gram = code_gram + swap(code_gram, "code", 4)
    inverse_mix = call(
        inverse_kernel, square, [VM, VM], (code_gram, sum_pat(weight_gram)), flops=4e9
    )
    got, inverse_mix = lax.optimization_barrier((got, inverse_mix))
    products = jnp.sum(got.astype(F32), axis=0).reshape(own * VBLOCKS, rank, rows)

    proj, polar = call(
        polar_kernel,
        (
            shape((n_code, own * rank // 2, 2 * rank), F32),
            shape((n_code, own * VBLOCKS * rank, rows), BF16),
        ),
        [SM, VM, VM, VM], (place, products, visit_mix, patient_weight), flops=5e9,
    )
    proj = lax.all_to_all(proj, "code", 0, 0, tiled=True)
    proj, polar = lax.optimization_barrier((proj, polar))
    polar = lax.all_to_all(polar, "code", 0, 0, tiled=True)
    sums = call(partial_kernel, shape((rank // 2, 2 * rank), F32), [VM, VM], (proj, patient_weight))
    sums = plus(sums, [swap(sums, "pat", bit) for bit in (2, 4, 6)])
    sums = sums + swap(sums, "pat", 8)
    mix_new, mix_gram, weights, wgram, weight_new = call(
        mix_kernel,
        (
            square, square, shape((patients, rank), F32),
            shape((rank // 2, 2 * rank), F32), shape((own, rank), F32),
        ),
        [SM] + [VM] * 5,
        (place, sums, swap(sums, "pat", 1), inverse_mix, code_gram, proj), flops=5e9,
    )
    block = shape((half, rank, cols), F32)
    keep, send = call(
        numer_kernel, (block, block), [SM, SM, SM, SM, VM, VM, VM, VM],
        (place, listing, tile_count, visit_counts, polar, mix_new, weights, tiles),
        [pltpu.VMEM((n_pat, rank, cols), F32)], flops=4e9,
    )
    groups = [[core + 2 * i for i in range(half)] for core in (0, 1)]

    def exchange(x):
        return lax.all_to_all(x, "pat", 0, 0, axis_index_groups=groups, tiled=True)

    lanes = 2 * rank
    packed = call(
        pair_kernel, shape((half, cols // lanes + 1, rank, lanes), BF16), [VM] * 4,
        (keep, swap(send, "pat", 1), wgram, swap(wgram, "pat", 1)),
    )
    code = call(
        factor_kernel, shape((half, rank, cols), BF16), [VM, VM], (exchange(packed), mix_gram)
    )
    mine = exchange(code)
    code_new = call(
        place_kernel, shape((rank, n_pat * cols), F32),
        [SM, VM, VM], (place, mine, swap(mine, "pat", 1)),
    )
    return (code_new, mix_new, weight_new)


def solution(mesh):
    placed = (
        P("pat", "code", None, None, None),
        P("pat", "code", None, None),
        P("pat", "code"),
        P("pat"),
        P(None, "code"),
        P(),
        P("pat", None),
    )
    return jax.shard_map(
        body,
        mesh=mesh,
        in_specs=placed,
        out_specs=(P(None, "code"), P(), P(("pat", "code"), None)),
        check_vma=False,
    )
```

```python
import functools

import jax
import jax.numpy as jnp
from jax import lax
from jax.experimental import pallas as pl
from jax.experimental.pallas import tpu as pltpu
from jax.sharding import PartitionSpec as P

VBLOCKS = 2
NS_STEPS = 8
damping = 0.1
epsilon = 1e-06
F32, BF16, F16 = jnp.float32, jnp.bfloat16, jnp.float16
VM = pl.BlockSpec(memory_space=pltpu.VMEM)
HBM = pl.BlockSpec(memory_space=pl.ANY)
SM = pl.BlockSpec(memory_space=pltpu.SMEM)
PARAMS = pltpu.CompilerParams(vmem_limit_bytes=48 * 1024 * 1024)


def mm(a, b, dims=((1,), (0,))):
    return lax.dot_general(
        a, b, (dims, ((), ())), precision=lax.Precision.HIGHEST, preferred_element_type=F32
    )


def mm16(a, b, dims=((1,), (0,))):
    return lax.dot_general(a, b, (dims, ((), ())), preferred_element_type=F32)


NT = ((1,), (1,))
TN = ((0,), (0,))


def split(x):
    high = x.astype(BF16)
    return high, (x - high.astype(F32)).astype(BF16)


def fold(x):
    half = x.shape[1] // 2
    return x[:, :half] + x[:, half:]


def times2(x, y):
    return [[x[i][0] * y[0][j] + x[i][1] * y[1][j] for j in (0, 1)] for i in (0, 1)]


def flip2(x):
    return [[x[0][0], x[1][0]], [x[0][1], x[1][1]]]


def inverse2(x):
    r = 1.0 / (x[0][0] * x[1][1] - x[0][1] * x[1][0])
    return [[x[1][1] * r, -x[0][1] * r], [-x[1][0] * r, x[0][0] * r]]


def inverse4(p):
    a = [[p[0][0], p[0][1]], [p[0][1], p[1][1]]]
    b = [[p[0][2], p[0][3]], [p[1][2], p[1][3]]]
    ai = inverse2(a)
    t = times2(ai, b)
    bt = times2(flip2(b), t)
    si = inverse2([[p[2][2] - bt[0][0], p[2][3] - bt[0][1]], [p[2][3] - bt[1][0], p[3][3] - bt[1][1]]])
    r = times2(t, si)
    u = times2(r, flip2(t))
    return [
        [ai[0][0] + u[0][0], ai[0][1] + u[0][1], -r[0][0], -r[0][1]],
        [ai[1][0] + u[1][0], ai[1][1] + u[1][1], -r[1][0], -r[1][1]],
        [-r[0][0], -r[1][0], si[0][0], si[0][1]],
        [-r[0][1], -r[1][1], si[1][0], si[1][1]],
    ]


def halves(x):
    low = x.shape[0] // 2
    return jnp.concatenate([x[:low], x[low:]], axis=1)


def damped_inverse(gram):
    size = gram.shape[0]
    eye = lax.broadcasted_iota(jnp.int32, (size, size), 0) == lax.broadcasted_iota(
        jnp.int32, (size, size), 1
    )
    mean = jnp.sum(jnp.where(eye, gram, 0.0), keepdims=True) / size
    work = jnp.concatenate(
        [gram + jnp.where(eye, damping * mean, 0.0), eye.astype(F32)], axis=1
    )
    lanes = 2 * size
    blocks = [work[i : i + 8] for i in range(0, size, 8)]
    row_at = lax.broadcasted_iota(jnp.int32, (8, lanes), 0)
    for j in range(0, size, 4):
        owner, at = j // 8, j % 8
        rows = [blocks[owner][at + i : at + i + 1] for i in range(4)]
        pivot = [
            [jnp.broadcast_to(row[:, j + k : j + k + 1], (1, lanes)) for k in range(4)]
            for row in rows
        ]
        inverse = inverse4(pivot)
        fresh = []
        for i in range(4):
            total = inverse[i][0] * rows[0]
            for k in range(1, 4):
                total = total + inverse[i][k] * rows[k]
            fresh.append(total)
        after = []
        for m, block in enumerate(blocks):
            value = block
            for k in range(4):
                value = value - block[:, j + k : j + k + 1] * fresh[k]
            if m == owner:
                for k in range(4):
                    value = jnp.where(row_at == at + k, fresh[k], value)
            after.append(value)
        blocks = after
    return jnp.concatenate(blocks, axis=0)[:, size:]


def live_rows(t, list_ref, count_ref, visits_ref, tile_rows):
    k, b, g = list_ref[0, 0, 0, t], list_ref[0, 0, 1, t], list_ref[0, 0, 2, t]
    kept = jnp.where(t < count_ref[0, 0], visits_ref[k] - tile_rows * b, 0)
    return k, b, g, kept


def products_kernel(
    list_ref, count_ref, visits_ref, tile_hbm, code_hbm, out_ref, acc_ref, tile_ref, code_ref, sems
):
    slots, rows, cols = tile_ref.shape
    rank = code_ref.shape[0]
    parts = sems.shape[0] - 1
    each = slots // parts
    code_copy = pltpu.make_async_copy(code_hbm, code_ref, sems.at[parts])
    code_copy.start()
    copies = []
    for i in range(parts):
        at = pl.ds(i * each, each)
        copies.append(pltpu.make_async_copy(tile_hbm.at[0, 0, at], tile_ref.at[at], sems.at[i]))
        copies[-1].start()
    acc_ref[...] = jnp.zeros(acc_ref.shape, F32)
    lane = lax.broadcasted_iota(jnp.int32, (rank, rows), 1)
    code_copy.wait()
    for t in range(slots):
        if t % each == 0:
            copies[t // each].wait()
        k, b, g, kept = live_rows(t, list_ref, count_ref, visits_ref, rows)
        codes = code_ref[:, pl.ds(pl.multiple_of(g * cols, cols), cols)].astype(BF16)
        part = mm16(codes, tile_ref[t], NT)
        acc_ref[k * VBLOCKS + b] += jnp.where(lane < kept, part, 0.0)
    out_ref[...] = acc_ref[...].astype(out_ref.dtype)


def gram_kernel(code_ref, out_ref):
    high, low = split(code_ref[...])
    cross = mm16(high, low, NT)
    out_ref[...] = halves(mm16(high, high, NT) + cross + cross.T)


def polar_kernel(at_ref, prod_ref, mix_ref, weight_ref, gram_ref, proj_ref, polar_ref):
    dests = polar_ref.shape[0]
    segs, rank, rows = prod_ref.shape
    own = segs // VBLOCKS
    prods = [
        jnp.concatenate([prod_ref[VBLOCKS * j + b] for b in range(VBLOCKS)], axis=1)
        for j in range(own)
    ]
    zs = []
    for j in range(own):
        weight = weight_ref[pl.ds(at_ref[0] * own + j, 1), :]
        target = mm(mix_ref[...] * weight, prods[j])
        zs.append(target / jnp.sqrt(jnp.sum(target * target, keepdims=True) + epsilon))
    for _ in range(NS_STEPS):
        grams = [mm(z, z, NT) for z in zs]
        zs = [1.5 * z - 0.5 * mm(g, z) for g, z in zip(grams, zs)]
    projected = [halves(mm(z, p, NT)) for z, p in zip(zs, prods)]
    polar = [z.astype(BF16) for z in zs]
    low = rank // 2
    for d in range(dests):
        proj_ref[d, own * low :, :] = gram_ref[...]
        for j in range(own):
            proj_ref[d, j * low : (j + 1) * low, :] = projected[j]
            for b in range(VBLOCKS):
                at = (VBLOCKS * j + b) * rank
                polar_ref[d, at : at + rank, :] = polar[j][:, b * rows : (b + 1) * rows]


def partial_kernel(got_ref, weight_ref, out_ref):
    sources = got_ref.shape[0]
    low = out_ref.shape[0] // 2
    weight = weight_ref[...]
    twice = jnp.concatenate([weight, weight], axis=1)
    own = weight.shape[0] // sources
    total = jnp.zeros((low, out_ref.shape[1]), F32)
    for d in range(sources):
        for j in range(own):
            k = d * own + j
            total += got_ref[d, j * low : (j + 1) * low, :] * twice[k : k + 1, :]
    out_ref[:low, :] = total
    out_ref[low:, :] = halves(mm(weight, weight, TN))


def whole(x):
    rank = x.shape[1] // 2
    return jnp.concatenate([x[:, :rank], x[:, rank:]], axis=0)


def mix_kernel(
    place_ref, sum_a, sum_b, got_ref, mix_ref, mgram_ref, weight_ref, wgram_ref, own_ref
):
    sources = got_ref.shape[0]
    rank = mix_ref.shape[0]
    own = own_ref.shape[0]
    low = rank // 2
    code_gram = got_ref[0, own * low :, :]
    for d in range(1, sources):
        code_gram += got_ref[d, own * low :, :]
    code_gram = whole(code_gram)
    numer = whole(sum_a[:low, :] + sum_b[:low, :])
    weight_gram = whole(sum_a[low:, :] + sum_b[low:, :])
    mix = mm(numer, damped_inverse(code_gram * weight_gram))
    mix_ref[...] = mix
    mix_gram = mm(mix, mix, TN)
    mgram_ref[...] = mix_gram
    inverse = damped_inverse(mix_gram * code_gram)
    beside = halves(mix)
    terms = []
    for d in range(sources):
        for j in range(own):
            part = got_ref[d, j * low : (j + 1) * low, :] * beside
            terms.append(jnp.sum(part, axis=0, keepdims=True))
    weight = jnp.maximum(mm(fold(jnp.concatenate(terms, axis=0)), inverse), 0.0)
    weight_ref[...] = weight
    for j in range(own):
        own_ref[j : j + 1, :] = weight_ref[pl.ds(place_ref[0] * own + j, 1), :]
    wgram_ref[...] = halves(mm(weight, weight, TN))


def numer_kernel(
    place_ref, list_ref, count_ref, visits_ref, got_ref, mix_ref, weight_ref, tile_ref,
    keep_ref, send_ref, acc_ref,
):
    slots, rows, cols = tile_ref.shape
    rank = mix_ref.shape[0]
    own = weight_ref.shape[0] // got_ref.shape[0]
    mix = mix_ref[...]
    acc_ref[...] = jnp.zeros(acc_ref.shape, F32)
    lane = lax.broadcasted_iota(jnp.int32, (rank, rows), 1)
    for t in range(slots):
        k, b, g, kept = live_rows(t, list_ref, count_ref, visits_ref, rows)
        high, low = split(mix * weight_ref[pl.ds(k, 1), :])
        at = pl.multiple_of((lax.rem(k, own) * VBLOCKS + b) * rank, rank)
        polar = got_ref[lax.div(k, own), pl.ds(at, rank), :]
        spread = mm16(high, polar, TN) + mm16(low, polar, TN)
        spread = jnp.where(lane < kept, spread, 0.0).astype(BF16)
        acc_ref[g] += mm16(spread, tile_ref[t])
    parity = place_ref[1]
    for j in range(keep_ref.shape[0]):
        keep_ref[j] = acc_ref[2 * j + parity]
        send_ref[j] = acc_ref[2 * j + 1 - parity]


def pair_kernel(keep_ref, came_ref, gram_a, gram_b, out_ref):
    low, lanes = gram_a.shape
    slabs = keep_ref.shape[2] // lanes
    piece = jnp.concatenate(split(gram_a[...] + gram_b[...]), axis=0)
    for j in range(keep_ref.shape[0]):
        both = (keep_ref[j] + came_ref[j]).astype(BF16)
        for i in range(slabs):
            out_ref[j, i] = both[:, i * lanes : (i + 1) * lanes]
        out_ref[j, slabs] = piece


def factor_kernel(got_ref, mgram_ref, out_ref):
    sources, slabs = got_ref.shape[0], got_ref.shape[1] - 1
    sums = []
    for i in range(slabs + 1):
        total = got_ref[0, i].astype(F32)
        for d in range(1, sources):
            total += got_ref[d, i].astype(F32)
        sums.append(total)
    low = sums[slabs].shape[0] // 2
    gram = whole(sums[slabs][:low] + sums[slabs][low:])
    inverse = damped_inverse(mgram_ref[...] * gram)
    code = jnp.maximum(mm(inverse, jnp.concatenate(sums[:slabs], axis=1)), 0.0).astype(BF16)
    for d in range(sources):
        out_ref[d] = code


def place_kernel(flip, place_ref, from_ref, *refs):
    out_hbm, wide_ref, sems = refs[-3:]
    parity = place_ref[1] if not flip else 1 - place_ref[1]
    cols = from_ref.shape[2]
    copies = []
    for j in range(from_ref.shape[0]):
        wide_ref[j] = from_ref[j].astype(F32)
        at = pl.multiple_of((2 * j + parity) * cols, cols)
        copies.append(
            pltpu.make_async_copy(wide_ref.at[j], out_hbm.at[:, pl.ds(at, cols)], sems.at[j])
        )
        copies[-1].start()
    for copy in copies:
        copy.wait()


def call(kernel, outs, specs, args, scratch=(), flops=1e9, spec=VM, alias=None):
    many = isinstance(outs, tuple)
    return pl.pallas_call(
        kernel,
        out_shape=outs,
        in_specs=specs,
        out_specs=(spec,) * len(outs) if many else spec,
        input_output_aliases=alias or {},
        scratch_shapes=scratch,
        compiler_params=PARAMS,
        cost_estimate=pl.CostEstimate(flops=int(flops), bytes_accessed=65536, transcendentals=0),
    )(*args)


def swap(x, axis, bit):
    size = lax.axis_size(axis)
    return lax.ppermute(x, axis, [(i, i ^ bit) for i in range(size)])


def plus(x, parts):
    for part in parts:
        x = x + part
    return x


def body(tile_data, tile_list, tile_count, visit_counts, code_factor_t, visit_mix, patient_weight):
    tiles = tile_data[0, 0]
    slots, rows, cols = tiles.shape
    rank = visit_mix.shape[0]
    patients = visit_counts.shape[0]
    n_code, n_pat = lax.axis_size("code"), lax.axis_size("pat")
    half = n_pat // 2
    own = patients // n_code
    code_at, pat_at = lax.axis_index("code"), lax.axis_index("pat")
    place = jnp.stack([code_at, lax.rem(pat_at, 2)]).astype(jnp.int32)
    shape = jax.ShapeDtypeStruct
    square = shape((rank, rank), F32)

    partial = call(
        products_kernel, shape((patients * VBLOCKS, rank, rows), F32), [SM, SM, SM, HBM, HBM],
        (tile_list, tile_count, visit_counts, tile_data, code_factor_t),
        [
            pltpu.VMEM((patients * VBLOCKS, rank, rows), F32), pltpu.VMEM(tiles.shape, BF16),
            pltpu.VMEM(code_factor_t.shape, F32), pltpu.SemaphoreType.DMA((5,)),
        ],
    )
    sent = partial.astype(F16).reshape(n_code, own * VBLOCKS * rank, rows)
    got = lax.all_to_all(sent, "code", 0, 0, tiled=True)
    gram = call(gram_kernel, shape((rank // 2, 2 * rank), F32), [VM], (code_factor_t,))
    products = jnp.sum(got.astype(F32), axis=0).reshape(own * VBLOCKS, rank, rows)

    proj, polar = call(
        polar_kernel,
        (
            shape((n_code, (own + 1) * rank // 2, 2 * rank), F32),
            shape((n_code, own * VBLOCKS * rank, rows), BF16),
        ),
        [SM, VM, VM, VM, VM], (place, products, visit_mix, patient_weight, gram), flops=5e9,
    )
    proj = lax.all_to_all(proj, "code", 0, 0, tiled=True)
    proj, polar = lax.optimization_barrier((proj, polar))
    polar = lax.all_to_all(polar, "code", 0, 0, tiled=True)
    sums = call(partial_kernel, shape((rank, 2 * rank), F32), [VM, VM], (proj, patient_weight))
    sums = plus(sums, [swap(sums, "pat", bit) for bit in (2, 4, 6)])
    sums = sums + swap(sums, "pat", 8)
    mix_new, mix_gram, weights, wgram, weight_new = call(
        mix_kernel,
        (
            square, square, shape((patients, rank), F32),
            shape((rank // 2, 2 * rank), F32), shape((own, rank), F32),
        ),
        [SM] + [VM] * 3,
        (place, sums, swap(sums, "pat", 1), proj), flops=8e9,
    )
    block = shape((half, rank, cols), F32)
    keep, send = call(
        numer_kernel, (block, block), [SM, SM, SM, SM, VM, VM, VM, VM],
        (place, tile_list, tile_count, visit_counts, polar, mix_new, weights, tiles),
        [pltpu.VMEM((n_pat, rank, cols), F32)], flops=4e9,
    )
    groups = [[core + 2 * i for i in range(half)] for core in (0, 1)]

    def exchange(x):
        return lax.all_to_all(x, "pat", 0, 0, axis_index_groups=groups, tiled=True)

    lanes = 2 * rank
    packed = call(
        pair_kernel, shape((half, cols // lanes + 1, rank, lanes), BF16), [VM] * 4,
        (keep, swap(send, "pat", 1), wgram, swap(wgram, "pat", 1)),
    )
    code = call(
        factor_kernel, shape((half, rank, cols), BF16), [VM, VM], (exchange(packed), mix_gram)
    )
    mine = exchange(code)
    place_scratch = [pltpu.VMEM(mine.shape, F32), pltpu.SemaphoreType.DMA((half,))]
    result = shape((rank, n_pat * cols), F32)
    came = swap(mine, "pat", 1)
    code_new = call(
        functools.partial(place_kernel, False), result, [SM, VM], (place, mine), place_scratch,
        spec=HBM,
    )
    code_new = call(
        functools.partial(place_kernel, True), result, [SM, VM, HBM], (place, came, code_new),
        place_scratch, spec=HBM, alias={2: 0},
    )
    return (code_new, mix_new, weight_new)


def solution(mesh):
    placed = (
        P("pat", "code", None, None, None),
        P("pat", "code", None, None),
        P("pat", "code"),
        P("pat"),
        P(None, "code"),
        P(),
        P("pat", None),
    )
    return jax.shard_map(
        body,
        mesh=mesh,
        in_specs=placed,
        out_specs=(P(None, "code"), P(), P(("pat", "code"), None)),
        check_vma=False,
    )
```

```python
import functools

import jax
import jax.numpy as jnp
from jax import lax
from jax.experimental import pallas as pl
from jax.experimental.pallas import tpu as pltpu
from jax.sharding import PartitionSpec as P

VBLOCKS = 2
NS_STEPS = 8
damping = 0.1
epsilon = 1e-06
F32, BF16, F16 = jnp.float32, jnp.bfloat16, jnp.float16
VM = pl.BlockSpec(memory_space=pltpu.VMEM)
HBM = pl.BlockSpec(memory_space=pl.ANY)
SM = pl.BlockSpec(memory_space=pltpu.SMEM)
MIB = 1024 * 1024


def mm(a, b, dims=((1,), (0,))):
    return lax.dot_general(
        a, b, (dims, ((), ())), precision=lax.Precision.HIGHEST, preferred_element_type=F32
    )


def mm16(a, b, dims=((1,), (0,))):
    return lax.dot_general(a, b, (dims, ((), ())), preferred_element_type=F32)


NT = ((1,), (1,))
TN = ((0,), (0,))


def split(x):
    high = x.astype(BF16)
    return high, (x - high.astype(F32)).astype(BF16)


def mm3(a, b, dims=((1,), (0,))):
    return mm16(a[0], b[0], dims) + (mm16(a[0], b[1], dims) + mm16(a[1], b[0], dims))


def fold(x):
    half = x.shape[1] // 2
    return x[:, :half] + x[:, half:]


def times2(x, y):
    return [[x[i][0] * y[0][j] + x[i][1] * y[1][j] for j in (0, 1)] for i in (0, 1)]


def inverse4(p):
    a = [[p[1][1], -p[0][1]], [-p[0][1], p[0][0]]]
    det = p[0][0] * p[1][1] - p[0][1] * p[0][1]
    b = [[p[0][2], p[0][3]], [p[1][2], p[1][3]]]
    t = times2(a, b)
    s00 = det * p[2][2] - (b[0][0] * t[0][0] + b[1][0] * t[1][0])
    s01 = det * p[2][3] - (b[0][0] * t[0][1] + b[1][0] * t[1][1])
    s11 = det * p[3][3] - (b[0][1] * t[0][1] + b[1][1] * t[1][1])
    over = 1.0 / (s00 * s11 - s01 * s01)
    over_det = 1.0 / det
    flip = [[s11, -s01], [-s01, s00]]
    u = times2(t, flip)
    v = times2(u, [[t[0][0], t[1][0]], [t[0][1], t[1][1]]])
    side = [[u[i][j] * over for j in (0, 1)] for i in (0, 1)]
    last = [[flip[i][j] * (det * over) for j in (0, 1)] for i in (0, 1)]
    first = [
        [a[i][j] * over_det + v[i][j] * (over * over_det) for j in (0, 1)] for i in (0, 1)
    ]
    return [
        [first[0][0], first[0][1], -side[0][0], -side[0][1]],
        [first[0][1], first[1][1], -side[1][0], -side[1][1]],
        [-side[0][0], -side[1][0], last[0][0], last[0][1]],
        [-side[0][1], -side[1][1], last[0][1], last[1][1]],
    ]


def halves(x):
    low = x.shape[0] // 2
    return jnp.concatenate([x[:low], x[low:]], axis=1)


def damped_inverse(gram):
    size = gram.shape[0]
    eye = lax.broadcasted_iota(jnp.int32, (size, size), 0) == lax.broadcasted_iota(
        jnp.int32, (size, size), 1
    )
    scale = size / jnp.sum(jnp.where(eye, gram, 0.0), keepdims=True)
    work = jnp.concatenate(
        [gram * scale + jnp.where(eye, damping, 0.0), eye.astype(F32)], axis=1
    )
    lanes = 2 * size
    blocks = [work[i : i + 8] for i in range(0, size, 8)]
    raw, fresh = [], []
    for j in range(0, size, 4):
        owner, at = j // 8, j % 8
        rows = [blocks[owner][at + i : at + i + 1] for i in range(4)]
        pivot = [
            [jnp.broadcast_to(row[:, j + k : j + k + 1], (1, lanes)) for k in range(4)]
            for row in rows
        ]
        inverse = inverse4(pivot)
        new = [
            (inverse[i][0] * rows[0] + inverse[i][1] * rows[1])
            + (inverse[i][2] * rows[2] + inverse[i][3] * rows[3])
            for i in range(4)
        ]
        raw += rows
        fresh += new
        for m in range(owner if at == 0 else owner + 1, len(blocks)):
            block = blocks[m]
            part = [block[:, j + k : j + k + 1] * new[k] for k in range(4)]
            blocks[m] = block - ((part[0] + part[1]) + (part[2] + part[3]))
    raw = jnp.concatenate(raw, axis=0)[:, size:]
    fresh = jnp.concatenate(fresh, axis=0)[:, size:]
    return scale * mm(raw, fresh, TN)


def live_rows(t, list_ref, count_ref, visits_ref, tile_rows):
    k, b, g = list_ref[0, 0, 0, t], list_ref[0, 1, 0, t], list_ref[0, 2, 0, t]
    kept = jnp.where(t < count_ref[0, 0], visits_ref[k] - tile_rows * b, 0)
    return k, b, g, kept


def products_kernel(
    list_hbm, count_hbm, visits_hbm, tile_hbm, code_hbm, out_ref,
    list_ref, count_ref, visits_ref, tile_ref, code_ref, small_sems, sems,
):
    slots, rows, cols = tile_ref.shape
    rank = code_ref.shape[0]
    parts = sems.shape[0] - 1
    each = slots // parts
    small = []
    for i, (src, dst) in enumerate(
        ((list_hbm, list_ref), (count_hbm, count_ref), (visits_hbm, visits_ref))
    ):
        small.append(pltpu.make_async_copy(src, dst, small_sems.at[i]))
        small[-1].start()
    code_copy = pltpu.make_async_copy(code_hbm, code_ref, sems.at[parts])
    code_copy.start()
    copies = []
    for i in range(parts):
        at = pl.ds(i * each, each)
        copies.append(pltpu.make_async_copy(tile_hbm.at[0, 0, at], tile_ref.at[at], sems.at[i]))
        copies[-1].start()
    out_ref[...] = jnp.zeros(out_ref.shape, F32)
    lane = lax.broadcasted_iota(jnp.int32, (rank, rows), 1)
    for copy in small:
        copy.wait()
    code_copy.wait()
    for t in range(slots):
        if t % each == 0:
            copies[t // each].wait()
        k, b, g, kept = live_rows(t, list_ref, count_ref, visits_ref, rows)
        codes = code_ref[:, pl.ds(pl.multiple_of(g * cols, cols), cols)].astype(BF16)
        part = mm16(codes, tile_ref[t], NT)
        out_ref[k * VBLOCKS + b] += jnp.where(lane < kept, part, 0.0)


def gram_kernel(code_ref, out_ref):
    high, low = split(code_ref[...])
    cross = mm16(high, low, NT)
    out_ref[...] = halves(mm16(high, high, NT) + cross + cross.T)


def polar_kernel(at_ref, prod_ref, mix_ref, weight_ref, gram_ref, proj_ref, polar_ref):
    dests = polar_ref.shape[0]
    segs, rank, rows = prod_ref.shape
    own = segs // VBLOCKS
    eye = lax.broadcasted_iota(jnp.int32, (rank, rank), 0) == lax.broadcasted_iota(
        jnp.int32, (rank, rank), 1
    )
    prods, zs = [], []
    for j in range(own):
        prods.append(
            split(jnp.concatenate([prod_ref[VBLOCKS * j + b] for b in range(VBLOCKS)], axis=1))
        )
        weight = weight_ref[pl.ds(at_ref[0] * own + j, 1), :]
        target = mm3(split(mix_ref[...] * weight), prods[j])
        zs.append(target / jnp.sqrt(jnp.sum(target * target, keepdims=True) + epsilon))
    zs = [split(z) for z in zs]
    for _ in range(NS_STEPS):
        factors = [split(jnp.where(eye, 1.5, 0.0) - 0.5 * mm3(z, z, NT)) for z in zs]
        zs = [split(mm3(q, z)) for q, z in zip(factors, zs)]
    projected = [halves(mm3(z, p, NT)) for z, p in zip(zs, prods)]
    polar = [z[0] for z in zs]
    low = rank // 2
    for d in range(dests):
        proj_ref[d, own * low :, :] = gram_ref[...]
        for j in range(own):
            proj_ref[d, j * low : (j + 1) * low, :] = projected[j]
            for b in range(VBLOCKS):
                at = (VBLOCKS * j + b) * rank
                polar_ref[d, at : at + rank, :] = polar[j][:, b * rows : (b + 1) * rows]


def partial_kernel(got_ref, weight_ref, out_ref, gram_ref):
    sources = got_ref.shape[0]
    low = gram_ref.shape[0]
    weight = weight_ref[...]
    twice = jnp.concatenate([weight, weight], axis=1)
    own = weight.shape[0] // sources
    total = jnp.zeros(gram_ref.shape, F32)
    gram = jnp.zeros(gram_ref.shape, F32)
    for d in range(sources):
        for j in range(own):
            k = d * own + j
            total += got_ref[d, j * low : (j + 1) * low, :] * twice[k : k + 1, :]
        gram += got_ref[d, own * low :, :]
    out_ref[:low, :] = total
    out_ref[low:, :] = halves(mm(weight, weight, TN))
    gram_ref[...] = gram


def whole(x):
    rank = x.shape[1] // 2
    return jnp.concatenate([x[:, :rank], x[:, rank:]], axis=0)


def mix_kernel(
    place_ref, sum_a, sum_b, gram_ref, got_hbm,
    mix_ref, again_ref, mgram_ref, weight_ref, wgram_ref, own_ref, got_ref, sem,
):
    copy = pltpu.make_async_copy(got_hbm, got_ref, sem)
    copy.start()
    sources = got_ref.shape[0]
    rank = mix_ref.shape[0]
    own = own_ref.shape[0]
    low = rank // 2
    code_gram = whole(gram_ref[...])
    numer = whole(sum_a[:low, :] + sum_b[:low, :])
    weight_gram = whole(sum_a[low:, :] + sum_b[low:, :])
    mix = mm(numer, damped_inverse(code_gram * weight_gram))
    again_ref[...] = mix
    mix_ref[...] = mix
    mix_gram = mm(mix, mix, TN)
    mgram_ref[...] = mix_gram
    inverse = damped_inverse(mix_gram * code_gram)
    beside = halves(mix)
    copy.wait()
    terms = []
    for d in range(sources):
        for j in range(own):
            part = got_ref[d, j * low : (j + 1) * low, :] * beside
            terms.append(jnp.sum(part, axis=0, keepdims=True))
    weight = jnp.maximum(mm(fold(jnp.concatenate(terms, axis=0)), inverse), 0.0)
    weight_ref[...] = weight
    for j in range(own):
        own_ref[j : j + 1, :] = weight_ref[pl.ds(place_ref[0] * own + j, 1), :]
    wgram_ref[...] = halves(mm(weight, weight, TN))


def numer_kernel(
    place_ref, list_ref, count_ref, visits_ref, got_ref, mix_ref, weight_ref, tile_ref,
    keep_ref, send_ref, acc_ref,
):
    slots, rows, cols = tile_ref.shape
    rank = mix_ref.shape[0]
    own = weight_ref.shape[0] // got_ref.shape[0]
    mix = mix_ref[...]
    acc_ref[...] = jnp.zeros(acc_ref.shape, F32)
    lane = lax.broadcasted_iota(jnp.int32, (rank, rows), 1)
    for t in range(slots):
        k, b, g, kept = live_rows(t, list_ref, count_ref, visits_ref, rows)
        high, low = split(mix * weight_ref[pl.ds(k, 1), :])
        at = pl.multiple_of((lax.rem(k, own) * VBLOCKS + b) * rank, rank)
        polar = got_ref[lax.div(k, own), pl.ds(at, rank), :]
        spread = mm16(high, polar, TN) + mm16(low, polar, TN)
        spread = jnp.where(lane < kept, spread, 0.0).astype(BF16)
        acc_ref[g] += mm16(spread, tile_ref[t])
    parity = place_ref[1]
    for j in range(keep_ref.shape[0]):
        keep_ref[j] = acc_ref[2 * j + parity]
        send_ref[j] = acc_ref[2 * j + 1 - parity]


def pair_kernel(keep_ref, came_ref, gram_a, gram_b, out_ref):
    low, lanes = gram_a.shape
    slabs = keep_ref.shape[2] // lanes
    piece = jnp.concatenate(split(gram_a[...] + gram_b[...]), axis=0)
    for j in range(keep_ref.shape[0]):
        both = (keep_ref[j] + came_ref[j]).astype(BF16)
        for i in range(slabs):
            out_ref[j, i] = both[:, i * lanes : (i + 1) * lanes]
        out_ref[j, slabs] = piece


def factor_kernel(got_ref, mgram_ref, out_ref):
    sources, slabs = got_ref.shape[0], got_ref.shape[1] - 1
    sums = []
    for i in range(slabs + 1):
        total = got_ref[0, i].astype(F32)
        for d in range(1, sources):
            total += got_ref[d, i].astype(F32)
        sums.append(total)
    low = sums[slabs].shape[0] // 2
    gram = whole(sums[slabs][:low] + sums[slabs][low:])
    inverse = damped_inverse(mgram_ref[...] * gram)
    code = jnp.maximum(mm(inverse, jnp.concatenate(sums[:slabs], axis=1)), 0.0).astype(BF16)
    for d in range(sources):
        out_ref[d] = code


def place_kernel(flip, place_ref, from_ref, *refs):
    out_hbm, wide_ref, sems = refs[-3:]
    parity = place_ref[1] if not flip else 1 - place_ref[1]
    cols = from_ref.shape[2]
    copies = []
    for j in range(from_ref.shape[0]):
        wide_ref[j] = from_ref[j].astype(F32)
        at = pl.multiple_of((2 * j + parity) * cols, cols)
        copies.append(
            pltpu.make_async_copy(wide_ref.at[j], out_hbm.at[:, pl.ds(at, cols)], sems.at[j])
        )
        copies[-1].start()
    for copy in copies:
        copy.wait()


def call(kernel, outs, specs, args, scratch=(), flops=1e9, spec=VM, alias=None, vmem=16):
    many = isinstance(outs, tuple)
    return pl.pallas_call(
        kernel,
        out_shape=outs,
        in_specs=specs,
        out_specs=(spec,) * len(outs) if many else spec,
        input_output_aliases=alias or {},
        scratch_shapes=scratch,
        compiler_params=pltpu.CompilerParams(vmem_limit_bytes=vmem * MIB),
        cost_estimate=pl.CostEstimate(flops=int(flops), bytes_accessed=65536, transcendentals=0),
    )(*args)


def swap(x, axis, bit):
    size = lax.axis_size(axis)
    return lax.ppermute(x, axis, [(i, i ^ bit) for i in range(size)])


def plus(x, parts):
    for part in parts:
        x = x + part
    return x


def body(tile_data, tile_list, tile_count, visit_counts, code_factor_t, visit_mix, patient_weight):
    tiles = tile_data[0, 0]
    tile_list = jnp.transpose(tile_list, (0, 2, 1, 3))
    slots, rows, cols = tiles.shape
    rank = visit_mix.shape[0]
    patients = visit_counts.shape[0]
    n_code, n_pat = lax.axis_size("code"), lax.axis_size("pat")
    half = n_pat // 2
    own = patients // n_code
    code_at, pat_at = lax.axis_index("code"), lax.axis_index("pat")
    place = jnp.stack([code_at, lax.rem(pat_at, 2)]).astype(jnp.int32)
    shape = jax.ShapeDtypeStruct
    square = shape((rank, rank), F32)

    partial = call(
        products_kernel, shape((patients * VBLOCKS, rank, rows), F32), [HBM] * 5,
        (tile_list, tile_count, visit_counts, tile_data, code_factor_t),
        [
            pltpu.SMEM(tile_list.shape, jnp.int32), pltpu.SMEM(tile_count.shape, jnp.int32),
            pltpu.SMEM(visit_counts.shape, jnp.int32), pltpu.VMEM(tiles.shape, BF16),
            pltpu.VMEM(code_factor_t.shape, F32), pltpu.SemaphoreType.DMA((3,)),
            pltpu.SemaphoreType.DMA((5,)),
        ],
        vmem=60,
    )
    sent = partial.astype(F16).reshape(n_code, own * VBLOCKS * rank, rows)
    got = lax.all_to_all(sent, "code", 0, 0, tiled=True)
    gram = call(gram_kernel, shape((rank // 2, 2 * rank), F32), [VM], (code_factor_t,))
    products = jnp.sum(got.astype(F32), axis=0).reshape(own * VBLOCKS, rank, rows)

    proj, polar = call(
        polar_kernel,
        (
            shape((n_code, (own + 1) * rank // 2, 2 * rank), F32),
            shape((n_code, own * VBLOCKS * rank, rows), BF16),
        ),
        [SM, VM, VM, VM, VM], (place, products, visit_mix, patient_weight, gram), flops=5e9,
    )
    proj = lax.all_to_all(proj, "code", 0, 0, tiled=True)
    sums, code_gram = call(
        partial_kernel, (shape((rank, 2 * rank), F32), shape((rank // 2, 2 * rank), F32)),
        [VM, VM], (proj, patient_weight), vmem=60,
    )
    sums = sums + swap(sums, "pat", 8)
    sums, polar = lax.optimization_barrier((sums, polar))
    polar = lax.all_to_all(polar, "code", 0, 0, tiled=True)
    sums = plus(sums, [swap(sums, "pat", bit) for bit in (2, 4, 6)])
    mix_new, mix_again, mix_gram, weights, wgram, weight_new = call(
        mix_kernel,
        (
            square, square, square, shape((patients, rank), F32),
            shape((rank // 2, 2 * rank), F32), shape((own, rank), F32),
        ),
        [SM, VM, VM, VM, HBM],
        (place, sums, swap(sums, "pat", 1), code_gram, proj),
        [pltpu.VMEM(proj.shape, F32), pltpu.SemaphoreType.DMA(())], flops=8e9, vmem=60,
    )
    block = shape((half, rank, cols), F32)
    keep, send = call(
        numer_kernel, (block, block), [SM, SM, SM, SM, VM, VM, VM, VM],
        (place, tile_list, tile_count, visit_counts, polar, mix_again, weights, tiles),
        [pltpu.VMEM((n_pat, rank, cols), F32)], flops=4e9,
    )
    groups = [[core + 2 * i for i in range(half)] for core in (0, 1)]

    def exchange(x):
        return lax.all_to_all(x, "pat", 0, 0, axis_index_groups=groups, tiled=True)

    lanes = 2 * rank
    packed = call(
        pair_kernel, shape((half, cols // lanes + 1, rank, lanes), BF16), [VM] * 4,
        (keep, swap(send, "pat", 1), wgram, swap(wgram, "pat", 1)),
    )
    code = call(
        factor_kernel, shape((half, rank, cols), BF16), [VM, VM], (exchange(packed), mix_gram)
    )
    mine = exchange(code)
    place_scratch = [pltpu.VMEM(mine.shape, F32), pltpu.SemaphoreType.DMA((half,))]
    result = shape((rank, n_pat * cols), F32)
    came = swap(mine, "pat", 1)
    code_new = call(
        functools.partial(place_kernel, False), result, [SM, VM], (place, mine), place_scratch,
        spec=HBM,
    )
    code_new = call(
        functools.partial(place_kernel, True), result, [SM, VM, HBM], (place, came, code_new),
        place_scratch, spec=HBM, alias={2: 0},
    )
    return (code_new, mix_new, weight_new)


def solution(mesh):
    placed = (
        P("pat", "code", None, None, None),
        P("pat", "code", None, None),
        P("pat", "code"),
        P("pat"),
        P(None, "code"),
        P(),
        P("pat", None),
    )
    return jax.shard_map(
        body,
        mesh=mesh,
        in_specs=placed,
        out_specs=(P(None, "code"), P(), P(("pat", "code"), None)),
        check_vma=False,
    )
```

```python
import functools

import jax
import jax.numpy as jnp
from jax import lax
from jax.experimental import pallas as pl
from jax.experimental.pallas import tpu as pltpu
from jax.sharding import PartitionSpec as P

VBLOCKS = 2
NS_STEPS = 8
damping = 0.1
epsilon = 1e-06
F32, BF16, F16 = jnp.float32, jnp.bfloat16, jnp.float16
VM = pl.BlockSpec(memory_space=pltpu.VMEM)
HBM = pl.BlockSpec(memory_space=pl.ANY)
SM = pl.BlockSpec(memory_space=pltpu.SMEM)
MIB = 1024 * 1024


def mm(a, b, dims=((1,), (0,))):
    return lax.dot_general(
        a, b, (dims, ((), ())), precision=lax.Precision.HIGHEST, preferred_element_type=F32
    )


def mm16(a, b, dims=((1,), (0,))):
    return lax.dot_general(a, b, (dims, ((), ())), preferred_element_type=F32)


NT = ((1,), (1,))
TN = ((0,), (0,))


def split(x):
    high = x.astype(BF16)
    return high, (x - high.astype(F32)).astype(BF16)


def mm3(a, b, dims=((1,), (0,))):
    return mm16(a[0], b[0], dims) + (mm16(a[0], b[1], dims) + mm16(a[1], b[0], dims))


def fold(x):
    half = x.shape[1] // 2
    return x[:, :half] + x[:, half:]


def times2(x, y):
    return [[x[i][0] * y[0][j] + x[i][1] * y[1][j] for j in (0, 1)] for i in (0, 1)]


def inverse4(p):
    a = [[p[1][1], -p[0][1]], [-p[0][1], p[0][0]]]
    det = p[0][0] * p[1][1] - p[0][1] * p[0][1]
    b = [[p[0][2], p[0][3]], [p[1][2], p[1][3]]]
    t = times2(a, b)
    s00 = det * p[2][2] - (b[0][0] * t[0][0] + b[1][0] * t[1][0])
    s01 = det * p[2][3] - (b[0][0] * t[0][1] + b[1][0] * t[1][1])
    s11 = det * p[3][3] - (b[0][1] * t[0][1] + b[1][1] * t[1][1])
    over = 1.0 / (s00 * s11 - s01 * s01)
    over_det = 1.0 / det
    flip = [[s11, -s01], [-s01, s00]]
    u = times2(t, flip)
    v = times2(u, [[t[0][0], t[1][0]], [t[0][1], t[1][1]]])
    side = [[u[i][j] * over for j in (0, 1)] for i in (0, 1)]
    last = [[flip[i][j] * (det * over) for j in (0, 1)] for i in (0, 1)]
    first = [
        [a[i][j] * over_det + v[i][j] * (over * over_det) for j in (0, 1)] for i in (0, 1)
    ]
    return [
        [first[0][0], first[0][1], -side[0][0], -side[0][1]],
        [first[0][1], first[1][1], -side[1][0], -side[1][1]],
        [-side[0][0], -side[1][0], last[0][0], last[0][1]],
        [-side[0][1], -side[1][1], last[0][1], last[1][1]],
    ]


def halves(x):
    low = x.shape[0] // 2
    return jnp.concatenate([x[:low], x[low:]], axis=1)


def damped_inverse(gram):
    size = gram.shape[0]
    eye = lax.broadcasted_iota(jnp.int32, (size, size), 0) == lax.broadcasted_iota(
        jnp.int32, (size, size), 1
    )
    scale = size / jnp.sum(jnp.where(eye, gram, 0.0), keepdims=True)
    work = jnp.concatenate(
        [gram * scale + jnp.where(eye, damping, 0.0), eye.astype(F32)], axis=1
    )
    lanes = 2 * size
    blocks = [work[i : i + 8] for i in range(0, size, 8)]
    raw, fresh = [], []
    for j in range(0, size, 4):
        owner, at = j // 8, j % 8
        rows = [blocks[owner][at + i : at + i + 1] for i in range(4)]
        pivot = [
            [jnp.broadcast_to(row[:, j + k : j + k + 1], (1, lanes)) for k in range(4)]
            for row in rows
        ]
        inverse = inverse4(pivot)
        new = [
            (inverse[i][0] * rows[0] + inverse[i][1] * rows[1])
            + (inverse[i][2] * rows[2] + inverse[i][3] * rows[3])
            for i in range(4)
        ]
        raw += rows
        fresh += new
        for m in range(owner if at == 0 else owner + 1, len(blocks)):
            block = blocks[m]
            part = [block[:, j + k : j + k + 1] * new[k] for k in range(4)]
            blocks[m] = block - ((part[0] + part[1]) + (part[2] + part[3]))
    raw = jnp.concatenate(raw, axis=0)[:, size:]
    fresh = jnp.concatenate(fresh, axis=0)[:, size:]
    return scale * mm(raw, fresh, TN)


def live_rows(t, list_ref, count_ref, visits_ref, tile_rows):
    k, b, g = list_ref[0, 0, 0, t], list_ref[0, 1, 0, t], list_ref[0, 2, 0, t]
    kept = jnp.where(t < count_ref[0, 0], visits_ref[k] - tile_rows * b, 0)
    return k, b, g, kept


def products_kernel(
    list_ref, count_ref, visits_hbm, tile_ref, code_ref, out_ref, visits_ref, sem
):
    copy = pltpu.make_async_copy(visits_hbm, visits_ref, sem)
    copy.start()
    slots, rows, cols = tile_ref.shape
    rank = code_ref.shape[0]
    out_ref[...] = jnp.zeros(out_ref.shape, F32)
    lane = lax.broadcasted_iota(jnp.int32, (rank, rows), 1)
    copy.wait()
    for t in range(slots):
        k, b, g, kept = live_rows(t, list_ref, count_ref, visits_ref, rows)
        codes = code_ref[:, pl.ds(pl.multiple_of(g * cols, cols), cols)].astype(BF16)
        part = mm16(codes, tile_ref[t], NT)
        out_ref[k * VBLOCKS + b] += jnp.where(lane < kept, part, 0.0)


def gram_kernel(code_ref, out_ref):
    high, low = split(code_ref[...])
    cross = mm16(high, low, NT)
    out_ref[...] = halves(mm16(high, high, NT) + cross + cross.T)


def polar_kernel(
    scales, at_ref, prod_ref, mix_ref, weight_ref, gram_ref, sums_ref, out_ref
):
    dests = out_ref.shape[0]
    segs, rank, rows = prod_ref.shape
    own = segs // VBLOCKS
    eye = lax.broadcasted_iota(jnp.int32, (rank, rank), 0) == lax.broadcasted_iota(
        jnp.int32, (rank, rank), 1
    )
    prods, zs, weights = [], [], []
    for j in range(own):
        prods.append(
            split(jnp.concatenate([prod_ref[VBLOCKS * j + b] for b in range(VBLOCKS)], axis=1))
        )
        weights.append(weight_ref[pl.ds(at_ref[0] * own + j, 1), :])
        target = mm3(split(mix_ref[...] * weights[j]), prods[j])
        zs.append(target / jnp.sqrt(jnp.sum(target * target, keepdims=True) + epsilon))
    zs = [split(z) for z in zs]
    for _ in range(NS_STEPS):
        factors = [split(jnp.where(eye, 1.5, 0.0) - 0.5 * mm3(z, z, NT)) for z in zs]
        zs = [split(mm3(q, z)) for q, z in zip(factors, zs)]
    pieces = [z[0][:, b * rows : (b + 1) * rows] for z in zs for b in range(VBLOCKS)]
    numer = jnp.zeros((rank, rank), F32)
    for z, p, weight in zip(zs, prods, weights):
        projected = mm3(z, p, NT)
        numer += projected * weight
        pieces.append(jnp.concatenate(split(projected), axis=1))
    low = rank // 2
    weight = weight_ref[...]
    sums_ref[:low, :] = halves(numer)
    sums_ref[low:rank, :] = halves(mm(weight, weight, TN)) * scales[0]
    sums_ref[rank:, :] = gram_ref[...] * scales[1]
    for d in range(dests):
        for i, piece in enumerate(pieces):
            out_ref[d, i * rank : (i + 1) * rank, :] = piece


def whole(x):
    rank = x.shape[1] // 2
    return jnp.concatenate([x[:, :rank], x[:, rank:]], axis=0)


def mix_kernel(a_ref, b_ref, c_ref, d_ref, mix_ref, again_ref, mgram_ref, inverse_ref):
    sums = (a_ref[...] + b_ref[...]) + (c_ref[...] + d_ref[...])
    rank = mix_ref.shape[0]
    low = rank // 2
    weight_gram, code_gram = whole(sums[low:rank]), whole(sums[rank:])
    mix = mm(whole(sums[:low]), damped_inverse(code_gram * weight_gram))
    again_ref[...] = mix
    mix_ref[...] = mix
    mix_gram = mm(mix, mix, TN)
    mgram_ref[...] = mix_gram
    inverse_ref[...] = damped_inverse(mix_gram * code_gram)


def numer_kernel(
    place_ref, list_ref, count_ref, visits_ref, got_ref, mix_ref, inverse_ref, tile_ref,
    keep_ref, send_ref, wgram_ref, own_ref, acc_ref, weight_ref,
):
    slots, rows, cols = tile_ref.shape
    sources = got_ref.shape[0]
    rank = mix_ref.shape[0]
    own = own_ref.shape[0]
    first = own * VBLOCKS * rank
    mix = mix_ref[...]
    twice = jnp.concatenate([mix, mix], axis=1)
    terms = []
    for d in range(sources):
        for j in range(own):
            at = first + j * rank
            part = got_ref[d, at : at + rank, :].astype(F32) * twice
            terms.append(jnp.sum(part, axis=0, keepdims=True))
    weight = jnp.maximum(mm(fold(jnp.concatenate(terms, axis=0)), inverse_ref[...]), 0.0)
    weight_ref[...] = weight
    for j in range(own):
        own_ref[j : j + 1, :] = weight_ref[pl.ds(place_ref[0] * own + j, 1), :]
    wgram_ref[...] = halves(mm(weight, weight, TN))
    acc_ref[...] = jnp.zeros(acc_ref.shape, F32)
    lane = lax.broadcasted_iota(jnp.int32, (rank, rows), 1)
    for t in range(slots):
        k, b, g, kept = live_rows(t, list_ref, count_ref, visits_ref, rows)
        both = jnp.concatenate(split(mix * weight_ref[pl.ds(k, 1), :]), axis=0)
        at = pl.multiple_of((lax.rem(k, own) * VBLOCKS + b) * rank, rank)
        polar = got_ref[lax.div(k, own), pl.ds(at, rank), :]
        spread = mm16(both, jnp.concatenate([polar, polar], axis=0), TN)
        spread = jnp.where(lane < kept, spread, 0.0).astype(BF16)
        acc_ref[g] += mm16(spread, tile_ref[t])
    parity = place_ref[1]
    for j in range(keep_ref.shape[0]):
        keep_ref[j] = acc_ref[2 * j + parity]
        send_ref[j] = acc_ref[2 * j + 1 - parity]


def pair_kernel(keep_ref, came_ref, gram_a, gram_b, out_ref):
    low, lanes = gram_a.shape
    slabs = keep_ref.shape[2] // lanes
    piece = jnp.concatenate(split(gram_a[...] + gram_b[...]), axis=0)
    for j in range(keep_ref.shape[0]):
        both = (keep_ref[j] + came_ref[j]).astype(BF16)
        for i in range(slabs):
            out_ref[j, i] = both[:, i * lanes : (i + 1) * lanes]
        out_ref[j, slabs] = piece


def factor_kernel(got_ref, mgram_ref, out_ref):
    sources, slabs = got_ref.shape[0], got_ref.shape[1] - 1
    sums = []
    for i in range(slabs + 1):
        total = got_ref[0, i].astype(F32)
        for d in range(1, sources):
            total += got_ref[d, i].astype(F32)
        sums.append(total)
    low = sums[slabs].shape[0] // 2
    gram = whole(sums[slabs][:low] + sums[slabs][low:])
    inverse = damped_inverse(mgram_ref[...] * gram)
    code = jnp.maximum(mm(inverse, jnp.concatenate(sums[:slabs], axis=1)), 0.0).astype(BF16)
    for d in range(sources):
        out_ref[d] = code


def place_kernel(flip, place_ref, from_ref, *refs):
    out_hbm, wide_ref, sems = refs[-3:]
    parity = place_ref[1] if not flip else 1 - place_ref[1]
    cols = from_ref.shape[2]
    copies = []
    for j in range(from_ref.shape[0]):
        wide_ref[j] = from_ref[j].astype(F32)
        at = pl.multiple_of((2 * j + parity) * cols, cols)
        copies.append(
            pltpu.make_async_copy(wide_ref.at[j], out_hbm.at[:, pl.ds(at, cols)], sems.at[j])
        )
        copies[-1].start()
    for copy in copies:
        copy.wait()


def call(kernel, outs, specs, args, scratch=(), flops=1e9, spec=VM, alias=None, vmem=16):
    many = isinstance(outs, tuple)
    return pl.pallas_call(
        kernel,
        out_shape=outs,
        in_specs=specs,
        out_specs=(spec,) * len(outs) if many else spec,
        input_output_aliases=alias or {},
        scratch_shapes=scratch,
        compiler_params=pltpu.CompilerParams(vmem_limit_bytes=vmem * MIB),
        cost_estimate=pl.CostEstimate(flops=int(flops), bytes_accessed=65536, transcendentals=0),
    )(*args)


def swap(x, axis, bit):
    size = lax.axis_size(axis)
    return lax.ppermute(x, axis, [(i, i ^ bit) for i in range(size)])


def swap_z(x, high, low):
    n_pat, n_code = lax.axis_size("pat"), lax.axis_size("code")
    pairs = [
        (p * n_code + c, (p ^ (high * n_pat // 2)) * n_code + (c ^ (low * n_code // 2)))
        for p in range(n_pat)
        for c in range(n_code)
    ]
    return lax.ppermute(x, ("pat", "code"), pairs)


def plus(x, parts):
    for part in parts:
        x = x + part
    return x


def body(tile_data, tile_list, tile_count, visit_counts, code_factor_t, visit_mix, patient_weight):
    tiles = tile_data[0, 0]
    tile_list = jnp.transpose(tile_list, (0, 2, 1, 3))
    slots, rows, cols = tiles.shape
    rank = visit_mix.shape[0]
    patients = visit_counts.shape[0]
    n_code, n_pat = lax.axis_size("code"), lax.axis_size("pat")
    half = n_pat // 2
    own = patients // n_code
    code_at, pat_at = lax.axis_index("code"), lax.axis_index("pat")
    place = jnp.stack([code_at, lax.rem(pat_at, 2)]).astype(jnp.int32)
    shape = jax.ShapeDtypeStruct
    square = shape((rank, rank), F32)

    partial = call(
        products_kernel, shape((patients * VBLOCKS, rank, rows), F32), [SM, SM, HBM, VM, VM],
        (tile_list, tile_count, visit_counts, tiles, code_factor_t),
        [pltpu.SMEM(visit_counts.shape, jnp.int32), pltpu.SemaphoreType.DMA(())],
    )
    sent = partial.astype(F16).reshape(n_code, own * VBLOCKS * rank, rows)
    got = lax.all_to_all(sent, "code", 0, 0, tiled=True)
    gram = call(gram_kernel, shape((rank // 2, 2 * rank), F32), [VM], (code_factor_t,))
    products = jnp.sum(got.astype(F32), axis=0).reshape(own * VBLOCKS, rank, rows)

    scales = (1.0 / n_code, 1.0 / n_pat)
    length = (own * VBLOCKS + own) * rank
    sums, message = call(
        functools.partial(polar_kernel, scales),
        (shape((3 * rank // 2, 2 * rank), F32), shape((n_code, length, rows), BF16)),
        [SM, VM, VM, VM, VM], (place, products, visit_mix, patient_weight, gram), flops=5e9,
    )
    shared = lax.all_to_all(message, "code", 0, 0, tiled=True)
    sums = plus(sums, [swap(sums, "pat", bit) for bit in (2, 4, 6)])
    sums = sums + swap(sums, "pat", 1)
    sums = plus(sums, [swap_z(sums, high, low) for high, low in ((0, 1), (1, 0), (1, 1))])
    mix_new, mix_again, mix_gram, inverse = call(
        mix_kernel, (square,) * 4, [VM] * 4,
        (sums, *(swap(sums, "code", bit) for bit in (1, 2, 3))), flops=5e9,
    )
    block = shape((half, rank, cols), F32)
    keep, send, wgram, weight_new = call(
        numer_kernel,
        (block, block, shape((rank // 2, 2 * rank), F32), shape((own, rank), F32)),
        [SM, SM, SM, SM, VM, VM, VM, VM],
        (place, tile_list, tile_count, visit_counts, shared, mix_again, inverse, tiles),
        [pltpu.VMEM((n_pat, rank, cols), F32), pltpu.VMEM((patients, rank), F32)], flops=5e9,
    )
    groups = [[core + 2 * i for i in range(half)] for core in (0, 1)]

    def exchange(x):
        return lax.all_to_all(x, "pat", 0, 0, axis_index_groups=groups, tiled=True)

    lanes = 2 * rank
    packed = call(
        pair_kernel, shape((half, cols // lanes + 1, rank, lanes), BF16), [VM] * 4,
        (keep, swap(send, "pat", 1), wgram, swap(wgram, "pat", 1)),
    )
    code = call(
        factor_kernel, shape((half, rank, cols), BF16), [VM, VM], (exchange(packed), mix_gram)
    )
    mine = exchange(code)
    place_scratch = [pltpu.VMEM(mine.shape, F32), pltpu.SemaphoreType.DMA((half,))]
    result = shape((rank, n_pat * cols), F32)
    came = swap(mine, "pat", 1)
    code_new = call(
        functools.partial(place_kernel, False), result, [SM, VM], (place, mine), place_scratch,
        spec=HBM,
    )
    code_new = call(
        functools.partial(place_kernel, True), result, [SM, VM, HBM], (place, came, code_new),
        place_scratch, spec=HBM, alias={2: 0},
    )
    return (code_new, mix_new, weight_new)


def solution(mesh):
    placed = (
        P("pat", "code", None, None, None),
        P("pat", "code", None, None),
        P("pat", "code"),
        P("pat"),
        P(None, "code"),
        P(),
        P("pat", None),
    )
    return jax.shard_map(
        body,
        mesh=mesh,
        in_specs=placed,
        out_specs=(P(None, "code"), P(), P(("pat", "code"), None)),
        check_vma=False,
    )
```

```python
import functools

import jax
import jax.numpy as jnp
from jax import lax
from jax.experimental import pallas as pl
from jax.experimental.pallas import tpu as pltpu
from jax.sharding import PartitionSpec as P

VBLOCKS = 2
NS_STEPS = 8
damping = 0.1
epsilon = 1e-06
F32, BF16, F16 = jnp.float32, jnp.bfloat16, jnp.float16
VM = pl.BlockSpec(memory_space=pltpu.VMEM)
HBM = pl.BlockSpec(memory_space=pl.ANY)
SM = pl.BlockSpec(memory_space=pltpu.SMEM)
MIB = 1024 * 1024


def mm(a, b, dims=((1,), (0,))):
    return lax.dot_general(
        a, b, (dims, ((), ())), precision=lax.Precision.HIGHEST, preferred_element_type=F32
    )


def mm16(a, b, dims=((1,), (0,))):
    return lax.dot_general(a, b, (dims, ((), ())), preferred_element_type=F32)


NT = ((1,), (1,))
TN = ((0,), (0,))


def split(x):
    high = x.astype(BF16)
    return high, (x - high.astype(F32)).astype(BF16)


def mm3(a, b, dims=((1,), (0,))):
    return mm16(a[0], b[0], dims) + (mm16(a[0], b[1], dims) + mm16(a[1], b[0], dims))


def fold(x):
    half = x.shape[1] // 2
    return x[:, :half] + x[:, half:]


def times2(x, y):
    return [[x[i][0] * y[0][j] + x[i][1] * y[1][j] for j in (0, 1)] for i in (0, 1)]


def inverse4(p):
    a = [[p[1][1], -p[0][1]], [-p[0][1], p[0][0]]]
    det = p[0][0] * p[1][1] - p[0][1] * p[0][1]
    b = [[p[0][2], p[0][3]], [p[1][2], p[1][3]]]
    t = times2(a, b)
    s00 = det * p[2][2] - (b[0][0] * t[0][0] + b[1][0] * t[1][0])
    s01 = det * p[2][3] - (b[0][0] * t[0][1] + b[1][0] * t[1][1])
    s11 = det * p[3][3] - (b[0][1] * t[0][1] + b[1][1] * t[1][1])
    over = 1.0 / (s00 * s11 - s01 * s01)
    over_det = 1.0 / det
    flip = [[s11, -s01], [-s01, s00]]
    u = times2(t, flip)
    v = times2(u, [[t[0][0], t[1][0]], [t[0][1], t[1][1]]])
    side = [[u[i][j] * over for j in (0, 1)] for i in (0, 1)]
    last = [[flip[i][j] * (det * over) for j in (0, 1)] for i in (0, 1)]
    first = [
        [a[i][j] * over_det + v[i][j] * (over * over_det) for j in (0, 1)] for i in (0, 1)
    ]
    return [
        [first[0][0], first[0][1], -side[0][0], -side[0][1]],
        [first[0][1], first[1][1], -side[1][0], -side[1][1]],
        [-side[0][0], -side[1][0], last[0][0], last[0][1]],
        [-side[0][1], -side[1][1], last[0][1], last[1][1]],
    ]


def halves(x):
    low = x.shape[0] // 2
    return jnp.concatenate([x[:low], x[low:]], axis=1)


def damped_inverse(gram):
    size = gram.shape[0]
    eye = lax.broadcasted_iota(jnp.int32, (size, size), 0) == lax.broadcasted_iota(
        jnp.int32, (size, size), 1
    )
    scale = size / jnp.sum(jnp.where(eye, gram, 0.0), keepdims=True)
    work = jnp.concatenate(
        [gram * scale + jnp.where(eye, damping, 0.0), eye.astype(F32)], axis=1
    )
    lanes = 2 * size
    blocks = [work[i : i + 8] for i in range(0, size, 8)]
    raw, fresh = [], []
    for j in range(0, size, 4):
        owner, at = j // 8, j % 8
        rows = [blocks[owner][at + i : at + i + 1] for i in range(4)]
        pivot = [
            [jnp.broadcast_to(row[:, j + k : j + k + 1], (1, lanes)) for k in range(4)]
            for row in rows
        ]
        inverse = inverse4(pivot)
        new = [
            (inverse[i][0] * rows[0] + inverse[i][1] * rows[1])
            + (inverse[i][2] * rows[2] + inverse[i][3] * rows[3])
            for i in range(4)
        ]
        raw += rows
        fresh += new
        for m in range(owner if at == 0 else owner + 1, len(blocks)):
            block = blocks[m]
            part = [block[:, j + k : j + k + 1] * new[k] for k in range(4)]
            blocks[m] = block - ((part[0] + part[1]) + (part[2] + part[3]))
    raw = jnp.concatenate(raw, axis=0)[:, size:]
    fresh = jnp.concatenate(fresh, axis=0)[:, size:]
    return scale * mm(raw, fresh, TN)


def live_rows(t, list_ref, count_ref, visits_ref, tile_rows):
    k, b, g = list_ref[0, 0, 0, t], list_ref[0, 1, 0, t], list_ref[0, 2, 0, t]
    kept = jnp.where(t < count_ref[0, 0], visits_ref[k] - tile_rows * b, 0)
    return k, b, g, kept


def products_kernel(
    list_hbm, count_hbm, visits_hbm, tile_hbm, code_hbm, out_ref,
    list_ref, count_ref, visits_ref, tile_ref, code_ref, small_sems, sems,
):
    slots, rows, cols = tile_ref.shape
    rank = code_ref.shape[0]
    parts = sems.shape[0] - 1
    each = slots // parts
    small = []
    for i, (src, dst) in enumerate(
        ((list_hbm, list_ref), (count_hbm, count_ref), (visits_hbm, visits_ref))
    ):
        small.append(pltpu.make_async_copy(src, dst, small_sems.at[i]))
        small[-1].start()
    code_copy = pltpu.make_async_copy(code_hbm, code_ref, sems.at[parts])
    code_copy.start()
    copies = []
    for i in range(parts):
        at = pl.ds(i * each, each)
        copies.append(pltpu.make_async_copy(tile_hbm.at[0, 0, at], tile_ref.at[at], sems.at[i]))
        copies[-1].start()
    out_ref[...] = jnp.zeros(out_ref.shape, F32)
    lane = lax.broadcasted_iota(jnp.int32, (rank, rows), 1)
    for copy in small:
        copy.wait()
    code_copy.wait()
    for t in range(slots):
        if t % each == 0:
            copies[t // each].wait()
        k, b, g, kept = live_rows(t, list_ref, count_ref, visits_ref, rows)
        codes = code_ref[:, pl.ds(pl.multiple_of(g * cols, cols), cols)].astype(BF16)
        part = mm16(codes, tile_ref[t], NT)
        out_ref[k * VBLOCKS + b] += jnp.where(lane < kept, part, 0.0)


def gram_kernel(code_ref, out_ref):
    high, low = split(code_ref[...])
    cross = mm16(high, low, NT)
    out_ref[...] = halves(mm16(high, high, NT) + cross + cross.T)


def polar_kernel(
    scales, at_ref, prod_ref, mix_ref, weight_ref, gram_ref, sums_ref, out_ref
):
    segs, rank, rows = prod_ref.shape
    own = segs // VBLOCKS
    eye = lax.broadcasted_iota(jnp.int32, (rank, rank), 0) == lax.broadcasted_iota(
        jnp.int32, (rank, rank), 1
    )
    prods, zs, weights = [], [], []
    for j in range(own):
        prods.append(
            split(jnp.concatenate([prod_ref[VBLOCKS * j + b] for b in range(VBLOCKS)], axis=1))
        )
        weights.append(weight_ref[pl.ds(at_ref[0] * own + j, 1), :])
        target = mm3(split(mix_ref[...] * weights[j]), prods[j])
        zs.append(target / jnp.sqrt(jnp.sum(target * target, keepdims=True) + epsilon))
    zs = [split(z) for z in zs]
    for _ in range(NS_STEPS):
        factors = [split(jnp.where(eye, 1.5, 0.0) - 0.5 * mm3(z, z, NT)) for z in zs]
        zs = [split(mm3(q, z)) for q, z in zip(factors, zs)]
    pieces = [z[0][:, b * rows : (b + 1) * rows] for z in zs for b in range(VBLOCKS)]
    numer = jnp.zeros((rank, rank), F32)
    for z, p, weight in zip(zs, prods, weights):
        projected = mm3(z, p, NT)
        numer += projected * weight
        pieces.append(jnp.concatenate(split(projected), axis=1))
    low = rank // 2
    weight = weight_ref[...]
    sums_ref[:low, :] = halves(numer)
    sums_ref[low:rank, :] = halves(mm(weight, weight, TN)) * scales[0]
    sums_ref[rank:, :] = gram_ref[...] * scales[1]
    for i, piece in enumerate(pieces):
        out_ref[i * rank : (i + 1) * rank, :] = piece


def whole(x):
    rank = x.shape[1] // 2
    return jnp.concatenate([x[:, :rank], x[:, rank:]], axis=0)


def mix_kernel(a_ref, b_ref, c_ref, d_ref, mix_ref, again_ref, mgram_ref, inverse_ref):
    sums = (a_ref[...] + b_ref[...]) + (c_ref[...] + d_ref[...])
    rank = mix_ref.shape[0]
    low = rank // 2
    weight_gram, code_gram = whole(sums[low:rank]), whole(sums[rank:])
    mix = mm(whole(sums[:low]), damped_inverse(code_gram * weight_gram))
    again_ref[...] = mix
    mix_ref[...] = mix
    mix_gram = mm(mix, mix, TN)
    mgram_ref[...] = mix_gram
    inverse_ref[...] = damped_inverse(mix_gram * code_gram)


def numer_kernel(
    place_ref, list_ref, count_ref, visits_ref, got_ref, mix_ref, inverse_ref, tile_ref,
    keep_ref, send_ref, wgram_ref, own_ref, acc_ref, weight_ref,
):
    slots, rows, cols = tile_ref.shape
    sources = got_ref.shape[0]
    rank = mix_ref.shape[0]
    own = own_ref.shape[0]
    first = own * VBLOCKS * rank
    layers = 2
    z_at = lax.div(place_ref[0], sources // layers)

    def source(d):
        x_at, layer = lax.rem(d, sources // layers), lax.div(d, sources // layers)
        return x_at * layers + jnp.where(layer == z_at, 0, 1)

    mix = mix_ref[...]
    twice = jnp.concatenate([mix, mix], axis=1)
    terms = []
    for d in range(sources):
        for j in range(own):
            at = first + j * rank
            part = got_ref[d, at : at + rank, :].astype(F32) * twice
            terms.append(jnp.sum(part, axis=0, keepdims=True))
    weight = jnp.maximum(mm(fold(jnp.concatenate(terms, axis=0)), inverse_ref[...]), 0.0)
    weight_ref[...] = weight
    for j in range(own):
        own_ref[j : j + 1, :] = weight_ref[pl.ds(source(place_ref[0]) * own + j, 1), :]
    wgram_ref[...] = halves(mm(weight, weight, TN))
    acc_ref[...] = jnp.zeros(acc_ref.shape, F32)
    lane = lax.broadcasted_iota(jnp.int32, (rank, rows), 1)
    for t in range(slots):
        k, b, g, kept = live_rows(t, list_ref, count_ref, visits_ref, rows)
        d, j = source(lax.div(k, own)), lax.rem(k, own)
        both = jnp.concatenate(split(mix * weight_ref[pl.ds(d * own + j, 1), :]), axis=0)
        at = pl.multiple_of((j * VBLOCKS + b) * rank, rank)
        polar = got_ref[d, pl.ds(at, rank), :]
        spread = mm16(both, jnp.concatenate([polar, polar], axis=0), TN)
        spread = jnp.where(lane < kept, spread, 0.0).astype(BF16)
        acc_ref[g] += mm16(spread, tile_ref[t])
    parity = place_ref[1]
    for j in range(keep_ref.shape[0]):
        keep_ref[j] = acc_ref[2 * j + parity]
        send_ref[j] = acc_ref[2 * j + 1 - parity]


def pair_kernel(keep_ref, came_ref, gram_a, gram_b, out_ref):
    low, lanes = gram_a.shape
    slabs = keep_ref.shape[2] // lanes
    piece = jnp.concatenate(split(gram_a[...] + gram_b[...]), axis=0)
    for j in range(keep_ref.shape[0]):
        both = (keep_ref[j] + came_ref[j]).astype(BF16)
        for i in range(slabs):
            out_ref[j, i] = both[:, i * lanes : (i + 1) * lanes]
        out_ref[j, slabs] = piece


def factor_kernel(got_ref, mgram_ref, out_ref):
    sources, slabs = got_ref.shape[0], got_ref.shape[1] - 1
    sums = []
    for i in range(slabs + 1):
        total = got_ref[0, i].astype(F32)
        for d in range(1, sources):
            total += got_ref[d, i].astype(F32)
        sums.append(total)
    low = sums[slabs].shape[0] // 2
    gram = whole(sums[slabs][:low] + sums[slabs][low:])
    inverse = damped_inverse(mgram_ref[...] * gram)
    code = jnp.maximum(mm(inverse, jnp.concatenate(sums[:slabs], axis=1)), 0.0).astype(BF16)
    for d in range(sources):
        out_ref[d] = code


def place_kernel(flip, place_ref, from_ref, *refs):
    out_hbm, wide_ref, sems = refs[-3:]
    parity = place_ref[1] if not flip else 1 - place_ref[1]
    cols = from_ref.shape[2]
    copies = []
    for j in range(from_ref.shape[0]):
        wide_ref[j] = from_ref[j].astype(F32)
        at = pl.multiple_of((2 * j + parity) * cols, cols)
        copies.append(
            pltpu.make_async_copy(wide_ref.at[j], out_hbm.at[:, pl.ds(at, cols)], sems.at[j])
        )
        copies[-1].start()
    for copy in copies:
        copy.wait()


def call(kernel, outs, specs, args, scratch=(), flops=1e9, spec=VM, alias=None, vmem=16):
    many = isinstance(outs, tuple)
    return pl.pallas_call(
        kernel,
        out_shape=outs,
        in_specs=specs,
        out_specs=(spec,) * len(outs) if many else spec,
        input_output_aliases=alias or {},
        scratch_shapes=scratch,
        compiler_params=pltpu.CompilerParams(vmem_limit_bytes=vmem * MIB),
        cost_estimate=pl.CostEstimate(flops=int(flops), bytes_accessed=65536, transcendentals=0),
    )(*args)


def swap(x, axis, bit):
    size = lax.axis_size(axis)
    return lax.ppermute(x, axis, [(i, i ^ bit) for i in range(size)])


def swap_z(x, high, low):
    n_pat, n_code = lax.axis_size("pat"), lax.axis_size("code")
    pairs = [
        (p * n_code + c, (p ^ (high * n_pat // 2)) * n_code + (c ^ (low * n_code // 2)))
        for p in range(n_pat)
        for c in range(n_code)
    ]
    return lax.ppermute(x, ("pat", "code"), pairs)


def plus(x, parts):
    for part in parts:
        x = x + part
    return x


def body(tile_data, tile_list, tile_count, visit_counts, code_factor_t, visit_mix, patient_weight):
    tiles = tile_data[0, 0]
    tile_list = jnp.transpose(tile_list, (0, 2, 1, 3))
    slots, rows, cols = tiles.shape
    rank = visit_mix.shape[0]
    patients = visit_counts.shape[0]
    n_code, n_pat = lax.axis_size("code"), lax.axis_size("pat")
    half = n_pat // 2
    own = patients // n_code
    code_at, pat_at = lax.axis_index("code"), lax.axis_index("pat")
    place = jnp.stack([code_at, lax.rem(pat_at, 2)]).astype(jnp.int32)
    shape = jax.ShapeDtypeStruct
    square = shape((rank, rank), F32)

    partial = call(
        products_kernel, shape((patients * VBLOCKS, rank, rows), F32), [HBM] * 5,
        (tile_list, tile_count, visit_counts, tile_data, code_factor_t),
        [
            pltpu.SMEM(tile_list.shape, jnp.int32), pltpu.SMEM(tile_count.shape, jnp.int32),
            pltpu.SMEM(visit_counts.shape, jnp.int32), pltpu.VMEM(tiles.shape, BF16),
            pltpu.VMEM(code_factor_t.shape, F32), pltpu.SemaphoreType.DMA((3,)),
            pltpu.SemaphoreType.DMA((5,)),
        ],
        vmem=50,
    )
    sent = partial.astype(F16).reshape(n_code, own * VBLOCKS * rank, rows)
    got = lax.all_to_all(sent, "code", 0, 0, tiled=True)
    gram = call(gram_kernel, shape((rank // 2, 2 * rank), F32), [VM], (code_factor_t,))
    products = jnp.sum(got.astype(F32), axis=0).reshape(own * VBLOCKS, rank, rows)

    scales = (1.0 / n_code, 1.0 / n_pat)
    length = (own * VBLOCKS + own) * rank
    sums, message = call(
        functools.partial(polar_kernel, scales),
        (shape((3 * rank // 2, 2 * rank), F32), shape((length, rows), BF16)),
        [SM, VM, VM, VM, VM], (place, products, visit_mix, patient_weight, gram), flops=5e9,
    )
    quarter = n_code // 2
    other = swap(message, "code", quarter)
    sums = plus(sums, [swap(sums, "code", bit) for bit in (1, 2, 3)])
    sums, message, other = lax.optimization_barrier((sums, message, other))
    message = jnp.broadcast_to(jnp.concatenate([message, other])[None], (quarter, 2 * length, rows))
    layers = [[z * quarter + i for i in range(quarter)] for z in (0, 1)]
    shared = lax.all_to_all(message, "code", 0, 0, axis_index_groups=layers, tiled=True)
    shared = shared.reshape(n_code, length, rows)
    sums = plus(sums, [swap(sums, "pat", bit) for bit in (2, 4, 6)])
    sums = sums + swap(sums, "pat", 1)
    mix_new, mix_again, mix_gram, inverse = call(
        mix_kernel, (square,) * 4, [VM] * 4,
        (sums, *(swap_z(sums, high, low) for high, low in ((0, 1), (1, 0), (1, 1)))), flops=5e9,
    )
    block = shape((half, rank, cols), F32)
    keep, send, wgram, weight_new = call(
        numer_kernel,
        (block, block, shape((rank // 2, 2 * rank), F32), shape((own, rank), F32)),
        [SM, SM, SM, SM, VM, VM, VM, VM],
        (place, tile_list, tile_count, visit_counts, shared, mix_again, inverse, tiles),
        [pltpu.VMEM((n_pat, rank, cols), F32), pltpu.VMEM((patients, rank), F32)], flops=5e9,
    )
    groups = [[core + 2 * i for i in range(half)] for core in (0, 1)]

    def exchange(x):
        return lax.all_to_all(x, "pat", 0, 0, axis_index_groups=groups, tiled=True)

    lanes = 2 * rank
    packed = call(
        pair_kernel, shape((half, cols // lanes + 1, rank, lanes), BF16), [VM] * 4,
        (keep, swap(send, "pat", 1), wgram, swap(wgram, "pat", 1)),
    )
    code = call(
        factor_kernel, shape((half, rank, cols), BF16), [VM, VM], (exchange(packed), mix_gram)
    )
    mine = exchange(code)
    place_scratch = [pltpu.VMEM(mine.shape, F32), pltpu.SemaphoreType.DMA((half,))]
    result = shape((rank, n_pat * cols), F32)
    came = swap(mine, "pat", 1)
    code_new = call(
        functools.partial(place_kernel, False), result, [SM, VM], (place, mine), place_scratch,
        spec=HBM,
    )
    code_new = call(
        functools.partial(place_kernel, True), result, [SM, VM, HBM], (place, came, code_new),
        place_scratch, spec=HBM, alias={2: 0},
    )
    return (code_new, mix_new, weight_new)


def solution(mesh):
    placed = (
        P("pat", "code", None, None, None),
        P("pat", "code", None, None),
        P("pat", "code"),
        P("pat"),
        P(None, "code"),
        P(),
        P("pat", None),
    )
    return jax.shard_map(
        body,
        mesh=mesh,
        in_specs=placed,
        out_specs=(P(None, "code"), P(), P(("pat", "code"), None)),
        check_vma=False,
    )
```

```python
import functools

import jax
import jax.numpy as jnp
from jax import lax
from jax.experimental import pallas as pl
from jax.experimental.pallas import tpu as pltpu
from jax.sharding import PartitionSpec as P

VBLOCKS = 2
NS_STEPS = 8
damping = 0.1
epsilon = 1e-06
F32, BF16, F16 = jnp.float32, jnp.bfloat16, jnp.float16
VM = pl.BlockSpec(memory_space=pltpu.VMEM)
HBM = pl.BlockSpec(memory_space=pl.ANY)
SM = pl.BlockSpec(memory_space=pltpu.SMEM)
MIB = 1024 * 1024


def mm(a, b, dims=((1,), (0,))):
    return lax.dot_general(
        a, b, (dims, ((), ())), precision=lax.Precision.HIGHEST, preferred_element_type=F32
    )


def mm16(a, b, dims=((1,), (0,))):
    return lax.dot_general(a, b, (dims, ((), ())), preferred_element_type=F32)


NT = ((1,), (1,))
TN = ((0,), (0,))


def split(x):
    high = x.astype(BF16)
    return high, (x - high.astype(F32)).astype(BF16)


def mm3(a, b, dims=((1,), (0,))):
    return mm16(a[0], b[0], dims) + (mm16(a[0], b[1], dims) + mm16(a[1], b[0], dims))


def fold(x):
    half = x.shape[1] // 2
    return x[:, :half] + x[:, half:]


def times2(x, y):
    return [[x[i][0] * y[0][j] + x[i][1] * y[1][j] for j in (0, 1)] for i in (0, 1)]


def inverse4(p):
    a = [[p[1][1], -p[0][1]], [-p[0][1], p[0][0]]]
    det = p[0][0] * p[1][1] - p[0][1] * p[0][1]
    b = [[p[0][2], p[0][3]], [p[1][2], p[1][3]]]
    t = times2(a, b)
    s00 = det * p[2][2] - (b[0][0] * t[0][0] + b[1][0] * t[1][0])
    s01 = det * p[2][3] - (b[0][0] * t[0][1] + b[1][0] * t[1][1])
    s11 = det * p[3][3] - (b[0][1] * t[0][1] + b[1][1] * t[1][1])
    over = 1.0 / (s00 * s11 - s01 * s01)
    over_det = 1.0 / det
    flip = [[s11, -s01], [-s01, s00]]
    u = times2(t, flip)
    v = times2(u, [[t[0][0], t[1][0]], [t[0][1], t[1][1]]])
    side = [[u[i][j] * over for j in (0, 1)] for i in (0, 1)]
    last = [[flip[i][j] * (det * over) for j in (0, 1)] for i in (0, 1)]
    first = [
        [a[i][j] * over_det + v[i][j] * (over * over_det) for j in (0, 1)] for i in (0, 1)
    ]
    return [
        [first[0][0], first[0][1], -side[0][0], -side[0][1]],
        [first[0][1], first[1][1], -side[1][0], -side[1][1]],
        [-side[0][0], -side[1][0], last[0][0], last[0][1]],
        [-side[0][1], -side[1][1], last[0][1], last[1][1]],
    ]


def halves(x):
    low = x.shape[0] // 2
    return jnp.concatenate([x[:low], x[low:]], axis=1)


def damped_inverse(gram):
    size = gram.shape[0]
    eye = lax.broadcasted_iota(jnp.int32, (size, size), 0) == lax.broadcasted_iota(
        jnp.int32, (size, size), 1
    )
    scale = size / jnp.sum(jnp.where(eye, gram, 0.0), keepdims=True)
    work = jnp.concatenate(
        [gram * scale + jnp.where(eye, damping, 0.0), eye.astype(F32)], axis=1
    )
    lanes = 2 * size
    blocks = [work[i : i + 8] for i in range(0, size, 8)]
    raw, fresh = [], []
    for j in range(0, size, 4):
        owner, at = j // 8, j % 8
        rows = [blocks[owner][at + i : at + i + 1] for i in range(4)]
        pivot = [
            [jnp.broadcast_to(row[:, j + k : j + k + 1], (1, lanes)) for k in range(4)]
            for row in rows
        ]
        inverse = inverse4(pivot)
        new = [
            (inverse[i][0] * rows[0] + inverse[i][1] * rows[1])
            + (inverse[i][2] * rows[2] + inverse[i][3] * rows[3])
            for i in range(4)
        ]
        raw += rows
        fresh += new
        for m in range(owner if at == 0 else owner + 1, len(blocks)):
            block = blocks[m]
            part = [block[:, j + k : j + k + 1] * new[k] for k in range(4)]
            blocks[m] = block - ((part[0] + part[1]) + (part[2] + part[3]))
    raw = jnp.concatenate(raw, axis=0)[:, size:]
    fresh = jnp.concatenate(fresh, axis=0)[:, size:]
    return scale * mm(raw, fresh, TN)


def live_rows(t, list_ref, count_ref, visits_ref, tile_rows):
    k, b, g = list_ref[0, 0, 0, t], list_ref[0, 1, 0, t], list_ref[0, 2, 0, t]
    kept = jnp.where(t < count_ref[0, 0], visits_ref[k] - tile_rows * b, 0)
    return k, b, g, kept


def products_kernel(
    list_hbm, count_hbm, visits_hbm, tile_hbm, code_hbm, out_ref,
    list_ref, count_ref, visits_ref, tile_ref, code_ref, small_sems, sems,
):
    slots, rows, cols = tile_ref.shape
    rank = code_ref.shape[0]
    parts = sems.shape[0] - 1
    each = slots // parts
    small = []
    for i, (src, dst) in enumerate(
        ((list_hbm, list_ref), (count_hbm, count_ref), (visits_hbm, visits_ref))
    ):
        small.append(pltpu.make_async_copy(src, dst, small_sems.at[i]))
        small[-1].start()
    code_copy = pltpu.make_async_copy(code_hbm, code_ref, sems.at[parts])
    code_copy.start()
    copies = []
    for i in range(parts):
        at = pl.ds(i * each, each)
        copies.append(pltpu.make_async_copy(tile_hbm.at[0, 0, at], tile_ref.at[at], sems.at[i]))
        copies[-1].start()
    out_ref[...] = jnp.zeros(out_ref.shape, F32)
    lane = lax.broadcasted_iota(jnp.int32, (rank, rows), 1)
    for copy in small:
        copy.wait()
    code_copy.wait()
    for t in range(slots):
        if t % each == 0:
            copies[t // each].wait()
        k, b, g, kept = live_rows(t, list_ref, count_ref, visits_ref, rows)
        codes = code_ref[:, pl.ds(pl.multiple_of(g * cols, cols), cols)].astype(BF16)
        part = mm16(codes, tile_ref[t], NT)
        out_ref[k * VBLOCKS + b] += jnp.where(lane < kept, part, 0.0)


def gram_kernel(code_ref, out_ref):
    high, low = split(code_ref[...])
    cross = mm16(high, low, NT)
    out_ref[...] = halves(mm16(high, high, NT) + cross + cross.T)


def polar_kernel(
    scales, at_ref, prod_ref, mix_ref, weight_ref, gram_ref, sums_ref, out_ref
):
    segs, rank, rows = prod_ref.shape
    own = segs // VBLOCKS
    eye = lax.broadcasted_iota(jnp.int32, (rank, rank), 0) == lax.broadcasted_iota(
        jnp.int32, (rank, rank), 1
    )
    prods, zs, weights = [], [], []
    for j in range(own):
        prods.append(
            split(jnp.concatenate([prod_ref[VBLOCKS * j + b] for b in range(VBLOCKS)], axis=1))
        )
        weights.append(weight_ref[pl.ds(at_ref[0] * own + j, 1), :])
        target = mm3(split(mix_ref[...] * weights[j]), prods[j])
        zs.append(target / jnp.sqrt(jnp.sum(target * target, keepdims=True) + epsilon))
    zs = [split(z) for z in zs]
    for _ in range(NS_STEPS):
        factors = [split(jnp.where(eye, 1.5, 0.0) - 0.5 * mm3(z, z, NT)) for z in zs]
        zs = [split(mm3(q, z)) for q, z in zip(factors, zs)]
    pieces = [z[0][:, b * rows : (b + 1) * rows] for z in zs for b in range(VBLOCKS)]
    numer = jnp.zeros((rank, rank), F32)
    for z, p, weight in zip(zs, prods, weights):
        projected = mm3(z, p, NT)
        numer += projected * weight
        pieces.append(jnp.concatenate(split(projected), axis=1))
    low = rank // 2
    weight = weight_ref[...]
    sums_ref[:low, :] = halves(numer)
    sums_ref[low:rank, :] = halves(mm(weight, weight, TN)) * scales[0]
    sums_ref[rank:, :] = gram_ref[...] * scales[1]
    for i, piece in enumerate(pieces):
        out_ref[i * rank : (i + 1) * rank, :] = piece


def whole(x):
    rank = x.shape[1] // 2
    return jnp.concatenate([x[:, :rank], x[:, rank:]], axis=0)


def mix_kernel(a_ref, b_ref, c_ref, d_ref, mix_ref, again_ref, mgram_ref, inverse_ref):
    sums = (a_ref[...] + b_ref[...]) + (c_ref[...] + d_ref[...])
    rank = mix_ref.shape[0]
    low = rank // 2
    weight_gram, code_gram = whole(sums[low:rank]), whole(sums[rank:])
    mix = mm(whole(sums[:low]), damped_inverse(code_gram * weight_gram))
    again_ref[...] = mix
    mix_ref[...] = mix
    mix_gram = mm(mix, mix, TN)
    mgram_ref[...] = mix_gram
    inverse_ref[...] = damped_inverse(mix_gram * code_gram)


def numer_kernel(
    place_ref, list_ref, count_ref, visits_ref, got_ref, mix_ref, inverse_ref, tile_ref,
    keep_ref, send_ref, wgram_ref, own_ref, acc_ref, weight_ref,
):
    slots, rows, cols = tile_ref.shape
    sources = got_ref.shape[0]
    rank = mix_ref.shape[0]
    own = own_ref.shape[0]
    first = own * VBLOCKS * rank
    layers = 2
    z_at = lax.div(place_ref[0], sources // layers)

    def source(d):
        x_at, layer = lax.rem(d, sources // layers), lax.div(d, sources // layers)
        return x_at * layers + jnp.where(layer == z_at, 0, 1)

    mix = mix_ref[...]
    twice = jnp.concatenate([mix, mix], axis=1)
    terms = []
    for d in range(sources):
        for j in range(own):
            at = first + j * rank
            part = got_ref[d, at : at + rank, :].astype(F32) * twice
            terms.append(jnp.sum(part, axis=0, keepdims=True))
    weight = jnp.maximum(mm(fold(jnp.concatenate(terms, axis=0)), inverse_ref[...]), 0.0)
    weight_ref[...] = weight
    for j in range(own):
        own_ref[j : j + 1, :] = weight_ref[pl.ds(source(place_ref[0]) * own + j, 1), :]
    wgram_ref[...] = halves(mm(weight, weight, TN))
    acc_ref[...] = jnp.zeros(acc_ref.shape, F32)
    lane = lax.broadcasted_iota(jnp.int32, (rank, rows), 1)
    for t in range(slots):
        k, b, g, kept = live_rows(t, list_ref, count_ref, visits_ref, rows)
        d, j = source(lax.div(k, own)), lax.rem(k, own)
        both = jnp.concatenate(split(mix * weight_ref[pl.ds(d * own + j, 1), :]), axis=0)
        at = pl.multiple_of((j * VBLOCKS + b) * rank, rank)
        polar = got_ref[d, pl.ds(at, rank), :]
        spread = mm16(both, jnp.concatenate([polar, polar], axis=0), TN)
        spread = jnp.where(lane < kept, spread, 0.0).astype(BF16)
        acc_ref[g] += mm16(spread, tile_ref[t])
    parity = place_ref[1]
    for j in range(keep_ref.shape[0]):
        keep_ref[j] = acc_ref[2 * j + parity]
        send_ref[j] = acc_ref[2 * j + 1 - parity]


def pair_kernel(keep_ref, came_ref, gram_a, gram_b, out_ref):
    low, lanes = gram_a.shape
    slabs = keep_ref.shape[2] // lanes
    piece = jnp.concatenate(split(gram_a[...] + gram_b[...]), axis=0)
    for j in range(keep_ref.shape[0]):
        both = (keep_ref[j] + came_ref[j]).astype(BF16)
        for i in range(slabs):
            out_ref[j, i] = both[:, i * lanes : (i + 1) * lanes]
        out_ref[j, slabs] = piece


def factor_kernel(got_ref, mgram_ref, out_ref):
    sources, slabs = got_ref.shape[0], got_ref.shape[1] - 1
    sums = []
    for i in range(slabs + 1):
        total = got_ref[0, i].astype(F32)
        for d in range(1, sources):
            total += got_ref[d, i].astype(F32)
        sums.append(total)
    low = sums[slabs].shape[0] // 2
    gram = whole(sums[slabs][:low] + sums[slabs][low:])
    inverse = damped_inverse(mgram_ref[...] * gram)
    code = jnp.maximum(mm(inverse, jnp.concatenate(sums[:slabs], axis=1)), 0.0).astype(BF16)
    for d in range(sources):
        out_ref[d] = code


def place_kernel(flip, place_ref, from_ref, *refs):
    out_hbm, wide_ref, sems = refs[-3:]
    parity = place_ref[1] if not flip else 1 - place_ref[1]
    cols = from_ref.shape[2]
    copies = []
    for j in range(from_ref.shape[0]):
        wide_ref[j] = from_ref[j].astype(F32)
        at = pl.multiple_of((2 * j + parity) * cols, cols)
        copies.append(
            pltpu.make_async_copy(wide_ref.at[j], out_hbm.at[:, pl.ds(at, cols)], sems.at[j])
        )
        copies[-1].start()
    for copy in copies:
        copy.wait()


def call(kernel, outs, specs, args, scratch=(), flops=1e9, spec=VM, alias=None, vmem=16):
    many = isinstance(outs, tuple)
    return pl.pallas_call(
        kernel,
        out_shape=outs,
        in_specs=specs,
        out_specs=(spec,) * len(outs) if many else spec,
        input_output_aliases=alias or {},
        scratch_shapes=scratch,
        compiler_params=pltpu.CompilerParams(vmem_limit_bytes=vmem * MIB),
        cost_estimate=pl.CostEstimate(flops=int(flops), bytes_accessed=65536, transcendentals=0),
    )(*args)


def swap(x, axis, bit):
    size = lax.axis_size(axis)
    return lax.ppermute(x, axis, [(i, i ^ bit) for i in range(size)])


def swap_z(x, high, low):
    n_pat, n_code = lax.axis_size("pat"), lax.axis_size("code")
    pairs = [
        (p * n_code + c, (p ^ (high * n_pat // 2)) * n_code + (c ^ (low * n_code // 2)))
        for p in range(n_pat)
        for c in range(n_code)
    ]
    return lax.ppermute(x, ("pat", "code"), pairs)


def plus(x, parts):
    for part in parts:
        x = x + part
    return x


def body(tile_data, tile_list, tile_count, visit_counts, code_factor_t, visit_mix, patient_weight):
    tiles = tile_data[0, 0]
    tile_list = jnp.transpose(tile_list, (0, 2, 1, 3))
    slots, rows, cols = tiles.shape
    rank = visit_mix.shape[0]
    patients = visit_counts.shape[0]
    n_code, n_pat = lax.axis_size("code"), lax.axis_size("pat")
    half = n_pat // 2
    own = patients // n_code
    code_at, pat_at = lax.axis_index("code"), lax.axis_index("pat")
    place = jnp.stack([code_at, lax.rem(pat_at, 2)]).astype(jnp.int32)
    shape = jax.ShapeDtypeStruct
    square = shape((rank, rank), F32)

    partial = call(
        products_kernel, shape((patients * VBLOCKS, rank, rows), F32), [HBM] * 5,
        (tile_list, tile_count, visit_counts, tile_data, code_factor_t),
        [
            pltpu.SMEM(tile_list.shape, jnp.int32), pltpu.SMEM(tile_count.shape, jnp.int32),
            pltpu.SMEM(visit_counts.shape, jnp.int32), pltpu.VMEM(tiles.shape, BF16),
            pltpu.VMEM(code_factor_t.shape, F32), pltpu.SemaphoreType.DMA((3,)),
            pltpu.SemaphoreType.DMA((5,)),
        ],
        vmem=50,
    )
    sent = partial.astype(F16).reshape(n_code, own * VBLOCKS * rank, rows)
    got = lax.all_to_all(sent, "code", 0, 0, tiled=True)
    gram = call(gram_kernel, shape((rank // 2, 2 * rank), F32), [VM], (code_factor_t,))
    products = jnp.sum(got.astype(F32), axis=0).reshape(own * VBLOCKS, rank, rows)

    scales = (1.0 / n_code, 1.0 / n_pat)
    length = (own * VBLOCKS + own) * rank
    sums, message = call(
        functools.partial(polar_kernel, scales),
        (shape((3 * rank // 2, 2 * rank), F32), shape((length, rows), BF16)),
        [SM, VM, VM, VM, VM], (place, products, visit_mix, patient_weight, gram), flops=5e9,
    )
    quarter = n_code // 2
    other = swap(message, "code", quarter)
    parts = [swap(sums, "code", bit) for bit in (1, 2, 3)]
    message = jnp.broadcast_to(jnp.concatenate([message, other])[None], (quarter, 2 * length, rows))
    message, *parts = lax.optimization_barrier((message, *parts))
    sums = plus(sums, parts)
    layers = [[z * quarter + i for i in range(quarter)] for z in (0, 1)]
    shared = lax.all_to_all(message, "code", 0, 0, axis_index_groups=layers, tiled=True)
    shared = shared.reshape(n_code, length, rows)
    sums = plus(sums, [swap(sums, "pat", bit) for bit in (2, 4, 6)])
    sums = sums + swap(sums, "pat", 1)
    mix_new, mix_again, mix_gram, inverse = call(
        mix_kernel, (square,) * 4, [VM] * 4,
        (sums, *(swap_z(sums, high, low) for high, low in ((0, 1), (1, 0), (1, 1)))), flops=5e9,
    )
    block = shape((half, rank, cols), F32)
    keep, send, wgram, weight_new = call(
        numer_kernel,
        (block, block, shape((rank // 2, 2 * rank), F32), shape((own, rank), F32)),
        [SM, SM, SM, SM, VM, VM, VM, VM],
        (place, tile_list, tile_count, visit_counts, shared, mix_again, inverse, tiles),
        [pltpu.VMEM((n_pat, rank, cols), F32), pltpu.VMEM((patients, rank), F32)], flops=5e9,
    )
    groups = [[core + 2 * i for i in range(half)] for core in (0, 1)]

    def exchange(x):
        return lax.all_to_all(x, "pat", 0, 0, axis_index_groups=groups, tiled=True)

    lanes = 2 * rank
    packed = call(
        pair_kernel, shape((half, cols // lanes + 1, rank, lanes), BF16), [VM] * 4,
        (keep, swap(send, "pat", 1), wgram, swap(wgram, "pat", 1)),
    )
    code = call(
        factor_kernel, shape((half, rank, cols), BF16), [VM, VM], (exchange(packed), mix_gram)
    )
    mine = exchange(code)
    place_scratch = [pltpu.VMEM(mine.shape, F32), pltpu.SemaphoreType.DMA((half,))]
    result = shape((rank, n_pat * cols), F32)
    came = swap(mine, "pat", 1)
    code_new = call(
        functools.partial(place_kernel, False), result, [SM, VM], (place, mine), place_scratch,
        spec=HBM,
    )
    code_new = call(
        functools.partial(place_kernel, True), result, [SM, VM, HBM], (place, came, code_new),
        place_scratch, spec=HBM, alias={2: 0},
    )
    return (code_new, mix_new, weight_new)


def solution(mesh):
    placed = (
        P("pat", "code", None, None, None),
        P("pat", "code", None, None),
        P("pat", "code"),
        P("pat"),
        P(None, "code"),
        P(),
        P("pat", None),
    )
    return jax.shard_map(
        body,
        mesh=mesh,
        in_specs=placed,
        out_specs=(P(None, "code"), P(), P(("pat", "code"), None)),
        check_vma=False,
    )
```

```python
import functools

import jax
import jax.numpy as jnp
from jax import lax
from jax.experimental import pallas as pl
from jax.experimental.pallas import tpu as pltpu
from jax.sharding import PartitionSpec as P

VBLOCKS = 2
NS_STEPS = 8
damping = 0.1
epsilon = 1e-06
F32, BF16, F16 = jnp.float32, jnp.bfloat16, jnp.float16
VM = pl.BlockSpec(memory_space=pltpu.VMEM)
HBM = pl.BlockSpec(memory_space=pl.ANY)
SM = pl.BlockSpec(memory_space=pltpu.SMEM)
MIB = 1024 * 1024


def mm(a, b, dims=((1,), (0,))):
    return lax.dot_general(
        a, b, (dims, ((), ())), precision=lax.Precision.HIGHEST, preferred_element_type=F32
    )


def mm16(a, b, dims=((1,), (0,))):
    return lax.dot_general(a, b, (dims, ((), ())), preferred_element_type=F32)


NT = ((1,), (1,))
TN = ((0,), (0,))


def split(x):
    high = x.astype(BF16)
    return high, (x - high.astype(F32)).astype(BF16)


def mm3(a, b, dims=((1,), (0,))):
    return mm16(a[0], b[0], dims) + (mm16(a[0], b[1], dims) + mm16(a[1], b[0], dims))


def fold(x):
    half = x.shape[1] // 2
    return x[:, :half] + x[:, half:]


def times2(x, y):
    return [[x[i][0] * y[0][j] + x[i][1] * y[1][j] for j in (0, 1)] for i in (0, 1)]


def inverse4(p):
    a = [[p[1][1], -p[0][1]], [-p[0][1], p[0][0]]]
    det = p[0][0] * p[1][1] - p[0][1] * p[0][1]
    b = [[p[0][2], p[0][3]], [p[1][2], p[1][3]]]
    t = times2(a, b)
    s00 = det * p[2][2] - (b[0][0] * t[0][0] + b[1][0] * t[1][0])
    s01 = det * p[2][3] - (b[0][0] * t[0][1] + b[1][0] * t[1][1])
    s11 = det * p[3][3] - (b[0][1] * t[0][1] + b[1][1] * t[1][1])
    over = 1.0 / (s00 * s11 - s01 * s01)
    over_det = 1.0 / det
    flip = [[s11, -s01], [-s01, s00]]
    u = times2(t, flip)
    v = times2(u, [[t[0][0], t[1][0]], [t[0][1], t[1][1]]])
    side = [[u[i][j] * over for j in (0, 1)] for i in (0, 1)]
    last = [[flip[i][j] * (det * over) for j in (0, 1)] for i in (0, 1)]
    first = [
        [a[i][j] * over_det + v[i][j] * (over * over_det) for j in (0, 1)] for i in (0, 1)
    ]
    return [
        [first[0][0], first[0][1], -side[0][0], -side[0][1]],
        [first[0][1], first[1][1], -side[1][0], -side[1][1]],
        [-side[0][0], -side[1][0], last[0][0], last[0][1]],
        [-side[0][1], -side[1][1], last[0][1], last[1][1]],
    ]


def halves(x):
    low = x.shape[0] // 2
    return jnp.concatenate([x[:low], x[low:]], axis=1)


def damped_inverse(gram):
    size = gram.shape[0]
    eye = lax.broadcasted_iota(jnp.int32, (size, size), 0) == lax.broadcasted_iota(
        jnp.int32, (size, size), 1
    )
    scale = size / jnp.sum(jnp.where(eye, gram, 0.0), keepdims=True)
    work = jnp.concatenate(
        [gram * scale + jnp.where(eye, damping, 0.0), eye.astype(F32)], axis=1
    )
    lanes = 2 * size
    blocks = [work[i : i + 8] for i in range(0, size, 8)]
    raw, fresh = [], []
    for j in range(0, size, 4):
        owner, at = j // 8, j % 8
        rows = [blocks[owner][at + i : at + i + 1] for i in range(4)]
        pivot = [
            [jnp.broadcast_to(row[:, j + k : j + k + 1], (1, lanes)) for k in range(4)]
            for row in rows
        ]
        inverse = inverse4(pivot)
        new = [
            (inverse[i][0] * rows[0] + inverse[i][1] * rows[1])
            + (inverse[i][2] * rows[2] + inverse[i][3] * rows[3])
            for i in range(4)
        ]
        raw += rows
        fresh += new
        for m in range(owner if at == 0 else owner + 1, len(blocks)):
            block = blocks[m]
            part = [block[:, j + k : j + k + 1] * new[k] for k in range(4)]
            blocks[m] = block - ((part[0] + part[1]) + (part[2] + part[3]))
    raw = jnp.concatenate(raw, axis=0)[:, size:]
    fresh = jnp.concatenate(fresh, axis=0)[:, size:]
    return scale * mm(raw, fresh, TN)


def live_rows(t, meta_ref, tile_rows):
    width = meta_ref.shape[3]
    k, b, g = meta_ref[0, 0, 0, t], meta_ref[0, 1, 0, t], meta_ref[0, 2, 0, t]
    visits = meta_ref[0, 4 + lax.div(k, width), 0, lax.rem(k, width)]
    kept = jnp.where(t < meta_ref[0, 3, 0, 0], visits - tile_rows * b, 0)
    return k, b, g, kept


def products_kernel(
    meta_ref, tile_hbm, code_hbm, out_ref, tile_ref, code_ref, sems
):
    slots, rows, cols = tile_ref.shape
    rank = code_ref.shape[0]
    parts = sems.shape[0] - 1
    each = slots // parts
    code_copy = pltpu.make_async_copy(code_hbm, code_ref, sems.at[parts])
    code_copy.start()
    copies = []
    for i in range(parts):
        at = pl.ds(i * each, each)
        copies.append(pltpu.make_async_copy(tile_hbm.at[0, 0, at], tile_ref.at[at], sems.at[i]))
        copies[-1].start()
    out_ref[...] = jnp.zeros(out_ref.shape, F32)
    lane = lax.broadcasted_iota(jnp.int32, (rank, rows), 1)
    code_copy.wait()
    for t in range(slots):
        if t % each == 0:
            copies[t // each].wait()
        k, b, g, kept = live_rows(t, meta_ref, rows)
        codes = code_ref[:, pl.ds(pl.multiple_of(g * cols, cols), cols)].astype(BF16)
        part = mm16(codes, tile_ref[t], NT)
        out_ref[k * VBLOCKS + b] += jnp.where(lane < kept, part, 0.0)


def gram_kernel(code_ref, out_ref):
    high, low = split(code_ref[...])
    cross = mm16(high, low, NT)
    out_ref[...] = halves(mm16(high, high, NT) + cross + cross.T)


def polar_kernel(
    scales, at_ref, prod_ref, mix_ref, weight_ref, gram_ref, sums_ref, out_ref
):
    segs, rank, rows = prod_ref.shape
    own = segs // VBLOCKS
    eye = lax.broadcasted_iota(jnp.int32, (rank, rank), 0) == lax.broadcasted_iota(
        jnp.int32, (rank, rank), 1
    )
    prods, zs, weights = [], [], []
    for j in range(own):
        prods.append(
            split(jnp.concatenate([prod_ref[VBLOCKS * j + b] for b in range(VBLOCKS)], axis=1))
        )
        weights.append(weight_ref[pl.ds(at_ref[0] * own + j, 1), :])
        target = mm3(split(mix_ref[...] * weights[j]), prods[j])
        zs.append(target / jnp.sqrt(jnp.sum(target * target, keepdims=True) + epsilon))
    zs = [split(z) for z in zs]
    for _ in range(NS_STEPS):
        factors = [split(jnp.where(eye, 1.5, 0.0) - 0.5 * mm3(z, z, NT)) for z in zs]
        zs = [split(mm3(q, z)) for q, z in zip(factors, zs)]
    pieces = [z[0][:, b * rows : (b + 1) * rows] for z in zs for b in range(VBLOCKS)]
    numer = jnp.zeros((rank, rank), F32)
    for z, p, weight in zip(zs, prods, weights):
        projected = mm3(z, p, NT)
        numer += projected * weight
        pieces.append(jnp.concatenate(split(projected), axis=1))
    low = rank // 2
    weight = weight_ref[...]
    sums_ref[:low, :] = halves(numer)
    sums_ref[low:rank, :] = halves(mm(weight, weight, TN)) * scales[0]
    sums_ref[rank:, :] = gram_ref[...] * scales[1]
    for i, piece in enumerate(pieces):
        out_ref[i * rank : (i + 1) * rank, :] = piece


def whole(x):
    rank = x.shape[1] // 2
    return jnp.concatenate([x[:, :rank], x[:, rank:]], axis=0)


def mix_kernel(a_ref, b_ref, c_ref, d_ref, mix_ref, again_ref, mgram_ref, inverse_ref):
    sums = (a_ref[...] + b_ref[...]) + (c_ref[...] + d_ref[...])
    rank = mix_ref.shape[0]
    low = rank // 2
    weight_gram, code_gram = whole(sums[low:rank]), whole(sums[rank:])
    mix = mm(whole(sums[:low]), damped_inverse(code_gram * weight_gram))
    again_ref[...] = mix
    mix_ref[...] = mix
    mix_gram = mm(mix, mix, TN)
    mgram_ref[...] = mix_gram
    inverse_ref[...] = damped_inverse(mix_gram * code_gram)


def numer_kernel(
    place_ref, meta_ref, got_ref, mix_ref, inverse_ref, tile_ref,
    keep_ref, send_ref, wgram_ref, own_ref, acc_ref, weight_ref,
):
    slots, rows, cols = tile_ref.shape
    sources = got_ref.shape[0]
    rank = mix_ref.shape[0]
    own = own_ref.shape[0]
    first = own * VBLOCKS * rank
    layers = 2
    z_at = lax.div(place_ref[0], sources // layers)

    def source(d):
        x_at, layer = lax.rem(d, sources // layers), lax.div(d, sources // layers)
        return x_at * layers + jnp.where(layer == z_at, 0, 1)

    mix = mix_ref[...]
    twice = jnp.concatenate([mix, mix], axis=1)
    terms = []
    for d in range(sources):
        for j in range(own):
            at = first + j * rank
            part = got_ref[d, at : at + rank, :].astype(F32) * twice
            terms.append(jnp.sum(part, axis=0, keepdims=True))
    weight = jnp.maximum(mm(fold(jnp.concatenate(terms, axis=0)), inverse_ref[...]), 0.0)
    weight_ref[...] = weight
    for j in range(own):
        own_ref[j : j + 1, :] = weight_ref[pl.ds(source(place_ref[0]) * own + j, 1), :]
    wgram_ref[...] = halves(mm(weight, weight, TN))
    acc_ref[...] = jnp.zeros(acc_ref.shape, F32)
    lane = lax.broadcasted_iota(jnp.int32, (rank, rows), 1)
    for t in range(slots):
        k, b, g, kept = live_rows(t, meta_ref, rows)
        d, j = source(lax.div(k, own)), lax.rem(k, own)
        both = jnp.concatenate(split(mix * weight_ref[pl.ds(d * own + j, 1), :]), axis=0)
        at = pl.multiple_of((j * VBLOCKS + b) * rank, rank)
        polar = got_ref[d, pl.ds(at, rank), :]
        spread = mm16(both, jnp.concatenate([polar, polar], axis=0), TN)
        spread = jnp.where(lane < kept, spread, 0.0).astype(BF16)
        acc_ref[g] += mm16(spread, tile_ref[t])
    parity = place_ref[1]
    for j in range(keep_ref.shape[0]):
        keep_ref[j] = acc_ref[2 * j + parity]
        send_ref[j] = acc_ref[2 * j + 1 - parity].astype(BF16)


def pair_kernel(keep_ref, came_ref, gram_a, gram_b, out_ref):
    low, lanes = gram_a.shape
    slabs = keep_ref.shape[2] // lanes
    piece = jnp.concatenate(split(gram_a[...] + gram_b[...]), axis=0)
    for j in range(keep_ref.shape[0]):
        both = (keep_ref[j] + came_ref[j]).astype(BF16)
        for i in range(slabs):
            out_ref[j, i] = both[:, i * lanes : (i + 1) * lanes]
        out_ref[j, slabs] = piece


def factor_kernel(got_ref, mgram_ref, out_ref):
    sources, slabs = got_ref.shape[0], got_ref.shape[1] - 1
    sums = []
    for i in range(slabs + 1):
        total = got_ref[0, i].astype(F32)
        for d in range(1, sources):
            total += got_ref[d, i].astype(F32)
        sums.append(total)
    low = sums[slabs].shape[0] // 2
    gram = whole(sums[slabs][:low] + sums[slabs][low:])
    inverse = damped_inverse(mgram_ref[...] * gram)
    code = jnp.maximum(mm(inverse, jnp.concatenate(sums[:slabs], axis=1)), 0.0).astype(BF16)
    for d in range(sources):
        out_ref[d] = code


def place_kernel(flip, place_ref, from_ref, *refs):
    out_hbm, wide_ref, sems = refs[-3:]
    parity = place_ref[1] if not flip else 1 - place_ref[1]
    cols = from_ref.shape[2]
    copies = []
    for j in range(from_ref.shape[0]):
        wide_ref[j] = from_ref[j].astype(F32)
        at = pl.multiple_of((2 * j + parity) * cols, cols)
        copies.append(
            pltpu.make_async_copy(wide_ref.at[j], out_hbm.at[:, pl.ds(at, cols)], sems.at[j])
        )
        copies[-1].start()
    for copy in copies:
        copy.wait()


def call(kernel, outs, specs, args, scratch=(), flops=1e9, spec=VM, alias=None, vmem=16):
    many = isinstance(outs, tuple)
    return pl.pallas_call(
        kernel,
        out_shape=outs,
        in_specs=specs,
        out_specs=(spec,) * len(outs) if many else spec,
        input_output_aliases=alias or {},
        scratch_shapes=scratch,
        compiler_params=pltpu.CompilerParams(vmem_limit_bytes=vmem * MIB),
        cost_estimate=pl.CostEstimate(flops=int(flops), bytes_accessed=65536, transcendentals=0),
    )(*args)


def swap(x, axis, bit):
    size = lax.axis_size(axis)
    return lax.ppermute(x, axis, [(i, i ^ bit) for i in range(size)])


def swap_z(x, high, low):
    n_pat, n_code = lax.axis_size("pat"), lax.axis_size("code")
    pairs = [
        (p * n_code + c, (p ^ (high * n_pat // 2)) * n_code + (c ^ (low * n_code // 2)))
        for p in range(n_pat)
        for c in range(n_code)
    ]
    return lax.ppermute(x, ("pat", "code"), pairs)


def plus(x, parts):
    for part in parts:
        x = x + part
    return x


def body(tile_data, tile_list, tile_count, visit_counts, code_factor_t, visit_mix, patient_weight):
    tiles = tile_data[0, 0]
    slots, rows, cols = tiles.shape
    meta = jnp.concatenate(
        [
            jnp.transpose(tile_list, (0, 2, 1, 3)),
            jnp.broadcast_to(tile_count.reshape(1, 1, 1, 1), (1, 1, 1, slots)),
            visit_counts.reshape(1, -1, 1, slots),
        ],
        axis=1,
    )
    rank = visit_mix.shape[0]
    patients = visit_counts.shape[0]
    n_code, n_pat = lax.axis_size("code"), lax.axis_size("pat")
    half = n_pat // 2
    own = patients // n_code
    code_at, pat_at = lax.axis_index("code"), lax.axis_index("pat")
    place = jnp.stack([code_at, lax.rem(pat_at, 2)]).astype(jnp.int32)
    shape = jax.ShapeDtypeStruct
    square = shape((rank, rank), F32)

    partial = call(
        products_kernel, shape((patients * VBLOCKS, rank, rows), F32), [SM, HBM, HBM],
        (meta, tile_data, code_factor_t),
        [
            pltpu.VMEM(tiles.shape, BF16), pltpu.VMEM(code_factor_t.shape, F32),
            pltpu.SemaphoreType.DMA((5,)),
        ],
        vmem=50,
    )
    sent = partial.astype(F16).reshape(n_code, own * VBLOCKS * rank, rows)
    got = lax.all_to_all(sent, "code", 0, 0, tiled=True)
    gram = call(gram_kernel, shape((rank // 2, 2 * rank), F32), [VM], (code_factor_t,))
    products = jnp.sum(got.astype(F32), axis=0).reshape(own * VBLOCKS, rank, rows)

    scales = (1.0 / n_code, 1.0 / n_pat)
    length = (own * VBLOCKS + own) * rank
    sums, message = call(
        functools.partial(polar_kernel, scales),
        (shape((3 * rank // 2, 2 * rank), F32), shape((length, rows), BF16)),
        [SM, VM, VM, VM, VM], (place, products, visit_mix, patient_weight, gram), flops=5e9,
    )
    quarter = n_code // 2
    other = swap(message, "code", quarter)
    parts = [swap(sums, "code", bit) for bit in (1, 2, 3)]
    message = jnp.broadcast_to(jnp.concatenate([message, other])[None], (quarter, 2 * length, rows))
    message, *parts = lax.optimization_barrier((message, *parts))
    sums = plus(sums, parts)
    layers = [[z * quarter + i for i in range(quarter)] for z in (0, 1)]
    shared = lax.all_to_all(message, "code", 0, 0, axis_index_groups=layers, tiled=True)
    shared = shared.reshape(n_code, length, rows)
    sums = plus(sums, [swap(sums, "pat", bit) for bit in (2, 4, 6)])
    sums = sums + swap(sums, "pat", 1)
    mix_new, mix_again, mix_gram, inverse = call(
        mix_kernel, (square,) * 4, [VM] * 4,
        (sums, *(swap_z(sums, high, low) for high, low in ((0, 1), (1, 0), (1, 1)))), flops=5e9,
    )
    block = shape((half, rank, cols), F32)
    keep, send, wgram, weight_new = call(
        numer_kernel,
        (
            block, shape(block.shape, BF16), shape((rank // 2, 2 * rank), F32),
            shape((own, rank), F32),
        ),
        [SM, SM, VM, VM, VM, VM],
        (place, meta, shared, mix_again, inverse, tiles),
        [pltpu.VMEM((n_pat, rank, cols), F32), pltpu.VMEM((patients, rank), F32)], flops=5e9,
    )
    groups = [[core + 2 * i for i in range(half)] for core in (0, 1)]

    def exchange(x):
        return lax.all_to_all(x, "pat", 0, 0, axis_index_groups=groups, tiled=True)

    lanes = 2 * rank
    packed = call(
        pair_kernel, shape((half, cols // lanes + 1, rank, lanes), BF16), [VM] * 4,
        (keep, swap(send, "pat", 1), wgram, swap(wgram, "pat", 1)),
    )
    code = call(
        factor_kernel, shape((half, rank, cols), BF16), [VM, VM], (exchange(packed), mix_gram)
    )
    mine = exchange(code)
    place_scratch = [pltpu.VMEM(mine.shape, F32), pltpu.SemaphoreType.DMA((half,))]
    result = shape((rank, n_pat * cols), F32)
    came = swap(mine, "pat", 1)
    code_new = call(
        functools.partial(place_kernel, False), result, [SM, VM], (place, mine), place_scratch,
        spec=HBM,
    )
    code_new = call(
        functools.partial(place_kernel, True), result, [SM, VM, HBM], (place, came, code_new),
        place_scratch, spec=HBM, alias={2: 0},
    )
    return (code_new, mix_new, weight_new)


def solution(mesh):
    placed = (
        P("pat", "code", None, None, None),
        P("pat", "code", None, None),
        P("pat", "code"),
        P("pat"),
        P(None, "code"),
        P(),
        P("pat", None),
    )
    return jax.shard_map(
        body,
        mesh=mesh,
        in_specs=placed,
        out_specs=(P(None, "code"), P(), P(("pat", "code"), None)),
        check_vma=False,
    )
```

```python
import functools

import jax
import jax.numpy as jnp
from jax import lax
from jax.experimental import pallas as pl
from jax.experimental.pallas import tpu as pltpu
from jax.sharding import PartitionSpec as P

VBLOCKS = 2
NS_STEPS = 8
damping = 0.1
epsilon = 1e-06
F32, BF16, F16 = jnp.float32, jnp.bfloat16, jnp.float16
VM = pl.BlockSpec(memory_space=pltpu.VMEM)
HBM = pl.BlockSpec(memory_space=pl.ANY)
SM = pl.BlockSpec(memory_space=pltpu.SMEM)
MIB = 1024 * 1024


def mm(a, b, dims=((1,), (0,))):
    return lax.dot_general(
        a, b, (dims, ((), ())), precision=lax.Precision.HIGHEST, preferred_element_type=F32
    )


def mm16(a, b, dims=((1,), (0,))):
    return lax.dot_general(a, b, (dims, ((), ())), preferred_element_type=F32)


NT = ((1,), (1,))
TN = ((0,), (0,))


def split(x):
    high = x.astype(BF16)
    return high, (x - high.astype(F32)).astype(BF16)


def mm3(a, b, dims=((1,), (0,))):
    return mm16(a[0], b[0], dims) + (mm16(a[0], b[1], dims) + mm16(a[1], b[0], dims))


def fold(x):
    half = x.shape[1] // 2
    return x[:, :half] + x[:, half:]


def times2(x, y):
    return [[x[i][0] * y[0][j] + x[i][1] * y[1][j] for j in (0, 1)] for i in (0, 1)]


def inverse4(p):
    a = [[p[1][1], -p[0][1]], [-p[0][1], p[0][0]]]
    det = p[0][0] * p[1][1] - p[0][1] * p[0][1]
    b = [[p[0][2], p[0][3]], [p[1][2], p[1][3]]]
    t = times2(a, b)
    s00 = det * p[2][2] - (b[0][0] * t[0][0] + b[1][0] * t[1][0])
    s01 = det * p[2][3] - (b[0][0] * t[0][1] + b[1][0] * t[1][1])
    s11 = det * p[3][3] - (b[0][1] * t[0][1] + b[1][1] * t[1][1])
    over = 1.0 / (s00 * s11 - s01 * s01)
    over_det = 1.0 / det
    flip = [[s11, -s01], [-s01, s00]]
    u = times2(t, flip)
    v = times2(u, [[t[0][0], t[1][0]], [t[0][1], t[1][1]]])
    side = [[u[i][j] * over for j in (0, 1)] for i in (0, 1)]
    last = [[flip[i][j] * (det * over) for j in (0, 1)] for i in (0, 1)]
    first = [
        [a[i][j] * over_det + v[i][j] * (over * over_det) for j in (0, 1)] for i in (0, 1)
    ]
    return [
        [first[0][0], first[0][1], -side[0][0], -side[0][1]],
        [first[0][1], first[1][1], -side[1][0], -side[1][1]],
        [-side[0][0], -side[1][0], last[0][0], last[0][1]],
        [-side[0][1], -side[1][1], last[0][1], last[1][1]],
    ]


def halves(x):
    low = x.shape[0] // 2
    return jnp.concatenate([x[:low], x[low:]], axis=1)


def damped_inverse(gram):
    size = gram.shape[0]
    eye = lax.broadcasted_iota(jnp.int32, (size, size), 0) == lax.broadcasted_iota(
        jnp.int32, (size, size), 1
    )
    scale = size / jnp.sum(jnp.where(eye, gram, 0.0), keepdims=True)
    work = jnp.concatenate(
        [gram * scale + jnp.where(eye, damping, 0.0), eye.astype(F32)], axis=1
    )
    lanes = 2 * size
    blocks = [work[i : i + 8] for i in range(0, size, 8)]
    raw, fresh = [], []
    for j in range(0, size, 4):
        owner, at = j // 8, j % 8
        rows = [blocks[owner][at + i : at + i + 1] for i in range(4)]
        pivot = [
            [jnp.broadcast_to(row[:, j + k : j + k + 1], (1, lanes)) for k in range(4)]
            for row in rows
        ]
        inverse = inverse4(pivot)
        new = [
            (inverse[i][0] * rows[0] + inverse[i][1] * rows[1])
            + (inverse[i][2] * rows[2] + inverse[i][3] * rows[3])
            for i in range(4)
        ]
        raw += rows
        fresh += new
        for m in range(owner if at == 0 else owner + 1, len(blocks)):
            block = blocks[m]
            part = [block[:, j + k : j + k + 1] * new[k] for k in range(4)]
            blocks[m] = block - ((part[0] + part[1]) + (part[2] + part[3]))
    raw = jnp.concatenate(raw, axis=0)[:, size:]
    fresh = jnp.concatenate(fresh, axis=0)[:, size:]
    return scale * mm(raw, fresh, TN)


def live_rows(t, list_ref, count_ref, visits_ref, tile_rows):
    k, b, g = list_ref[0, 0, 0, t], list_ref[0, 1, 0, t], list_ref[0, 2, 0, t]
    kept = jnp.where(t < count_ref[0, 0], visits_ref[k] - tile_rows * b, 0)
    return k, b, g, kept


def products_kernel(
    list_hbm, count_hbm, visits_hbm, tile_hbm, code_hbm, out_ref,
    list_ref, count_ref, visits_ref, tile_ref, code_ref, small_sems, sems,
):
    slots, rows, cols = tile_ref.shape
    rank = code_ref.shape[0]
    parts = sems.shape[0] - 1
    each = slots // parts
    small = []
    for i, (src, dst) in enumerate(
        ((list_hbm, list_ref), (count_hbm, count_ref), (visits_hbm, visits_ref))
    ):
        small.append(pltpu.make_async_copy(src, dst, small_sems.at[i]))
        small[-1].start()
    code_copy = pltpu.make_async_copy(code_hbm, code_ref, sems.at[parts])
    code_copy.start()
    copies = []
    for i in range(parts):
        at = pl.ds(i * each, each)
        copies.append(pltpu.make_async_copy(tile_hbm.at[0, 0, at], tile_ref.at[at], sems.at[i]))
        copies[-1].start()
    out_ref[...] = jnp.zeros(out_ref.shape, F32)
    lane = lax.broadcasted_iota(jnp.int32, (rank, rows), 1)
    for copy in small:
        copy.wait()
    code_copy.wait()
    for t in range(slots):
        if t % each == 0:
            copies[t // each].wait()
        k, b, g, kept = live_rows(t, list_ref, count_ref, visits_ref, rows)
        codes = code_ref[:, pl.ds(pl.multiple_of(g * cols, cols), cols)].astype(BF16)
        part = mm16(codes, tile_ref[t], NT)
        out_ref[k * VBLOCKS + b] += jnp.where(lane < kept, part, 0.0)


def gram_kernel(code_ref, out_ref):
    high, low = split(code_ref[...])
    cross = mm16(high, low, NT)
    out_ref[...] = halves(mm16(high, high, NT) + cross + cross.T)


def polar_kernel(
    scales, at_ref, prod_ref, mix_ref, weight_ref, gram_ref, sums_ref, out_ref
):
    segs, rank, rows = prod_ref.shape
    own = segs // VBLOCKS
    eye = lax.broadcasted_iota(jnp.int32, (rank, rank), 0) == lax.broadcasted_iota(
        jnp.int32, (rank, rank), 1
    )
    prods, zs, weights = [], [], []
    for j in range(own):
        prods.append(
            split(jnp.concatenate([prod_ref[VBLOCKS * j + b] for b in range(VBLOCKS)], axis=1))
        )
        weights.append(weight_ref[pl.ds(at_ref[0] * own + j, 1), :])
        target = mm3(split(mix_ref[...] * weights[j]), prods[j])
        zs.append(target / jnp.sqrt(jnp.sum(target * target, keepdims=True) + epsilon))
    zs = [split(z) for z in zs]
    for _ in range(NS_STEPS):
        factors = [split(jnp.where(eye, 1.5, 0.0) - 0.5 * mm3(z, z, NT)) for z in zs]
        zs = [split(mm3(q, z)) for q, z in zip(factors, zs)]
    pieces = [z[0][:, b * rows : (b + 1) * rows] for z in zs for b in range(VBLOCKS)]
    numer = jnp.zeros((rank, rank), F32)
    for z, p, weight in zip(zs, prods, weights):
        projected = mm3(z, p, NT)
        numer += projected * weight
        pieces.append(jnp.concatenate(split(projected), axis=1))
    low = rank // 2
    weight = weight_ref[...]
    sums_ref[:low, :] = halves(numer)
    sums_ref[low:rank, :] = halves(mm(weight, weight, TN)) * scales[0]
    sums_ref[rank:, :] = gram_ref[...] * scales[1]
    for i, piece in enumerate(pieces):
        out_ref[i * rank : (i + 1) * rank, :] = piece


def whole(x):
    rank = x.shape[1] // 2
    return jnp.concatenate([x[:, :rank], x[:, rank:]], axis=0)


def mix_kernel(a_ref, b_ref, c_ref, d_ref, mix_ref, again_ref, mgram_ref, inverse_ref):
    sums = (a_ref[...] + b_ref[...]) + (c_ref[...] + d_ref[...])
    rank = mix_ref.shape[0]
    low = rank // 2
    weight_gram, code_gram = whole(sums[low:rank]), whole(sums[rank:])
    mix = mm(whole(sums[:low]), damped_inverse(code_gram * weight_gram))
    again_ref[...] = mix
    mix_ref[...] = mix
    mix_gram = mm(mix, mix, TN)
    mgram_ref[...] = mix_gram
    inverse_ref[...] = damped_inverse(mix_gram * code_gram)


def numer_kernel(
    place_ref, list_ref, count_ref, visits_ref, got_ref, mix_ref, inverse_ref, tile_ref,
    keep_ref, send_ref, wgram_ref, own_ref, acc_ref, weight_ref,
):
    slots, rows, cols = tile_ref.shape
    sources = got_ref.shape[0]
    rank = mix_ref.shape[0]
    own = own_ref.shape[0]
    first = own * VBLOCKS * rank
    layers = 2
    z_at = lax.div(place_ref[0], sources // layers)

    def source(d):
        x_at, layer = lax.rem(d, sources // layers), lax.div(d, sources // layers)
        return x_at * layers + jnp.where(layer == z_at, 0, 1)

    mix = mix_ref[...]
    twice = jnp.concatenate([mix, mix], axis=1)
    terms = []
    for d in range(sources):
        for j in range(own):
            at = first + j * rank
            part = got_ref[d, at : at + rank, :].astype(F32) * twice
            terms.append(jnp.sum(part, axis=0, keepdims=True))
    weight = jnp.maximum(mm(fold(jnp.concatenate(terms, axis=0)), inverse_ref[...]), 0.0)
    weight_ref[...] = weight
    for j in range(own):
        own_ref[j : j + 1, :] = weight_ref[pl.ds(source(place_ref[0]) * own + j, 1), :]
    wgram_ref[...] = halves(mm(weight, weight, TN))
    acc_ref[...] = jnp.zeros(acc_ref.shape, F32)
    lane = lax.broadcasted_iota(jnp.int32, (rank, rows), 1)
    for t in range(slots):
        k, b, g, kept = live_rows(t, list_ref, count_ref, visits_ref, rows)
        d, j = source(lax.div(k, own)), lax.rem(k, own)
        both = jnp.concatenate(split(mix * weight_ref[pl.ds(d * own + j, 1), :]), axis=0)
        at = pl.multiple_of((j * VBLOCKS + b) * rank, rank)
        polar = got_ref[d, pl.ds(at, rank), :]
        spread = mm16(both, jnp.concatenate([polar, polar], axis=0), TN)
        spread = jnp.where(lane < kept, spread, 0.0).astype(BF16)
        acc_ref[g] += mm16(spread, tile_ref[t])
    parity = place_ref[1]
    for j in range(keep_ref.shape[0]):
        keep_ref[j] = acc_ref[2 * j + parity]
        send_ref[j] = acc_ref[2 * j + 1 - parity].astype(BF16)


def pair_kernel(keep_ref, came_ref, gram_a, gram_b, out_ref):
    low, lanes = gram_a.shape
    slabs = keep_ref.shape[2] // lanes
    piece = jnp.concatenate(split(gram_a[...] + gram_b[...]), axis=0)
    for j in range(keep_ref.shape[0]):
        both = (keep_ref[j] + came_ref[j]).astype(BF16)
        for i in range(slabs):
            out_ref[j, i] = both[:, i * lanes : (i + 1) * lanes]
        out_ref[j, slabs] = piece


def factor_kernel(got_ref, mgram_ref, out_ref):
    sources, slabs = got_ref.shape[0], got_ref.shape[1] - 1
    sums = []
    for i in range(slabs + 1):
        total = got_ref[0, i].astype(F32)
        for d in range(1, sources):
            total += got_ref[d, i].astype(F32)
        sums.append(total)
    low = sums[slabs].shape[0] // 2
    gram = whole(sums[slabs][:low] + sums[slabs][low:])
    inverse = damped_inverse(mgram_ref[...] * gram)
    code = jnp.maximum(mm(inverse, jnp.concatenate(sums[:slabs], axis=1)), 0.0).astype(BF16)
    for d in range(sources):
        out_ref[d] = code


def place_kernel(flip, place_ref, from_ref, *refs):
    out_hbm, wide_ref, sems = refs[-3:]
    parity = place_ref[1] if not flip else 1 - place_ref[1]
    cols = from_ref.shape[2]
    copies = []
    for j in range(from_ref.shape[0]):
        wide_ref[j] = from_ref[j].astype(F32)
        at = pl.multiple_of((2 * j + parity) * cols, cols)
        copies.append(
            pltpu.make_async_copy(wide_ref.at[j], out_hbm.at[:, pl.ds(at, cols)], sems.at[j])
        )
        copies[-1].start()
    for copy in copies:
        copy.wait()


def call(kernel, outs, specs, args, scratch=(), flops=1e9, spec=VM, alias=None, vmem=16):
    many = isinstance(outs, tuple)
    return pl.pallas_call(
        kernel,
        out_shape=outs,
        in_specs=specs,
        out_specs=(spec,) * len(outs) if many else spec,
        input_output_aliases=alias or {},
        scratch_shapes=scratch,
        compiler_params=pltpu.CompilerParams(vmem_limit_bytes=vmem * MIB),
        cost_estimate=pl.CostEstimate(flops=int(flops), bytes_accessed=65536, transcendentals=0),
    )(*args)


def swap(x, axis, bit):
    size = lax.axis_size(axis)
    return lax.ppermute(x, axis, [(i, i ^ bit) for i in range(size)])


def swap_z(x, high, low):
    n_pat, n_code = lax.axis_size("pat"), lax.axis_size("code")
    pairs = [
        (p * n_code + c, (p ^ (high * n_pat // 2)) * n_code + (c ^ (low * n_code // 2)))
        for p in range(n_pat)
        for c in range(n_code)
    ]
    return lax.ppermute(x, ("pat", "code"), pairs)


def plus(x, parts):
    for part in parts:
        x = x + part
    return x


def body(tile_data, tile_list, tile_count, visit_counts, code_factor_t, visit_mix, patient_weight):
    tiles = tile_data[0, 0]
    tile_list = jnp.transpose(tile_list, (0, 2, 1, 3))
    slots, rows, cols = tiles.shape
    rank = visit_mix.shape[0]
    patients = visit_counts.shape[0]
    n_code, n_pat = lax.axis_size("code"), lax.axis_size("pat")
    half = n_pat // 2
    own = patients // n_code
    code_at, pat_at = lax.axis_index("code"), lax.axis_index("pat")
    place = jnp.stack([code_at, lax.rem(pat_at, 2)]).astype(jnp.int32)
    shape = jax.ShapeDtypeStruct
    square = shape((rank, rank), F32)

    partial = call(
        products_kernel, shape((patients * VBLOCKS, rank, rows), F32), [HBM] * 5,
        (tile_list, tile_count, visit_counts, tile_data, code_factor_t),
        [
            pltpu.SMEM(tile_list.shape, jnp.int32), pltpu.SMEM(tile_count.shape, jnp.int32),
            pltpu.SMEM(visit_counts.shape, jnp.int32), pltpu.VMEM(tiles.shape, BF16),
            pltpu.VMEM(code_factor_t.shape, F32), pltpu.SemaphoreType.DMA((3,)),
            pltpu.SemaphoreType.DMA((5,)),
        ],
        vmem=50,
    )
    sent = partial.astype(F16).reshape(n_code, own * VBLOCKS * rank, rows)
    got = lax.all_to_all(sent, "code", 0, 0, tiled=True)
    gram = call(gram_kernel, shape((rank // 2, 2 * rank), F32), [VM], (code_factor_t,))
    products = jnp.sum(got.astype(F32), axis=0).reshape(own * VBLOCKS, rank, rows)

    scales = (1.0 / n_code, 1.0 / n_pat)
    length = (own * VBLOCKS + own) * rank
    sums, message = call(
        functools.partial(polar_kernel, scales),
        (shape((3 * rank // 2, 2 * rank), F32), shape((length, rows), BF16)),
        [SM, VM, VM, VM, VM], (place, products, visit_mix, patient_weight, gram), flops=5e9,
    )
    quarter = n_code // 2
    other = swap(message, "code", quarter)
    parts = [swap(sums, "code", bit) for bit in (1, 2, 3)]
    message = jnp.broadcast_to(jnp.concatenate([message, other])[None], (quarter, 2 * length, rows))
    message, *parts = lax.optimization_barrier((message, *parts))
    sums = plus(sums, parts)
    layers = [[z * quarter + i for i in range(quarter)] for z in (0, 1)]
    shared = lax.all_to_all(message, "code", 0, 0, axis_index_groups=layers, tiled=True)
    shared = shared.reshape(n_code, length, rows)
    sums = plus(sums, [swap(sums, "pat", bit) for bit in (2, 4, 6)])
    sums = sums + swap(sums, "pat", 1)
    mix_new, mix_again, mix_gram, inverse = call(
        mix_kernel, (square,) * 4, [VM] * 4,
        (sums, *(swap_z(sums, high, low) for high, low in ((0, 1), (1, 0), (1, 1)))), flops=5e9,
    )
    block = shape((half, rank, cols), F32)
    keep, send, wgram, weight_new = call(
        numer_kernel,
        (
            block, shape(block.shape, BF16), shape((rank // 2, 2 * rank), F32),
            shape((own, rank), F32),
        ),
        [SM, SM, SM, SM, VM, VM, VM, VM],
        (place, tile_list, tile_count, visit_counts, shared, mix_again, inverse, tiles),
        [pltpu.VMEM((n_pat, rank, cols), F32), pltpu.VMEM((patients, rank), F32)], flops=5e9,
    )
    groups = [[core + 2 * i for i in range(half)] for core in (0, 1)]

    def exchange(x):
        return lax.all_to_all(x, "pat", 0, 0, axis_index_groups=groups, tiled=True)

    lanes = 2 * rank
    packed = call(
        pair_kernel, shape((half, cols // lanes + 1, rank, lanes), BF16), [VM] * 4,
        (keep, swap(send, "pat", 1), wgram, swap(wgram, "pat", 1)),
    )
    code = call(
        factor_kernel, shape((half, rank, cols), BF16), [VM, VM], (exchange(packed), mix_gram)
    )
    mine = exchange(code)
    place_scratch = [pltpu.VMEM(mine.shape, F32), pltpu.SemaphoreType.DMA((half,))]
    result = shape((rank, n_pat * cols), F32)
    came = swap(mine, "pat", 1)
    code_new = call(
        functools.partial(place_kernel, False), result, [SM, VM], (place, mine), place_scratch,
        spec=HBM,
    )
    code_new = call(
        functools.partial(place_kernel, True), result, [SM, VM, HBM], (place, came, code_new),
        place_scratch, spec=HBM, alias={2: 0},
    )
    return (code_new, mix_new, weight_new)


def solution(mesh):
    placed = (
        P("pat", "code", None, None, None),
        P("pat", "code", None, None),
        P("pat", "code"),
        P("pat"),
        P(None, "code"),
        P(),
        P("pat", None),
    )
    return jax.shard_map(
        body,
        mesh=mesh,
        in_specs=placed,
        out_specs=(P(None, "code"), P(), P(("pat", "code"), None)),
        check_vma=False,
    )
```

```python
import functools

import jax
import jax.numpy as jnp
from jax import lax
from jax.experimental import pallas as pl
from jax.experimental.pallas import tpu as pltpu
from jax.sharding import PartitionSpec as P

VBLOCKS = 2
NS_STEPS = 8
damping = 0.1
epsilon = 1e-06
F32, BF16, F16 = jnp.float32, jnp.bfloat16, jnp.float16
VM = pl.BlockSpec(memory_space=pltpu.VMEM)
HBM = pl.BlockSpec(memory_space=pl.ANY)
SM = pl.BlockSpec(memory_space=pltpu.SMEM)
MIB = 1024 * 1024


def mm(a, b, dims=((1,), (0,))):
    return lax.dot_general(
        a, b, (dims, ((), ())), precision=lax.Precision.HIGHEST, preferred_element_type=F32
    )


def mm16(a, b, dims=((1,), (0,))):
    return lax.dot_general(a, b, (dims, ((), ())), preferred_element_type=F32)


NT = ((1,), (1,))
TN = ((0,), (0,))


def split(x):
    high = x.astype(BF16)
    return high, (x - high.astype(F32)).astype(BF16)


def mm3(a, b, dims=((1,), (0,))):
    return mm16(a[0], b[0], dims) + (mm16(a[0], b[1], dims) + mm16(a[1], b[0], dims))


def fold(x):
    half = x.shape[1] // 2
    return x[:, :half] + x[:, half:]


def times2(x, y):
    return [[x[i][0] * y[0][j] + x[i][1] * y[1][j] for j in (0, 1)] for i in (0, 1)]


def dot4(x, y):
    return (x[0] * y[0] + x[1] * y[1]) + (x[2] * y[2] + x[3] * y[3])


def inverse4(p):
    a = [[p[1][1], -p[0][1]], [-p[0][1], p[0][0]]]
    det = p[0][0] * p[1][1] - p[0][1] * p[0][1]
    b = [[p[0][2], p[0][3]], [p[1][2], p[1][3]]]
    t = times2(a, b)
    s00 = det * p[2][2] - (b[0][0] * t[0][0] + b[1][0] * t[1][0])
    s01 = det * p[2][3] - (b[0][0] * t[0][1] + b[1][0] * t[1][1])
    s11 = det * p[3][3] - (b[0][1] * t[0][1] + b[1][1] * t[1][1])
    over = 1.0 / (s00 * s11 - s01 * s01)
    over_det = 1.0 / det
    flip = [[s11, -s01], [-s01, s00]]
    u = times2(t, flip)
    v = times2(u, [[t[0][0], t[1][0]], [t[0][1], t[1][1]]])
    side = [[u[i][j] * over for j in (0, 1)] for i in (0, 1)]
    last = [[flip[i][j] * (det * over) for j in (0, 1)] for i in (0, 1)]
    first = [
        [a[i][j] * over_det + v[i][j] * (over * over_det) for j in (0, 1)] for i in (0, 1)
    ]
    return [
        [first[0][0], first[0][1], -side[0][0], -side[0][1]],
        [first[0][1], first[1][1], -side[1][0], -side[1][1]],
        [-side[0][0], -side[1][0], last[0][0], last[0][1]],
        [-side[0][1], -side[1][1], last[0][1], last[1][1]],
    ]


def halves(x):
    low = x.shape[0] // 2
    return jnp.concatenate([x[:low], x[low:]], axis=1)


def damped_inverse(gram):
    size = gram.shape[0]
    eye = lax.broadcasted_iota(jnp.int32, (size, size), 0) == lax.broadcasted_iota(
        jnp.int32, (size, size), 1
    )
    scale = size / jnp.sum(jnp.where(eye, gram, 0.0), keepdims=True)
    work = jnp.concatenate(
        [gram * scale + jnp.where(eye, damping, 0.0), eye.astype(F32)], axis=1
    )
    lanes = 2 * size
    four = range(4)
    blocks = [work[i : i + 8] for i in range(0, size, 8)]
    fresh = []
    for step in range(len(blocks)):
        j = 8 * step
        rows = [blocks[step][i : i + 1] for i in range(8)]

        def entry(i, k):
            return jnp.broadcast_to(rows[i][:, j + k : j + k + 1], (1, lanes))

        a = inverse4([[entry(i, k) if k >= i else None for k in four] for i in four])
        b = [[entry(i, 4 + k) for i in four] for k in four]
        t = [[dot4(a[i], b[k]) for i in four] for k in four]
        d = inverse4(
            [
                [entry(4 + i, 4 + k) - dot4(b[i], t[k]) if k >= i else None for k in four]
                for i in four
            ]
        )
        top = [dot4(a[i], rows[:4]) for i in four]
        rest = [rows[4 + i] - dot4(b[i], top) for i in four]
        low = [dot4(d[i], rest) for i in four]
        new = [top[i] - dot4([t[k][i] for k in four], low) for i in four] + low
        fresh += new
        for m in range(step + 1, len(blocks)):
            block = blocks[m]
            part = [block[:, j + k : j + k + 1] * new[k] for k in range(8)]
            blocks[m] = block - (
                ((part[0] + part[1]) + (part[2] + part[3]))
                + ((part[4] + part[5]) + (part[6] + part[7]))
            )
    raw = jnp.concatenate(blocks, axis=0)[:, size:]
    fresh = jnp.concatenate(fresh, axis=0)[:, size:]
    return scale * mm(raw, fresh, TN)


def live_rows(t, meta_ref, tile_rows):
    k, b, g = meta_ref[0, 0, 0, t], meta_ref[0, 1, 0, t], meta_ref[0, 2, 0, t]
    kept = jnp.where(t < meta_ref[0, 3, 0, 0], meta_ref[0, 4, 0, k] - tile_rows * b, 0)
    return k, b, g, kept


def products_kernel(
    meta_hbm, tile_hbm, code_hbm, out_ref, meta_ref, tile_ref, code_ref, small_sem, sems
):
    slots, rows, cols = tile_ref.shape
    rank = code_ref.shape[0]
    parts = sems.shape[0] - 1
    each = slots // parts
    small = pltpu.make_async_copy(meta_hbm, meta_ref, small_sem)
    small.start()
    code_copy = pltpu.make_async_copy(code_hbm, code_ref, sems.at[parts])
    code_copy.start()
    copies = []
    for i in range(parts):
        at = pl.ds(i * each, each)
        copies.append(pltpu.make_async_copy(tile_hbm.at[0, 0, at], tile_ref.at[at], sems.at[i]))
        copies[-1].start()
    out_ref[...] = jnp.zeros(out_ref.shape, F32)
    lane = lax.broadcasted_iota(jnp.int32, (rank, rows), 1)
    small.wait()
    code_copy.wait()
    for t in range(slots):
        if t % each == 0:
            copies[t // each].wait()
        k, b, g, kept = live_rows(t, meta_ref, rows)
        codes = code_ref[:, pl.ds(pl.multiple_of(g * cols, cols), cols)].astype(BF16)
        part = mm16(codes, tile_ref[t], NT)
        out_ref[k * VBLOCKS + b] += jnp.where(lane < kept, part, 0.0)


def gram_kernel(code_ref, out_ref):
    high, low = split(code_ref[...])
    cross = mm16(high, low, NT)
    out_ref[...] = halves(mm16(high, high, NT) + cross + cross.T)


def polar_kernel(
    scales, at_ref, prod_ref, mix_ref, weight_ref, gram_ref, sums_ref, out_ref
):
    segs, rank, rows = prod_ref.shape
    own = segs // VBLOCKS
    eye = lax.broadcasted_iota(jnp.int32, (rank, rank), 0) == lax.broadcasted_iota(
        jnp.int32, (rank, rank), 1
    )
    prods, zs, weights = [], [], []
    for j in range(own):
        prods.append(
            split(jnp.concatenate([prod_ref[VBLOCKS * j + b] for b in range(VBLOCKS)], axis=1))
        )
        weights.append(weight_ref[pl.ds(at_ref[0] * own + j, 1), :])
        target = mm3(split(mix_ref[...] * weights[j]), prods[j])
        zs.append(target / jnp.sqrt(jnp.sum(target * target, keepdims=True) + epsilon))
    zs = [split(z) for z in zs]
    for _ in range(NS_STEPS):
        factors = [split(jnp.where(eye, 1.5, 0.0) - 0.5 * mm3(z, z, NT)) for z in zs]
        zs = [split(mm3(q, z)) for q, z in zip(factors, zs)]
    pieces = [z[0][:, b * rows : (b + 1) * rows] for z in zs for b in range(VBLOCKS)]
    numer = jnp.zeros((rank, rank), F32)
    for z, p, weight in zip(zs, prods, weights):
        projected = mm3(z, p, NT)
        numer += projected * weight
        pieces.append(jnp.concatenate(split(projected), axis=1))
    low = rank // 2
    weight = weight_ref[...]
    sums_ref[:low, :] = halves(numer)
    sums_ref[low:rank, :] = halves(mm(weight, weight, TN)) * scales[0]
    sums_ref[rank:, :] = gram_ref[...] * scales[1]
    for i, piece in enumerate(pieces):
        out_ref[i * rank : (i + 1) * rank, :] = piece


def whole(x):
    rank = x.shape[1] // 2
    return jnp.concatenate([x[:, :rank], x[:, rank:]], axis=0)


def mix_kernel(a_ref, b_ref, c_ref, d_ref, mix_ref, again_ref, mgram_ref, inverse_ref):
    sums = (a_ref[...] + b_ref[...]) + (c_ref[...] + d_ref[...])
    rank = mix_ref.shape[0]
    low = rank // 2
    weight_gram, code_gram = whole(sums[low:rank]), whole(sums[rank:])
    mix = mm(whole(sums[:low]), damped_inverse(code_gram * weight_gram))
    again_ref[...] = mix
    mix_ref[...] = mix
    mix_gram = mm(mix, mix, TN)
    mgram_ref[...] = mix_gram
    inverse_ref[...] = damped_inverse(mix_gram * code_gram)


def numer_kernel(
    place_ref, meta_ref, got_ref, mix_ref, inverse_ref, tile_ref,
    keep_ref, send_ref, wgram_ref, own_ref, acc_ref, weight_ref,
):
    slots, rows, cols = tile_ref.shape
    sources = got_ref.shape[0]
    rank = mix_ref.shape[0]
    own = own_ref.shape[0]
    first = own * VBLOCKS * rank
    layers = 2
    z_at = lax.div(place_ref[0], sources // layers)

    def source(d):
        x_at, layer = lax.rem(d, sources // layers), lax.div(d, sources // layers)
        return x_at * layers + jnp.where(layer == z_at, 0, 1)

    mix = mix_ref[...]
    twice = jnp.concatenate([mix, mix], axis=1)
    terms = []
    for d in range(sources):
        for j in range(own):
            at = first + j * rank
            part = got_ref[d, at : at + rank, :].astype(F32) * twice
            terms.append(jnp.sum(part, axis=0, keepdims=True))
    weight = jnp.maximum(mm(fold(jnp.concatenate(terms, axis=0)), inverse_ref[...]), 0.0)
    weight_ref[...] = weight
    for j in range(own):
        own_ref[j : j + 1, :] = weight_ref[pl.ds(source(place_ref[0]) * own + j, 1), :]
    wgram_ref[...] = halves(mm(weight, weight, TN))
    acc_ref[...] = jnp.zeros(acc_ref.shape, F32)
    lane = lax.broadcasted_iota(jnp.int32, (rank, rows), 1)
    for t in range(slots):
        k, b, g, kept = live_rows(t, meta_ref, rows)
        d, j = source(lax.div(k, own)), lax.rem(k, own)
        both = jnp.concatenate(split(mix * weight_ref[pl.ds(d * own + j, 1), :]), axis=0)
        at = pl.multiple_of((j * VBLOCKS + b) * rank, rank)
        polar = got_ref[d, pl.ds(at, rank), :]
        spread = mm16(both, jnp.concatenate([polar, polar], axis=0), TN)
        spread = jnp.where(lane < kept, spread, 0.0).astype(BF16)
        acc_ref[g] += mm16(spread, tile_ref[t])
    parity = place_ref[1]
    for j in range(keep_ref.shape[0]):
        keep_ref[j] = acc_ref[2 * j + parity]
        send_ref[j] = acc_ref[2 * j + 1 - parity].astype(BF16)


def pair_kernel(keep_ref, came_ref, gram_a, gram_b, out_ref):
    low, lanes = gram_a.shape
    slabs = keep_ref.shape[2] // lanes
    piece = jnp.concatenate(split(gram_a[...] + gram_b[...]), axis=0)
    for j in range(keep_ref.shape[0]):
        both = (keep_ref[j] + came_ref[j]).astype(BF16)
        for i in range(slabs):
            out_ref[j, i] = both[:, i * lanes : (i + 1) * lanes]
        out_ref[j, slabs] = piece


def factor_kernel(got_ref, mgram_ref, out_ref):
    sources, slabs = got_ref.shape[0], got_ref.shape[1] - 1
    sums = []
    for i in range(slabs + 1):
        total = got_ref[0, i].astype(F32)
        for d in range(1, sources):
            total += got_ref[d, i].astype(F32)
        sums.append(total)
    low = sums[slabs].shape[0] // 2
    gram = whole(sums[slabs][:low] + sums[slabs][low:])
    inverse = damped_inverse(mgram_ref[...] * gram)
    code = jnp.maximum(mm(inverse, jnp.concatenate(sums[:slabs], axis=1)), 0.0).astype(BF16)
    for d in range(sources):
        out_ref[d] = code


def place_kernel(flip, place_ref, from_ref, *refs):
    out_hbm, wide_ref, sems = refs[-3:]
    parity = place_ref[1] if not flip else 1 - place_ref[1]
    cols = from_ref.shape[2]
    copies = []
    for j in range(from_ref.shape[0]):
        wide_ref[j] = from_ref[j].astype(F32)
        at = pl.multiple_of((2 * j + parity) * cols, cols)
        copies.append(
            pltpu.make_async_copy(wide_ref.at[j], out_hbm.at[:, pl.ds(at, cols)], sems.at[j])
        )
        copies[-1].start()
    for copy in copies:
        copy.wait()


def call(kernel, outs, specs, args, scratch=(), flops=1e9, spec=VM, alias=None, vmem=16):
    many = isinstance(outs, tuple)
    return pl.pallas_call(
        kernel,
        out_shape=outs,
        in_specs=specs,
        out_specs=(spec,) * len(outs) if many else spec,
        input_output_aliases=alias or {},
        scratch_shapes=scratch,
        compiler_params=pltpu.CompilerParams(vmem_limit_bytes=vmem * MIB),
        cost_estimate=pl.CostEstimate(flops=int(flops), bytes_accessed=65536, transcendentals=0),
    )(*args)


def swap(x, axis, bit):
    size = lax.axis_size(axis)
    return lax.ppermute(x, axis, [(i, i ^ bit) for i in range(size)])


def swap_z(x, high, low):
    n_pat, n_code = lax.axis_size("pat"), lax.axis_size("code")
    pairs = [
        (p * n_code + c, (p ^ (high * n_pat // 2)) * n_code + (c ^ (low * n_code // 2)))
        for p in range(n_pat)
        for c in range(n_code)
    ]
    return lax.ppermute(x, ("pat", "code"), pairs)


def plus(x, parts):
    for part in parts:
        x = x + part
    return x


def body(tile_data, tile_list, tile_count, visit_counts, code_factor_t, visit_mix, patient_weight):
    tiles = tile_data[0, 0]
    slots, rows, cols = tiles.shape
    rank = visit_mix.shape[0]
    patients = visit_counts.shape[0]
    n_code, n_pat = lax.axis_size("code"), lax.axis_size("pat")
    half = n_pat // 2
    own = patients // n_code
    code_at, pat_at = lax.axis_index("code"), lax.axis_index("pat")
    meta = jnp.concatenate(
        [
            jnp.pad(
                jnp.transpose(tile_list, (0, 2, 1, 3)),
                ((0, 0), (0, 0), (0, 0), (0, patients - slots)),
            ),
            jnp.broadcast_to(tile_count[0, 0], (1, 1, 1, patients)),
            visit_counts.reshape(1, 1, 1, patients),
        ],
        axis=1,
    )
    place = jnp.stack([code_at, lax.rem(pat_at, 2)]).astype(jnp.int32)
    shape = jax.ShapeDtypeStruct
    square = shape((rank, rank), F32)

    partial = call(
        products_kernel, shape((patients * VBLOCKS, rank, rows), F32), [HBM] * 3,
        (meta, tile_data, code_factor_t),
        [
            pltpu.SMEM(meta.shape, jnp.int32), pltpu.VMEM(tiles.shape, BF16),
            pltpu.VMEM(code_factor_t.shape, F32), pltpu.SemaphoreType.DMA(()),
            pltpu.SemaphoreType.DMA((5,)),
        ],
        vmem=50,
    )
    sent = partial.astype(F16).reshape(n_code, own * VBLOCKS * rank, rows)
    got = lax.all_to_all(sent, "code", 0, 0, tiled=True)
    gram = call(gram_kernel, shape((rank // 2, 2 * rank), F32), [VM], (code_factor_t,))
    products = jnp.sum(got.astype(F32), axis=0).reshape(own * VBLOCKS, rank, rows)

    scales = (1.0 / n_code, 1.0 / n_pat)
    length = (own * VBLOCKS + own) * rank
    sums, message = call(
        functools.partial(polar_kernel, scales),
        (shape((3 * rank // 2, 2 * rank), F32), shape((length, rows), BF16)),
        [SM, VM, VM, VM, VM], (place, products, visit_mix, patient_weight, gram), flops=5e9,
    )
    quarter = n_code // 2
    other = swap(message, "code", quarter)
    parts = [swap(sums, "code", bit) for bit in (1, 2, 3)]
    message = jnp.broadcast_to(jnp.concatenate([message, other])[None], (quarter, 2 * length, rows))
    message, *parts = lax.optimization_barrier((message, *parts))
    sums = plus(sums, parts)
    layers = [[z * quarter + i for i in range(quarter)] for z in (0, 1)]
    shared = lax.all_to_all(message, "code", 0, 0, axis_index_groups=layers, tiled=True)
    shared = shared.reshape(n_code, length, rows)
    sums = plus(sums, [swap(sums, "pat", bit) for bit in (2, 4, 6)])
    sums = sums + swap(sums, "pat", 1)
    mix_new, mix_again, mix_gram, inverse = call(
        mix_kernel, (square,) * 4, [VM] * 4,
        (sums, *(swap_z(sums, high, low) for high, low in ((0, 1), (1, 0), (1, 1)))), flops=5e9,
    )
    block = shape((half, rank, cols), F32)
    keep, send, wgram, weight_new = call(
        numer_kernel,
        (
            block, shape(block.shape, BF16), shape((rank // 2, 2 * rank), F32),
            shape((own, rank), F32),
        ),
        [SM, SM, VM, VM, VM, VM],
        (place, meta, shared, mix_again, inverse, tiles),
        [pltpu.VMEM((n_pat, rank, cols), F32), pltpu.VMEM((patients, rank), F32)], flops=5e9,
    )
    groups = [[core + 2 * i for i in range(half)] for core in (0, 1)]

    def exchange(x):
        return lax.all_to_all(x, "pat", 0, 0, axis_index_groups=groups, tiled=True)

    lanes = 2 * rank
    packed = call(
        pair_kernel, shape((half, cols // lanes + 1, rank, lanes), BF16), [VM] * 4,
        (keep, swap(send, "pat", 1), wgram, swap(wgram, "pat", 1)),
    )
    code = call(
        factor_kernel, shape((half, rank, cols), BF16), [VM, VM], (exchange(packed), mix_gram)
    )
    mine = exchange(code)
    place_scratch = [pltpu.VMEM(mine.shape, F32), pltpu.SemaphoreType.DMA((half,))]
    result = shape((rank, n_pat * cols), F32)
    came = swap(mine, "pat", 1)
    code_new = call(
        functools.partial(place_kernel, False), result, [SM, VM], (place, mine), place_scratch,
        spec=HBM,
    )
    code_new = call(
        functools.partial(place_kernel, True), result, [SM, VM, HBM], (place, came, code_new),
        place_scratch, spec=HBM, alias={2: 0},
    )
    return (code_new, mix_new, weight_new)


def solution(mesh):
    placed = (
        P("pat", "code", None, None, None),
        P("pat", "code", None, None),
        P("pat", "code"),
        P("pat"),
        P(None, "code"),
        P(),
        P("pat", None),
    )
    return jax.shard_map(
        body,
        mesh=mesh,
        in_specs=placed,
        out_specs=(P(None, "code"), P(), P(("pat", "code"), None)),
        check_vma=False,
    )
```

```python
import functools

import jax
import jax.numpy as jnp
from jax import lax
from jax.experimental import pallas as pl
from jax.experimental.pallas import tpu as pltpu
from jax.sharding import PartitionSpec as P

VBLOCKS = 2
NS_STEPS = 8
damping = 0.1
epsilon = 1e-06
F32, BF16, F16 = jnp.float32, jnp.bfloat16, jnp.float16
VM = pl.BlockSpec(memory_space=pltpu.VMEM)
HBM = pl.BlockSpec(memory_space=pl.ANY)
SM = pl.BlockSpec(memory_space=pltpu.SMEM)
MIB = 1024 * 1024


def mm(a, b, dims=((1,), (0,))):
    return lax.dot_general(
        a, b, (dims, ((), ())), precision=lax.Precision.HIGHEST, preferred_element_type=F32
    )


def mm16(a, b, dims=((1,), (0,))):
    return lax.dot_general(a, b, (dims, ((), ())), preferred_element_type=F32)


NT = ((1,), (1,))
TN = ((0,), (0,))


def split(x):
    high = x.astype(BF16)
    return high, (x - high.astype(F32)).astype(BF16)


def mm3(a, b, dims=((1,), (0,))):
    return mm16(a[0], b[0], dims) + (mm16(a[0], b[1], dims) + mm16(a[1], b[0], dims))


def fold(x):
    half = x.shape[1] // 2
    return x[:, :half] + x[:, half:]


def times2(x, y):
    return [[x[i][0] * y[0][j] + x[i][1] * y[1][j] for j in (0, 1)] for i in (0, 1)]


def dot4(x, y):
    return (x[0] * y[0] + x[1] * y[1]) + (x[2] * y[2] + x[3] * y[3])


def inverse4(p):
    a = [[p[1][1], -p[0][1]], [-p[0][1], p[0][0]]]
    det = p[0][0] * p[1][1] - p[0][1] * p[0][1]
    b = [[p[0][2], p[0][3]], [p[1][2], p[1][3]]]
    t = times2(a, b)
    s00 = det * p[2][2] - (b[0][0] * t[0][0] + b[1][0] * t[1][0])
    s01 = det * p[2][3] - (b[0][0] * t[0][1] + b[1][0] * t[1][1])
    s11 = det * p[3][3] - (b[0][1] * t[0][1] + b[1][1] * t[1][1])
    over = 1.0 / (s00 * s11 - s01 * s01)
    over_det = 1.0 / det
    flip = [[s11, -s01], [-s01, s00]]
    u = times2(t, flip)
    v = times2(u, [[t[0][0], t[1][0]], [t[0][1], t[1][1]]])
    side = [[u[i][j] * over for j in (0, 1)] for i in (0, 1)]
    last = [[flip[i][j] * (det * over) for j in (0, 1)] for i in (0, 1)]
    first = [
        [a[i][j] * over_det + v[i][j] * (over * over_det) for j in (0, 1)] for i in (0, 1)
    ]
    return [
        [first[0][0], first[0][1], -side[0][0], -side[0][1]],
        [first[0][1], first[1][1], -side[1][0], -side[1][1]],
        [-side[0][0], -side[1][0], last[0][0], last[0][1]],
        [-side[0][1], -side[1][1], last[0][1], last[1][1]],
    ]


def halves(x):
    low = x.shape[0] // 2
    return jnp.concatenate([x[:low], x[low:]], axis=1)


def damped_inverse(gram):
    size = gram.shape[0]
    eye = lax.broadcasted_iota(jnp.int32, (size, size), 0) == lax.broadcasted_iota(
        jnp.int32, (size, size), 1
    )
    scale = size / jnp.sum(jnp.where(eye, gram, 0.0), keepdims=True)
    work = jnp.concatenate(
        [gram * scale + jnp.where(eye, damping, 0.0), eye.astype(F32)], axis=1
    )
    lanes = 2 * size
    four = range(4)
    blocks = [work[i : i + 8] for i in range(0, size, 8)]
    fresh = []
    for step in range(len(blocks)):
        j = 8 * step
        rows = [blocks[step][i : i + 1] for i in range(8)]

        def entry(i, k):
            return jnp.broadcast_to(rows[i][:, j + k : j + k + 1], (1, lanes))

        a = inverse4([[entry(i, k) if k >= i else None for k in four] for i in four])
        b = [[entry(i, 4 + k) for i in four] for k in four]
        t = [[dot4(a[i], b[k]) for i in four] for k in four]
        d = inverse4(
            [
                [entry(4 + i, 4 + k) - dot4(b[i], t[k]) if k >= i else None for k in four]
                for i in four
            ]
        )
        top = [dot4(a[i], rows[:4]) for i in four]
        rest = [rows[4 + i] - dot4(b[i], top) for i in four]
        low = [dot4(d[i], rest) for i in four]
        new = [top[i] - dot4([t[k][i] for k in four], low) for i in four] + low
        fresh += new
        for m in range(step + 1, len(blocks)):
            block = blocks[m]
            part = [block[:, j + k : j + k + 1] * new[k] for k in range(8)]
            blocks[m] = block - (
                ((part[0] + part[1]) + (part[2] + part[3]))
                + ((part[4] + part[5]) + (part[6] + part[7]))
            )
    raw = jnp.concatenate(blocks, axis=0)[:, size:]
    fresh = jnp.concatenate(fresh, axis=0)[:, size:]
    return scale * mm(raw, fresh, TN)


def live_rows(t, meta_ref, tile_rows):
    k, b, g = meta_ref[0, 0, 0, t], meta_ref[0, 1, 0, t], meta_ref[0, 2, 0, t]
    kept = jnp.where(t < meta_ref[0, 3, 0, 0], meta_ref[0, 4, 0, k] - tile_rows * b, 0)
    return k, b, g, kept


def products_kernel(
    meta_hbm, tile_hbm, code_hbm, out_ref, meta_ref, tile_ref, code_ref, small_sem, band_sems, sems
):
    slots, rows, cols = tile_ref.shape
    rank = code_ref.shape[0]
    parts = sems.shape[0]
    each = slots // parts
    small = pltpu.make_async_copy(meta_hbm, meta_ref, small_sem)
    small.start()
    bands = band_sems.shape[0]
    band = rank // bands
    band_copies = []
    for i in range(bands):
        at = pl.ds(i * band, band)
        band_copies.append(
            pltpu.make_async_copy(code_hbm.at[at], code_ref.at[at], band_sems.at[i])
        )
        band_copies[-1].start()
    copies = []
    for i in range(parts):
        at = pl.ds(i * each, each)
        copies.append(pltpu.make_async_copy(tile_hbm.at[0, 0, at], tile_ref.at[at], sems.at[i]))
        copies[-1].start()
    out_ref[...] = jnp.zeros(out_ref.shape, F32)
    lane = lax.broadcasted_iota(jnp.int32, (rank, rows), 1)
    small.wait()
    for copy in band_copies:
        copy.wait()
    for t in range(slots):
        if t % each == 0:
            copies[t // each].wait()
        k, b, g, kept = live_rows(t, meta_ref, rows)
        codes = code_ref[:, pl.ds(pl.multiple_of(g * cols, cols), cols)].astype(BF16)
        part = mm16(codes, tile_ref[t], NT)
        out_ref[k * VBLOCKS + b] += jnp.where(lane < kept, part, 0.0)


def gram_kernel(code_ref, out_ref):
    high, low = split(code_ref[...])
    cross = mm16(high, low, NT)
    out_ref[...] = halves(mm16(high, high, NT) + cross + cross.T)


def polar_kernel(
    scales, at_ref, prod_ref, mix_ref, weight_ref, gram_ref, sums_ref, out_ref
):
    segs, rank, rows = prod_ref.shape
    own = segs // VBLOCKS
    eye = lax.broadcasted_iota(jnp.int32, (rank, rank), 0) == lax.broadcasted_iota(
        jnp.int32, (rank, rank), 1
    )
    prods, zs, weights = [], [], []
    for j in range(own):
        prods.append(
            split(jnp.concatenate([prod_ref[VBLOCKS * j + b] for b in range(VBLOCKS)], axis=1))
        )
        weights.append(weight_ref[pl.ds(at_ref[0] * own + j, 1), :])
        target = mm3(split(mix_ref[...] * weights[j]), prods[j])
        zs.append(target / jnp.sqrt(jnp.sum(target * target, keepdims=True) + epsilon))
    zs = [split(z) for z in zs]
    for _ in range(NS_STEPS):
        factors = [split(jnp.where(eye, 1.5, 0.0) - 0.5 * mm3(z, z, NT)) for z in zs]
        zs = [split(mm3(q, z)) for q, z in zip(factors, zs)]
    pieces = [z[0][:, b * rows : (b + 1) * rows] for z in zs for b in range(VBLOCKS)]
    numer = jnp.zeros((rank, rank), F32)
    for z, p, weight in zip(zs, prods, weights):
        projected = mm3(z, p, NT)
        numer += projected * weight
        pieces.append(jnp.concatenate(split(projected), axis=1))
    low = rank // 2
    weight = weight_ref[...]
    sums_ref[:low, :] = halves(numer)
    sums_ref[low:rank, :] = halves(mm(weight, weight, TN)) * scales[0]
    sums_ref[rank:, :] = gram_ref[...] * scales[1]
    for i, piece in enumerate(pieces):
        out_ref[i * rank : (i + 1) * rank, :] = piece


def whole(x):
    rank = x.shape[1] // 2
    return jnp.concatenate([x[:, :rank], x[:, rank:]], axis=0)


def mix_kernel(a_ref, b_ref, c_ref, d_ref, mix_ref, again_ref, mgram_ref, inverse_ref):
    sums = (a_ref[...] + b_ref[...]) + (c_ref[...] + d_ref[...])
    rank = mix_ref.shape[0]
    low = rank // 2
    weight_gram, code_gram = whole(sums[low:rank]), whole(sums[rank:])
    mix = mm(whole(sums[:low]), damped_inverse(code_gram * weight_gram))
    again_ref[...] = mix
    mix_ref[...] = mix
    mix_gram = mm(mix, mix, TN)
    mgram_ref[...] = mix_gram
    inverse_ref[...] = damped_inverse(mix_gram * code_gram)


def numer_kernel(
    place_ref, meta_ref, got_ref, mix_ref, inverse_ref, tile_ref,
    keep_ref, send_ref, wgram_ref, own_ref, acc_ref, weight_ref,
):
    slots, rows, cols = tile_ref.shape
    sources = got_ref.shape[0]
    rank = mix_ref.shape[0]
    own = own_ref.shape[0]
    first = own * VBLOCKS * rank
    layers = 2
    z_at = lax.div(place_ref[0], sources // layers)

    def source(d):
        x_at, layer = lax.rem(d, sources // layers), lax.div(d, sources // layers)
        return x_at * layers + jnp.where(layer == z_at, 0, 1)

    mix = mix_ref[...]
    twice = jnp.concatenate([mix, mix], axis=1)
    terms = []
    for d in range(sources):
        for j in range(own):
            at = first + j * rank
            part = got_ref[d, at : at + rank, :].astype(F32) * twice
            terms.append(jnp.sum(part, axis=0, keepdims=True))
    weight = jnp.maximum(mm(fold(jnp.concatenate(terms, axis=0)), inverse_ref[...]), 0.0)
    weight_ref[...] = weight
    for j in range(own):
        own_ref[j : j + 1, :] = weight_ref[pl.ds(source(place_ref[0]) * own + j, 1), :]
    wgram_ref[...] = halves(mm(weight, weight, TN))
    acc_ref[...] = jnp.zeros(acc_ref.shape, F32)
    lane = lax.broadcasted_iota(jnp.int32, (rank, rows), 1)
    for t in range(slots):
        k, b, g, kept = live_rows(t, meta_ref, rows)
        d, j = source(lax.div(k, own)), lax.rem(k, own)
        both = jnp.concatenate(split(mix * weight_ref[pl.ds(d * own + j, 1), :]), axis=0)
        at = pl.multiple_of((j * VBLOCKS + b) * rank, rank)
        polar = got_ref[d, pl.ds(at, rank), :]
        spread = mm16(both, jnp.concatenate([polar, polar], axis=0), TN)
        spread = jnp.where(lane < kept, spread, 0.0).astype(BF16)
        acc_ref[g] += mm16(spread, tile_ref[t])
    parity = place_ref[1]
    for j in range(keep_ref.shape[0]):
        keep_ref[j] = acc_ref[2 * j + parity]
        send_ref[j] = acc_ref[2 * j + 1 - parity].astype(BF16)


def pair_kernel(keep_ref, came_ref, gram_a, gram_b, out_ref):
    low, lanes = gram_a.shape
    slabs = keep_ref.shape[2] // lanes
    piece = jnp.concatenate(split(gram_a[...] + gram_b[...]), axis=0)
    for j in range(keep_ref.shape[0]):
        both = (keep_ref[j] + came_ref[j]).astype(BF16)
        for i in range(slabs):
            out_ref[j, i] = both[:, i * lanes : (i + 1) * lanes]
        out_ref[j, slabs] = piece


def factor_kernel(got_ref, mgram_ref, out_ref):
    sources, slabs = got_ref.shape[0], got_ref.shape[1] - 1
    sums = []
    for i in range(slabs + 1):
        total = got_ref[0, i].astype(F32)
        for d in range(1, sources):
            total += got_ref[d, i].astype(F32)
        sums.append(total)
    low = sums[slabs].shape[0] // 2
    gram = whole(sums[slabs][:low] + sums[slabs][low:])
    inverse = damped_inverse(mgram_ref[...] * gram)
    code = jnp.maximum(mm(inverse, jnp.concatenate(sums[:slabs], axis=1)), 0.0).astype(BF16)
    for d in range(sources):
        out_ref[d] = code


def place_kernel(flip, place_ref, from_ref, *refs):
    out_hbm, wide_ref, sems = refs[-3:]
    parity = place_ref[1] if not flip else 1 - place_ref[1]
    cols = from_ref.shape[2]
    copies = []
    for j in range(from_ref.shape[0]):
        wide_ref[j] = from_ref[j].astype(F32)
        at = pl.multiple_of((2 * j + parity) * cols, cols)
        copies.append(
            pltpu.make_async_copy(wide_ref.at[j], out_hbm.at[:, pl.ds(at, cols)], sems.at[j])
        )
        copies[-1].start()
    for copy in copies:
        copy.wait()


def call(kernel, outs, specs, args, scratch=(), flops=1e9, spec=VM, alias=None, vmem=16):
    many = isinstance(outs, tuple)
    return pl.pallas_call(
        kernel,
        out_shape=outs,
        in_specs=specs,
        out_specs=(spec,) * len(outs) if many else spec,
        input_output_aliases=alias or {},
        scratch_shapes=scratch,
        compiler_params=pltpu.CompilerParams(vmem_limit_bytes=vmem * MIB),
        cost_estimate=pl.CostEstimate(flops=int(flops), bytes_accessed=65536, transcendentals=0),
    )(*args)


def swap(x, axis, bit):
    size = lax.axis_size(axis)
    return lax.ppermute(x, axis, [(i, i ^ bit) for i in range(size)])


def swap_z(x, high, low):
    n_pat, n_code = lax.axis_size("pat"), lax.axis_size("code")
    pairs = [
        (p * n_code + c, (p ^ (high * n_pat // 2)) * n_code + (c ^ (low * n_code // 2)))
        for p in range(n_pat)
        for c in range(n_code)
    ]
    return lax.ppermute(x, ("pat", "code"), pairs)


def plus(x, parts):
    for part in parts:
        x = x + part
    return x


def body(tile_data, tile_list, tile_count, visit_counts, code_factor_t, visit_mix, patient_weight):
    tiles = tile_data[0, 0]
    slots, rows, cols = tiles.shape
    rank = visit_mix.shape[0]
    patients = visit_counts.shape[0]
    n_code, n_pat = lax.axis_size("code"), lax.axis_size("pat")
    half = n_pat // 2
    own = patients // n_code
    code_at, pat_at = lax.axis_index("code"), lax.axis_index("pat")
    meta = jnp.concatenate(
        [
            jnp.pad(
                jnp.transpose(tile_list, (0, 2, 1, 3)),
                ((0, 0), (0, 0), (0, 0), (0, patients - slots)),
            ),
            jnp.broadcast_to(tile_count[0, 0], (1, 1, 1, patients)),
            visit_counts.reshape(1, 1, 1, patients),
        ],
        axis=1,
    )
    place = jnp.stack([code_at, lax.rem(pat_at, 2)]).astype(jnp.int32)
    shape = jax.ShapeDtypeStruct
    square = shape((rank, rank), F32)

    partial = call(
        products_kernel, shape((patients * VBLOCKS, rank, rows), F32), [HBM] * 3,
        (meta, tile_data, code_factor_t),
        [
            pltpu.SMEM(meta.shape, jnp.int32), pltpu.VMEM(tiles.shape, BF16),
            pltpu.VMEM(code_factor_t.shape, F32), pltpu.SemaphoreType.DMA(()),
            pltpu.SemaphoreType.DMA((8,)), pltpu.SemaphoreType.DMA((4,)),
        ],
        vmem=50,
    )
    sent = partial.astype(F16).reshape(n_code, own * VBLOCKS * rank, rows)
    got = lax.all_to_all(sent, "code", 0, 0, tiled=True)
    gram = call(gram_kernel, shape((rank // 2, 2 * rank), F32), [VM], (code_factor_t,))
    products = jnp.sum(got.astype(F32), axis=0).reshape(own * VBLOCKS, rank, rows)

    scales = (1.0 / n_code, 1.0 / n_pat)
    length = (own * VBLOCKS + own) * rank
    sums, message = call(
        functools.partial(polar_kernel, scales),
        (shape((3 * rank // 2, 2 * rank), F32), shape((length, rows), BF16)),
        [SM, VM, VM, VM, VM], (place, products, visit_mix, patient_weight, gram), flops=5e9,
    )
    quarter = n_code // 2
    other = swap(message, "code", quarter)
    parts = [swap(sums, "code", bit) for bit in (1, 2, 3)]
    message = jnp.broadcast_to(jnp.concatenate([message, other])[None], (quarter, 2 * length, rows))
    message, *parts = lax.optimization_barrier((message, *parts))
    sums = plus(sums, parts)
    layers = [[z * quarter + i for i in range(quarter)] for z in (0, 1)]
    shared = lax.all_to_all(message, "code", 0, 0, axis_index_groups=layers, tiled=True)
    shared = shared.reshape(n_code, length, rows)
    sums = plus(sums, [swap(sums, "pat", bit) for bit in (2, 4, 6)])
    sums = sums + swap(sums, "pat", 1)
    mix_new, mix_again, mix_gram, inverse = call(
        mix_kernel, (square,) * 4, [VM] * 4,
        (sums, *(swap_z(sums, high, low) for high, low in ((0, 1), (1, 0), (1, 1)))), flops=5e9,
    )
    block = shape((half, rank, cols), F32)
    keep, send, wgram, weight_new = call(
        numer_kernel,
        (
            block, shape(block.shape, BF16), shape((rank // 2, 2 * rank), F32),
            shape((own, rank), F32),
        ),
        [SM, SM, VM, VM, VM, VM],
        (place, meta, shared, mix_again, inverse, tiles),
        [pltpu.VMEM((n_pat, rank, cols), F32), pltpu.VMEM((patients, rank), F32)], flops=5e9,
    )
    groups = [[core + 2 * i for i in range(half)] for core in (0, 1)]

    def exchange(x):
        return lax.all_to_all(x, "pat", 0, 0, axis_index_groups=groups, tiled=True)

    lanes = 2 * rank
    packed = call(
        pair_kernel, shape((half, cols // lanes + 1, rank, lanes), BF16), [VM] * 4,
        (keep, swap(send, "pat", 1), wgram, swap(wgram, "pat", 1)),
    )
    code = call(
        factor_kernel, shape((half, rank, cols), BF16), [VM, VM], (exchange(packed), mix_gram)
    )
    mine = exchange(code)
    place_scratch = [pltpu.VMEM(mine.shape, F32), pltpu.SemaphoreType.DMA((half,))]
    result = shape((rank, n_pat * cols), F32)
    came = swap(mine, "pat", 1)
    code_new = call(
        functools.partial(place_kernel, False), result, [SM, VM], (place, mine), place_scratch,
        spec=HBM,
    )
    code_new = call(
        functools.partial(place_kernel, True), result, [SM, VM, HBM], (place, came, code_new),
        place_scratch, spec=HBM, alias={2: 0},
    )
    return (code_new, mix_new, weight_new)


def solution(mesh):
    placed = (
        P("pat", "code", None, None, None),
        P("pat", "code", None, None),
        P("pat", "code"),
        P("pat"),
        P(None, "code"),
        P(),
        P("pat", None),
    )
    return jax.shard_map(
        body,
        mesh=mesh,
        in_specs=placed,
        out_specs=(P(None, "code"), P(), P(("pat", "code"), None)),
        check_vma=False,
    )
```

```python
import functools

import jax
import jax.numpy as jnp
from jax import lax
from jax.experimental import pallas as pl
from jax.experimental.pallas import tpu as pltpu
from jax.sharding import PartitionSpec as P

VBLOCKS = 2
NS_STEPS = 8
damping = 0.1
epsilon = 1e-06
F32, BF16, F16 = jnp.float32, jnp.bfloat16, jnp.float16
VM = pl.BlockSpec(memory_space=pltpu.VMEM)
HBM = pl.BlockSpec(memory_space=pl.ANY)
SM = pl.BlockSpec(memory_space=pltpu.SMEM)
MIB = 1024 * 1024


def mm(a, b, dims=((1,), (0,))):
    return lax.dot_general(
        a, b, (dims, ((), ())), precision=lax.Precision.HIGHEST, preferred_element_type=F32
    )


def mm16(a, b, dims=((1,), (0,))):
    return lax.dot_general(a, b, (dims, ((), ())), preferred_element_type=F32)


NT = ((1,), (1,))
TN = ((0,), (0,))


def split(x):
    high = x.astype(BF16)
    return high, (x - high.astype(F32)).astype(BF16)


def mm3(a, b, dims=((1,), (0,))):
    return mm16(a[0], b[0], dims) + (mm16(a[0], b[1], dims) + mm16(a[1], b[0], dims))


def fold(x):
    half = x.shape[1] // 2
    return x[:, :half] + x[:, half:]


def times2(x, y):
    return [[x[i][0] * y[0][j] + x[i][1] * y[1][j] for j in (0, 1)] for i in (0, 1)]


def dot4(x, y):
    return (x[0] * y[0] + x[1] * y[1]) + (x[2] * y[2] + x[3] * y[3])


def inverse4(p):
    a = [[p[1][1], -p[0][1]], [-p[0][1], p[0][0]]]
    det = p[0][0] * p[1][1] - p[0][1] * p[0][1]
    b = [[p[0][2], p[0][3]], [p[1][2], p[1][3]]]
    t = times2(a, b)
    s00 = det * p[2][2] - (b[0][0] * t[0][0] + b[1][0] * t[1][0])
    s01 = det * p[2][3] - (b[0][0] * t[0][1] + b[1][0] * t[1][1])
    s11 = det * p[3][3] - (b[0][1] * t[0][1] + b[1][1] * t[1][1])
    over = 1.0 / (s00 * s11 - s01 * s01)
    over_det = 1.0 / det
    flip = [[s11, -s01], [-s01, s00]]
    u = times2(t, flip)
    v = times2(u, [[t[0][0], t[1][0]], [t[0][1], t[1][1]]])
    side = [[u[i][j] * over for j in (0, 1)] for i in (0, 1)]
    last = [[flip[i][j] * (det * over) for j in (0, 1)] for i in (0, 1)]
    first = [
        [a[i][j] * over_det + v[i][j] * (over * over_det) for j in (0, 1)] for i in (0, 1)
    ]
    return [
        [first[0][0], first[0][1], -side[0][0], -side[0][1]],
        [first[0][1], first[1][1], -side[1][0], -side[1][1]],
        [-side[0][0], -side[1][0], last[0][0], last[0][1]],
        [-side[0][1], -side[1][1], last[0][1], last[1][1]],
    ]


def halves(x):
    low = x.shape[0] // 2
    return jnp.concatenate([x[:low], x[low:]], axis=1)


def damped_inverse(gram):
    size = gram.shape[0]
    eye = lax.broadcasted_iota(jnp.int32, (size, size), 0) == lax.broadcasted_iota(
        jnp.int32, (size, size), 1
    )
    scale = size / jnp.sum(jnp.where(eye, gram, 0.0), keepdims=True)
    work = jnp.concatenate(
        [gram * scale + jnp.where(eye, damping, 0.0), eye.astype(F32)], axis=1
    )
    lanes = 2 * size
    four = range(4)
    blocks = [work[i : i + 8] for i in range(0, size, 8)]
    fresh = []
    for step in range(len(blocks)):
        j = 8 * step
        rows = [blocks[step][i : i + 1] for i in range(8)]

        def entry(i, k):
            return jnp.broadcast_to(rows[i][:, j + k : j + k + 1], (1, lanes))

        a = inverse4([[entry(i, k) if k >= i else None for k in four] for i in four])
        b = [[entry(i, 4 + k) for i in four] for k in four]
        t = [[dot4(a[i], b[k]) for i in four] for k in four]
        d = inverse4(
            [
                [entry(4 + i, 4 + k) - dot4(b[i], t[k]) if k >= i else None for k in four]
                for i in four
            ]
        )
        top = [dot4(a[i], rows[:4]) for i in four]
        rest = [rows[4 + i] - dot4(b[i], top) for i in four]
        low = [dot4(d[i], rest) for i in four]
        new = [top[i] - dot4([t[k][i] for k in four], low) for i in four] + low
        fresh += new
        for m in range(step + 1, len(blocks)):
            block = blocks[m]
            part = [block[:, j + k : j + k + 1] * new[k] for k in range(8)]
            blocks[m] = block - (
                ((part[0] + part[1]) + (part[2] + part[3]))
                + ((part[4] + part[5]) + (part[6] + part[7]))
            )
    raw = jnp.concatenate(blocks, axis=0)[:, size:]
    fresh = jnp.concatenate(fresh, axis=0)[:, size:]
    return scale * mm(raw, fresh, TN)


def live_rows(t, meta_ref, tile_rows):
    k, b, g = meta_ref[0, 0, 0, t], meta_ref[0, 1, 0, t], meta_ref[0, 2, 0, t]
    kept = jnp.where(t < meta_ref[0, 3, 0, 0], meta_ref[0, 4, 0, k] - tile_rows * b, 0)
    return k, b, g, kept


def products_kernel(
    meta_hbm, tile_hbm, code_hbm, out_ref, meta_ref, tile_ref, code_ref, small_sem, sems
):
    slots, rows, cols = tile_ref.shape
    rank = code_ref.shape[0]
    parts = sems.shape[0] - 1
    each = slots // parts
    small = pltpu.make_async_copy(meta_hbm, meta_ref, small_sem)
    small.start()
    code_copy = pltpu.make_async_copy(code_hbm, code_ref, sems.at[parts])
    code_copy.start()
    copies = []
    for i in range(parts):
        at = pl.ds(i * each, each)
        copies.append(pltpu.make_async_copy(tile_hbm.at[0, 0, at], tile_ref.at[at], sems.at[i]))
        copies[-1].start()
    out_ref[...] = jnp.zeros(out_ref.shape, F32)
    lane = lax.broadcasted_iota(jnp.int32, (rank, rows), 1)
    small.wait()
    code_copy.wait()
    for t in range(slots):
        if t % each == 0:
            copies[t // each].wait()
        k, b, g, kept = live_rows(t, meta_ref, rows)
        codes = code_ref[:, pl.ds(pl.multiple_of(g * cols, cols), cols)].astype(BF16)
        part = mm16(codes, tile_ref[t], NT)
        out_ref[k * VBLOCKS + b] += jnp.where(lane < kept, part, 0.0)


def gram_kernel(code_ref, out_ref):
    high, low = split(code_ref[...])
    cross = mm16(high, low, NT)
    out_ref[...] = halves(mm16(high, high, NT) + cross + cross.T)


def polar_kernel(
    scales, at_ref, prod_ref, mix_ref, weight_ref, gram_ref, sums_ref, out_ref
):
    segs, rank, rows = prod_ref.shape
    own = segs // VBLOCKS
    eye = lax.broadcasted_iota(jnp.int32, (rank, rank), 0) == lax.broadcasted_iota(
        jnp.int32, (rank, rank), 1
    )
    prods, zs, weights = [], [], []
    for j in range(own):
        prods.append(
            split(jnp.concatenate([prod_ref[VBLOCKS * j + b] for b in range(VBLOCKS)], axis=1))
        )
        weights.append(weight_ref[pl.ds(at_ref[0] * own + j, 1), :])
        target = mm3(split(mix_ref[...] * weights[j]), prods[j])
        zs.append(target / jnp.sqrt(jnp.sum(target * target, keepdims=True) + epsilon))
    zs = [split(z) for z in zs]
    for _ in range(NS_STEPS):
        factors = [split(jnp.where(eye, 1.5, 0.0) - 0.5 * mm3(z, z, NT)) for z in zs]
        zs = [split(mm3(q, z)) for q, z in zip(factors, zs)]
    pieces = [z[0][:, b * rows : (b + 1) * rows] for z in zs for b in range(VBLOCKS)]
    numer = jnp.zeros((rank, rank), F32)
    for z, p, weight in zip(zs, prods, weights):
        projected = mm3(z, p, NT)
        numer += projected * weight
        pieces.append(jnp.concatenate(split(projected), axis=1))
    low = rank // 2
    weight = weight_ref[...]
    sums_ref[:low, :] = halves(mm(weight, weight, TN)) * scales[0]
    sums_ref[low:rank, :] = halves(numer)
    sums_ref[rank:, :] = gram_ref[...] * scales[1]
    for i, piece in enumerate(pieces):
        out_ref[i * rank : (i + 1) * rank, :] = piece


def whole(x):
    rank = x.shape[1] // 2
    return jnp.concatenate([x[:, :rank], x[:, rank:]], axis=0)


def mix_kernel(a_ref, b_ref, c_ref, d_ref, mix_ref, again_ref, mgram_ref, inverse_ref):
    sums = (a_ref[...] + b_ref[...]) + (c_ref[...] + d_ref[...])
    rank = mix_ref.shape[0]
    low = rank // 2
    weight_gram, code_gram = whole(sums[:low]), whole(sums[rank:])
    mix = mm(whole(sums[low:rank]), damped_inverse(code_gram * weight_gram))
    again_ref[...] = mix
    mix_ref[...] = mix
    mix_gram = mm(mix, mix, TN)
    mgram_ref[...] = mix_gram
    inverse_ref[...] = damped_inverse(mix_gram * code_gram)


def numer_kernel(
    place_ref, meta_ref, got_ref, mix_ref, inverse_ref, tile_ref,
    keep_ref, send_ref, wgram_ref, own_ref, acc_ref, weight_ref,
):
    slots, rows, cols = tile_ref.shape
    sources = got_ref.shape[0]
    rank = mix_ref.shape[0]
    own = own_ref.shape[0]
    first = own * VBLOCKS * rank
    layers = 2
    z_at = lax.div(place_ref[0], sources // layers)

    def source(d):
        x_at, layer = lax.rem(d, sources // layers), lax.div(d, sources // layers)
        return x_at * layers + jnp.where(layer == z_at, 0, 1)

    mix = mix_ref[...]
    twice = jnp.concatenate([mix, mix], axis=1)
    terms = []
    for d in range(sources):
        for j in range(own):
            at = first + j * rank
            part = got_ref[d, at : at + rank, :].astype(F32) * twice
            terms.append(jnp.sum(part, axis=0, keepdims=True))
    weight = jnp.maximum(mm(fold(jnp.concatenate(terms, axis=0)), inverse_ref[...]), 0.0)
    weight_ref[...] = weight
    for j in range(own):
        own_ref[j : j + 1, :] = weight_ref[pl.ds(source(place_ref[0]) * own + j, 1), :]
    wgram_ref[...] = halves(mm(weight, weight, TN))
    acc_ref[...] = jnp.zeros(acc_ref.shape, F32)
    lane = lax.broadcasted_iota(jnp.int32, (rank, rows), 1)
    for t in range(slots):
        k, b, g, kept = live_rows(t, meta_ref, rows)
        d, j = source(lax.div(k, own)), lax.rem(k, own)
        both = jnp.concatenate(split(mix * weight_ref[pl.ds(d * own + j, 1), :]), axis=0)
        at = pl.multiple_of((j * VBLOCKS + b) * rank, rank)
        polar = got_ref[d, pl.ds(at, rank), :]
        spread = mm16(both, jnp.concatenate([polar, polar], axis=0), TN)
        spread = jnp.where(lane < kept, spread, 0.0).astype(BF16)
        acc_ref[g] += mm16(spread, tile_ref[t])
    parity = place_ref[1]
    for j in range(keep_ref.shape[0]):
        keep_ref[j] = acc_ref[2 * j + parity]
        send_ref[j] = acc_ref[2 * j + 1 - parity].astype(BF16)


def pair_kernel(keep_ref, came_ref, gram_a, gram_b, out_ref):
    low, lanes = gram_a.shape
    slabs = keep_ref.shape[2] // lanes
    piece = jnp.concatenate(split(gram_a[...] + gram_b[...]), axis=0)
    for j in range(keep_ref.shape[0]):
        both = (keep_ref[j] + came_ref[j]).astype(BF16)
        for i in range(slabs):
            out_ref[j, i] = both[:, i * lanes : (i + 1) * lanes]
        out_ref[j, slabs] = piece


def factor_kernel(got_ref, mgram_ref, out_ref):
    sources, slabs = got_ref.shape[0], got_ref.shape[1] - 1
    sums = []
    for i in range(slabs + 1):
        total = got_ref[0, i].astype(F32)
        for d in range(1, sources):
            total += got_ref[d, i].astype(F32)
        sums.append(total)
    low = sums[slabs].shape[0] // 2
    gram = whole(sums[slabs][:low] + sums[slabs][low:])
    inverse = damped_inverse(mgram_ref[...] * gram)
    code = jnp.maximum(mm(inverse, jnp.concatenate(sums[:slabs], axis=1)), 0.0).astype(BF16)
    for d in range(sources):
        out_ref[d] = code


def place_kernel(flip, place_ref, from_ref, *refs):
    out_hbm, wide_ref, sems = refs[-3:]
    parity = place_ref[1] if not flip else 1 - place_ref[1]
    cols = from_ref.shape[2]
    copies = []
    for j in range(from_ref.shape[0]):
        wide_ref[j] = from_ref[j].astype(F32)
        at = pl.multiple_of((2 * j + parity) * cols, cols)
        copies.append(
            pltpu.make_async_copy(wide_ref.at[j], out_hbm.at[:, pl.ds(at, cols)], sems.at[j])
        )
        copies[-1].start()
    for copy in copies:
        copy.wait()


def call(kernel, outs, specs, args, scratch=(), flops=1e9, spec=VM, alias=None, vmem=16):
    many = isinstance(outs, tuple)
    return pl.pallas_call(
        kernel,
        out_shape=outs,
        in_specs=specs,
        out_specs=(spec,) * len(outs) if many else spec,
        input_output_aliases=alias or {},
        scratch_shapes=scratch,
        compiler_params=pltpu.CompilerParams(vmem_limit_bytes=vmem * MIB),
        cost_estimate=pl.CostEstimate(flops=int(flops), bytes_accessed=65536, transcendentals=0),
    )(*args)


def swap(x, axis, bit):
    size = lax.axis_size(axis)
    return lax.ppermute(x, axis, [(i, i ^ bit) for i in range(size)])


def swap_z(x, high, low):
    n_pat, n_code = lax.axis_size("pat"), lax.axis_size("code")
    pairs = [
        (p * n_code + c, (p ^ (high * n_pat // 2)) * n_code + (c ^ (low * n_code // 2)))
        for p in range(n_pat)
        for c in range(n_code)
    ]
    return lax.ppermute(x, ("pat", "code"), pairs)


def plus(x, parts):
    for part in parts:
        x = x + part
    return x


def body(tile_data, tile_list, tile_count, visit_counts, code_factor_t, visit_mix, patient_weight):
    tiles = tile_data[0, 0]
    slots, rows, cols = tiles.shape
    rank = visit_mix.shape[0]
    patients = visit_counts.shape[0]
    n_code, n_pat = lax.axis_size("code"), lax.axis_size("pat")
    half = n_pat // 2
    own = patients // n_code
    code_at, pat_at = lax.axis_index("code"), lax.axis_index("pat")
    meta = jnp.concatenate(
        [
            jnp.pad(
                jnp.transpose(tile_list, (0, 2, 1, 3)),
                ((0, 0), (0, 0), (0, 0), (0, patients - slots)),
            ),
            jnp.broadcast_to(tile_count[0, 0], (1, 1, 1, patients)),
            visit_counts.reshape(1, 1, 1, patients),
        ],
        axis=1,
    )
    place = jnp.stack([code_at, lax.rem(pat_at, 2)]).astype(jnp.int32)
    shape = jax.ShapeDtypeStruct
    square = shape((rank, rank), F32)

    partial = call(
        products_kernel, shape((patients * VBLOCKS, rank, rows), F32), [HBM] * 3,
        (meta, tile_data, code_factor_t),
        [
            pltpu.SMEM(meta.shape, jnp.int32), pltpu.VMEM(tiles.shape, BF16),
            pltpu.VMEM(code_factor_t.shape, F32), pltpu.SemaphoreType.DMA(()),
            pltpu.SemaphoreType.DMA((5,)),
        ],
        vmem=50,
    )
    sent = partial.astype(F16).reshape(n_code, own * VBLOCKS * rank, rows)
    got = lax.all_to_all(sent, "code", 0, 0, tiled=True)
    gram = call(gram_kernel, shape((rank // 2, 2 * rank), F32), [VM], (code_factor_t,))
    products = jnp.sum(got.astype(F32), axis=0).reshape(own * VBLOCKS, rank, rows)

    scales = (0.5, 0.5)
    length = (own * VBLOCKS + own) * rank
    sums, message = call(
        functools.partial(polar_kernel, scales),
        (shape((3 * rank // 2, 2 * rank), F32), shape((length, rows), BF16)),
        [SM, VM, VM, VM, VM], (place, products, visit_mix, patient_weight, gram), flops=5e9,
    )
    quarter = n_code // 2
    other = swap(message, "code", quarter)
    low = rank // 2
    weight_gram, sums = sums[:low], sums[low:]
    parts = [swap(sums, "code", bit) for bit in (1, 2, 3)]
    message = jnp.broadcast_to(jnp.concatenate([message, other])[None], (quarter, 2 * length, rows))
    message, *parts = lax.optimization_barrier((message, *parts))
    sums = plus(sums, parts)
    code_gram, sums = sums[low:], jnp.concatenate([weight_gram, sums[:low]])
    layers = [[z * quarter + i for i in range(quarter)] for z in (0, 1)]
    shared = lax.all_to_all(message, "code", 0, 0, axis_index_groups=layers, tiled=True)
    shared = shared.reshape(n_code, length, rows)
    sums = plus(sums, [swap(sums, "pat", bit) for bit in (2, 4, 6)])
    sums = sums + swap(sums, "pat", 1)
    sums = jnp.concatenate([sums, code_gram])
    mix_new, mix_again, mix_gram, inverse = call(
        mix_kernel, (square,) * 4, [VM] * 4,
        (sums, *(swap_z(sums, high, low) for high, low in ((0, 1), (1, 0), (1, 1)))), flops=5e9,
    )
    block = shape((half, rank, cols), F32)
    keep, send, wgram, weight_new = call(
        numer_kernel,
        (
            block, shape(block.shape, BF16), shape((rank // 2, 2 * rank), F32),
            shape((own, rank), F32),
        ),
        [SM, SM, VM, VM, VM, VM],
        (place, meta, shared, mix_again, inverse, tiles),
        [pltpu.VMEM((n_pat, rank, cols), F32), pltpu.VMEM((patients, rank), F32)], flops=5e9,
    )
    groups = [[core + 2 * i for i in range(half)] for core in (0, 1)]

    def exchange(x):
        return lax.all_to_all(x, "pat", 0, 0, axis_index_groups=groups, tiled=True)

    lanes = 2 * rank
    packed = call(
        pair_kernel, shape((half, cols // lanes + 1, rank, lanes), BF16), [VM] * 4,
        (keep, swap(send, "pat", 1), wgram, swap(wgram, "pat", 1)),
    )
    code = call(
        factor_kernel, shape((half, rank, cols), BF16), [VM, VM], (exchange(packed), mix_gram)
    )
    mine = exchange(code)
    place_scratch = [pltpu.VMEM(mine.shape, F32), pltpu.SemaphoreType.DMA((half,))]
    result = shape((rank, n_pat * cols), F32)
    came = swap(mine, "pat", 1)
    code_new = call(
        functools.partial(place_kernel, False), result, [SM, VM], (place, mine), place_scratch,
        spec=HBM,
    )
    code_new = call(
        functools.partial(place_kernel, True), result, [SM, VM, HBM], (place, came, code_new),
        place_scratch, spec=HBM, alias={2: 0},
    )
    return (code_new, mix_new, weight_new)


def solution(mesh):
    placed = (
        P("pat", "code", None, None, None),
        P("pat", "code", None, None),
        P("pat", "code"),
        P("pat"),
        P(None, "code"),
        P(),
        P("pat", None),
    )
    return jax.shard_map(
        body,
        mesh=mesh,
        in_specs=placed,
        out_specs=(P(None, "code"), P(), P(("pat", "code"), None)),
        check_vma=False,
    )
```

```python
import functools

import jax
import jax.numpy as jnp
from jax import lax
from jax.experimental import pallas as pl
from jax.experimental.pallas import tpu as pltpu
from jax.sharding import PartitionSpec as P

VBLOCKS = 2
NS_STEPS = 8
damping = 0.1
epsilon = 1e-06
F32, BF16, F16 = jnp.float32, jnp.bfloat16, jnp.float16
VM = pl.BlockSpec(memory_space=pltpu.VMEM)
HBM = pl.BlockSpec(memory_space=pl.ANY)
SM = pl.BlockSpec(memory_space=pltpu.SMEM)
MIB = 1024 * 1024


def mm(a, b, dims=((1,), (0,))):
    return lax.dot_general(
        a, b, (dims, ((), ())), precision=lax.Precision.HIGHEST, preferred_element_type=F32
    )


def mm16(a, b, dims=((1,), (0,))):
    return lax.dot_general(a, b, (dims, ((), ())), preferred_element_type=F32)


NT = ((1,), (1,))
TN = ((0,), (0,))


def split(x):
    high = x.astype(BF16)
    return high, (x - high.astype(F32)).astype(BF16)


def mm3(a, b, dims=((1,), (0,))):
    return mm16(a[0], b[0], dims) + (mm16(a[0], b[1], dims) + mm16(a[1], b[0], dims))


def fold(x):
    half = x.shape[1] // 2
    return x[:, :half] + x[:, half:]


def times2(x, y):
    return [[x[i][0] * y[0][j] + x[i][1] * y[1][j] for j in (0, 1)] for i in (0, 1)]


def dot4(x, y):
    return (x[0] * y[0] + x[1] * y[1]) + (x[2] * y[2] + x[3] * y[3])


def inverse4(p):
    a = [[p[1][1], -p[0][1]], [-p[0][1], p[0][0]]]
    det = p[0][0] * p[1][1] - p[0][1] * p[0][1]
    b = [[p[0][2], p[0][3]], [p[1][2], p[1][3]]]
    t = times2(a, b)
    s00 = det * p[2][2] - (b[0][0] * t[0][0] + b[1][0] * t[1][0])
    s01 = det * p[2][3] - (b[0][0] * t[0][1] + b[1][0] * t[1][1])
    s11 = det * p[3][3] - (b[0][1] * t[0][1] + b[1][1] * t[1][1])
    over = 1.0 / (s00 * s11 - s01 * s01)
    over_det = 1.0 / det
    flip = [[s11, -s01], [-s01, s00]]
    u = times2(t, flip)
    v = times2(u, [[t[0][0], t[1][0]], [t[0][1], t[1][1]]])
    side = [[u[i][j] * over for j in (0, 1)] for i in (0, 1)]
    last = [[flip[i][j] * (det * over) for j in (0, 1)] for i in (0, 1)]
    first = [
        [a[i][j] * over_det + v[i][j] * (over * over_det) for j in (0, 1)] for i in (0, 1)
    ]
    return [
        [first[0][0], first[0][1], -side[0][0], -side[0][1]],
        [first[0][1], first[1][1], -side[1][0], -side[1][1]],
        [-side[0][0], -side[1][0], last[0][0], last[0][1]],
        [-side[0][1], -side[1][1], last[0][1], last[1][1]],
    ]


def halves(x):
    low = x.shape[0] // 2
    return jnp.concatenate([x[:low], x[low:]], axis=1)


def damped_inverse(gram):
    size = gram.shape[0]
    eye = lax.broadcasted_iota(jnp.int32, (size, size), 0) == lax.broadcasted_iota(
        jnp.int32, (size, size), 1
    )
    scale = size / jnp.sum(jnp.where(eye, gram, 0.0), keepdims=True)
    work = jnp.concatenate(
        [gram * scale + jnp.where(eye, damping, 0.0), eye.astype(F32)], axis=1
    )
    lanes = 2 * size
    four = range(4)
    blocks = [work[i : i + 8] for i in range(0, size, 8)]
    fresh = []
    for step in range(len(blocks)):
        j = 8 * step
        rows = [blocks[step][i : i + 1] for i in range(8)]

        def entry(i, k):
            return jnp.broadcast_to(rows[i][:, j + k : j + k + 1], (1, lanes))

        a = inverse4([[entry(i, k) if k >= i else None for k in four] for i in four])
        b = [[entry(i, 4 + k) for i in four] for k in four]
        t = [[dot4(a[i], b[k]) for i in four] for k in four]
        d = inverse4(
            [
                [entry(4 + i, 4 + k) - dot4(b[i], t[k]) if k >= i else None for k in four]
                for i in four
            ]
        )
        top = [dot4(a[i], rows[:4]) for i in four]
        rest = [rows[4 + i] - dot4(b[i], top) for i in four]
        low = [dot4(d[i], rest) for i in four]
        new = [top[i] - dot4([t[k][i] for k in four], low) for i in four] + low
        fresh += new
        for m in range(step + 1, len(blocks)):
            block = blocks[m]
            part = [block[:, j + k : j + k + 1] * new[k] for k in range(8)]
            blocks[m] = block - (
                ((part[0] + part[1]) + (part[2] + part[3]))
                + ((part[4] + part[5]) + (part[6] + part[7]))
            )
    raw = jnp.concatenate(blocks, axis=0)[:, size:]
    fresh = jnp.concatenate(fresh, axis=0)[:, size:]
    return scale * mm(raw, fresh, TN)


def live_rows(t, meta_ref, tile_rows):
    k, b, g = meta_ref[0, 0, 0, t], meta_ref[0, 1, 0, t], meta_ref[0, 2, 0, t]
    kept = jnp.where(t < meta_ref[0, 3, 0, 0], meta_ref[0, 4, 0, k] - tile_rows * b, 0)
    return k, b, g, kept


def products_kernel(
    meta_hbm, tile_hbm, code_hbm, out_ref, meta_ref, tile_ref, code_ref, small_sem, sems
):
    slots, rows, cols = tile_ref.shape
    rank = code_ref.shape[0]
    parts = sems.shape[0] - 1
    each = slots // parts
    small = pltpu.make_async_copy(meta_hbm, meta_ref, small_sem)
    small.start()
    code_copy = pltpu.make_async_copy(code_hbm, code_ref, sems.at[parts])
    code_copy.start()
    copies = []
    for i in range(parts):
        at = pl.ds(i * each, each)
        copies.append(pltpu.make_async_copy(tile_hbm.at[0, 0, at], tile_ref.at[at], sems.at[i]))
        copies[-1].start()
    out_ref[...] = jnp.zeros(out_ref.shape, F32)
    lane = lax.broadcasted_iota(jnp.int32, (rank, rows), 1)
    small.wait()
    code_copy.wait()
    for t in range(slots):
        if t % each == 0:
            copies[t // each].wait()
        k, b, g, kept = live_rows(t, meta_ref, rows)
        codes = code_ref[:, pl.ds(pl.multiple_of(g * cols, cols), cols)].astype(BF16)
        part = mm16(codes, tile_ref[t], NT)
        out_ref[k * VBLOCKS + b] += jnp.where(lane < kept, part, 0.0)


def gram_kernel(code_ref, out_ref):
    high, low = split(code_ref[...])
    cross = mm16(high, low, NT)
    out_ref[...] = halves(mm16(high, high, NT) + cross + cross.T)


def polar_kernel(
    scales, at_ref, prod_ref, mix_ref, weight_ref, gram_ref, sums_ref, out_ref
):
    segs, rank, rows = prod_ref.shape
    own = segs // VBLOCKS
    eye = lax.broadcasted_iota(jnp.int32, (rank, rank), 0) == lax.broadcasted_iota(
        jnp.int32, (rank, rank), 1
    )
    prods, zs, weights = [], [], []
    for j in range(own):
        prods.append(
            split(jnp.concatenate([prod_ref[VBLOCKS * j + b] for b in range(VBLOCKS)], axis=1))
        )
        weights.append(weight_ref[pl.ds(at_ref[0] * own + j, 1), :])
        target = mm3(split(mix_ref[...] * weights[j]), prods[j])
        zs.append(target / jnp.sqrt(jnp.sum(target * target, keepdims=True) + epsilon))
    zs = [split(z) for z in zs]
    for _ in range(NS_STEPS):
        factors = [split(jnp.where(eye, 1.5, 0.0) - 0.5 * mm3(z, z, NT)) for z in zs]
        zs = [split(mm3(q, z)) for q, z in zip(factors, zs)]
    pieces = [z[0][:, b * rows : (b + 1) * rows] for z in zs for b in range(VBLOCKS)]
    numer = jnp.zeros((rank, rank), F32)
    for z, p, weight in zip(zs, prods, weights):
        projected = mm3(z, p, NT)
        numer += projected * weight
        pieces.append(jnp.concatenate(split(projected), axis=1))
    low = rank // 2
    weight = weight_ref[...]
    sums_ref[:low, :] = halves(mm(weight, weight, TN)) * scales[0]
    sums_ref[low:rank, :] = halves(numer)
    sums_ref[rank:, :] = gram_ref[...] * scales[1]
    for i, piece in enumerate(pieces):
        out_ref[i * rank : (i + 1) * rank, :] = piece


def whole(x):
    rank = x.shape[1] // 2
    return jnp.concatenate([x[:, :rank], x[:, rank:]], axis=0)


def mix_kernel(a_ref, b_ref, c_ref, d_ref, mix_ref, again_ref, mgram_ref, inverse_ref):
    sums = (a_ref[...] + b_ref[...]) + (c_ref[...] + d_ref[...])
    rank = mix_ref.shape[0]
    low = rank // 2
    weight_gram, code_gram = whole(sums[:low]), whole(sums[rank:])
    mix = mm(whole(sums[low:rank]), damped_inverse(code_gram * weight_gram))
    again_ref[...] = mix
    mix_ref[...] = mix
    mix_gram = mm(mix, mix, TN)
    mgram_ref[...] = mix_gram
    inverse_ref[...] = damped_inverse(mix_gram * code_gram)


def numer_kernel(
    place_ref, meta_ref, got_ref, mix_ref, inverse_ref, tile_ref,
    keep_ref, send_ref, wgram_ref, own_ref, acc_ref, weight_ref,
):
    acc_ref[...] = jnp.zeros(acc_ref.shape, F32)
    slots, rows, cols = tile_ref.shape
    sources = got_ref.shape[0]
    rank = mix_ref.shape[0]
    own = own_ref.shape[0]
    first = own * VBLOCKS * rank
    layers = 2
    z_at = lax.div(place_ref[0], sources // layers)

    def source(d):
        x_at, layer = lax.rem(d, sources // layers), lax.div(d, sources // layers)
        return x_at * layers + jnp.where(layer == z_at, 0, 1)

    mix = mix_ref[...]
    twice = jnp.concatenate([mix, mix], axis=1)
    terms = []
    for d in range(sources):
        for j in range(own):
            at = first + j * rank
            part = got_ref[d, at : at + rank, :].astype(F32) * twice
            terms.append(jnp.sum(part, axis=0, keepdims=True))
    weight = jnp.maximum(mm(fold(jnp.concatenate(terms, axis=0)), inverse_ref[...]), 0.0)
    weight_ref[...] = weight
    for j in range(own):
        own_ref[j : j + 1, :] = weight_ref[pl.ds(source(place_ref[0]) * own + j, 1), :]
    wgram_ref[...] = halves(mm(weight, weight, TN))
    lane = lax.broadcasted_iota(jnp.int32, (rank, rows), 1)
    for t in range(slots):
        k, b, g, kept = live_rows(t, meta_ref, rows)
        d, j = source(lax.div(k, own)), lax.rem(k, own)
        both = jnp.concatenate(split(mix * weight_ref[pl.ds(d * own + j, 1), :]), axis=0)
        at = pl.multiple_of((j * VBLOCKS + b) * rank, rank)
        polar = got_ref[d, pl.ds(at, rank), :]
        spread = mm16(both, jnp.concatenate([polar, polar], axis=0), TN)
        spread = jnp.where(lane < kept, spread, 0.0).astype(BF16)
        acc_ref[g] += mm16(spread, tile_ref[t])
    parity = place_ref[1]
    for j in range(keep_ref.shape[0]):
        keep_ref[j] = acc_ref[2 * j + parity]
        send_ref[j] = acc_ref[2 * j + 1 - parity].astype(BF16)


def pair_kernel(keep_ref, came_ref, gram_a, gram_b, out_ref):
    low, lanes = gram_a.shape
    slabs = keep_ref.shape[2] // lanes
    piece = jnp.concatenate(split(gram_a[...] + gram_b[...]), axis=0)
    for j in range(keep_ref.shape[0]):
        both = (keep_ref[j] + came_ref[j]).astype(BF16)
        for i in range(slabs):
            out_ref[j, i] = both[:, i * lanes : (i + 1) * lanes]
        out_ref[j, slabs] = piece


def factor_kernel(got_ref, mgram_ref, out_ref):
    sources, slabs = got_ref.shape[0], got_ref.shape[1] - 1
    sums = []
    for i in range(slabs + 1):
        total = got_ref[0, i].astype(F32)
        for d in range(1, sources):
            total += got_ref[d, i].astype(F32)
        sums.append(total)
    low = sums[slabs].shape[0] // 2
    gram = whole(sums[slabs][:low] + sums[slabs][low:])
    inverse = damped_inverse(mgram_ref[...] * gram)
    code = jnp.maximum(mm(inverse, jnp.concatenate(sums[:slabs], axis=1)), 0.0).astype(BF16)
    for d in range(sources):
        out_ref[d] = code


def place_kernel(flip, place_ref, from_ref, *refs):
    out_hbm, wide_ref, sems = refs[-3:]
    parity = place_ref[1] if not flip else 1 - place_ref[1]
    cols = from_ref.shape[2]
    copies = []
    for j in range(from_ref.shape[0]):
        wide_ref[j] = from_ref[j].astype(F32)
        at = pl.multiple_of((2 * j + parity) * cols, cols)
        copies.append(
            pltpu.make_async_copy(wide_ref.at[j], out_hbm.at[:, pl.ds(at, cols)], sems.at[j])
        )
        copies[-1].start()
    for copy in copies:
        copy.wait()


def call(kernel, outs, specs, args, scratch=(), flops=1e9, spec=VM, alias=None, vmem=16):
    many = isinstance(outs, tuple)
    return pl.pallas_call(
        kernel,
        out_shape=outs,
        in_specs=specs,
        out_specs=(spec,) * len(outs) if many else spec,
        input_output_aliases=alias or {},
        scratch_shapes=scratch,
        compiler_params=pltpu.CompilerParams(vmem_limit_bytes=vmem * MIB),
        cost_estimate=pl.CostEstimate(flops=int(flops), bytes_accessed=65536, transcendentals=0),
    )(*args)


def swap(x, axis, bit):
    size = lax.axis_size(axis)
    return lax.ppermute(x, axis, [(i, i ^ bit) for i in range(size)])


def swap_z(x, high, low):
    n_pat, n_code = lax.axis_size("pat"), lax.axis_size("code")
    pairs = [
        (p * n_code + c, (p ^ (high * n_pat // 2)) * n_code + (c ^ (low * n_code // 2)))
        for p in range(n_pat)
        for c in range(n_code)
    ]
    return lax.ppermute(x, ("pat", "code"), pairs)


def plus(x, parts):
    for part in parts:
        x = x + part
    return x


def body(tile_data, tile_list, tile_count, visit_counts, code_factor_t, visit_mix, patient_weight):
    tiles = tile_data[0, 0]
    slots, rows, cols = tiles.shape
    rank = visit_mix.shape[0]
    patients = visit_counts.shape[0]
    n_code, n_pat = lax.axis_size("code"), lax.axis_size("pat")
    half = n_pat // 2
    own = patients // n_code
    code_at, pat_at = lax.axis_index("code"), lax.axis_index("pat")
    meta = jnp.concatenate(
        [
            jnp.pad(
                jnp.transpose(tile_list, (0, 2, 1, 3)),
                ((0, 0), (0, 0), (0, 0), (0, patients - slots)),
            ),
            jnp.broadcast_to(tile_count[0, 0], (1, 1, 1, patients)),
            visit_counts.reshape(1, 1, 1, patients),
        ],
        axis=1,
    )
    place = jnp.stack([code_at, lax.rem(pat_at, 2)]).astype(jnp.int32)
    shape = jax.ShapeDtypeStruct
    square = shape((rank, rank), F32)

    partial = call(
        products_kernel, shape((patients * VBLOCKS, rank, rows), F32), [HBM] * 3,
        (meta, tile_data, code_factor_t),
        [
            pltpu.SMEM(meta.shape, jnp.int32), pltpu.VMEM(tiles.shape, BF16),
            pltpu.VMEM(code_factor_t.shape, F32), pltpu.SemaphoreType.DMA(()),
            pltpu.SemaphoreType.DMA((5,)),
        ],
        vmem=50,
    )
    sent = partial.astype(F16).reshape(n_code, own * VBLOCKS * rank, rows)
    got = lax.all_to_all(sent, "code", 0, 0, tiled=True)
    gram = call(gram_kernel, shape((rank // 2, 2 * rank), F32), [VM], (code_factor_t,))
    products = jnp.sum(got.astype(F32), axis=0).reshape(own * VBLOCKS, rank, rows)

    scales = (0.5, 0.5)
    length = (own * VBLOCKS + own) * rank
    sums, message = call(
        functools.partial(polar_kernel, scales),
        (shape((3 * rank // 2, 2 * rank), F32), shape((length, rows), BF16)),
        [SM, VM, VM, VM, VM], (place, products, visit_mix, patient_weight, gram), flops=5e9,
    )
    quarter = n_code // 2
    other = swap(message, "code", quarter)
    low = rank // 2
    weight_gram, sums = sums[:low], sums[low:]
    parts = [swap(sums, "code", bit) for bit in (1, 2, 3)]
    message = jnp.broadcast_to(jnp.concatenate([message, other])[None], (quarter, 2 * length, rows))
    message, *parts = lax.optimization_barrier((message, *parts))
    sums = plus(sums, parts)
    code_gram, sums = sums[low:], jnp.concatenate([weight_gram, sums[:low]])
    layers = [[z * quarter + i for i in range(quarter)] for z in (0, 1)]
    shared = lax.all_to_all(message, "code", 0, 0, axis_index_groups=layers, tiled=True)
    shared = shared.reshape(n_code, length, rows)
    sums = plus(sums, [swap(sums, "pat", bit) for bit in (2, 4, 6)])
    sums = sums + swap(sums, "pat", 1)
    sums = jnp.concatenate([sums, code_gram])
    mix_new, mix_again, mix_gram, inverse = call(
        mix_kernel, (square,) * 4, [VM] * 4,
        (sums, *(swap_z(sums, high, low) for high, low in ((0, 1), (1, 0), (1, 1)))), flops=5e9,
    )
    block = shape((half, rank, cols), F32)
    keep, send, wgram, weight_new = call(
        numer_kernel,
        (
            block, shape(block.shape, BF16), shape((rank // 2, 2 * rank), F32),
            shape((own, rank), F32),
        ),
        [SM, SM, VM, VM, VM, VM],
        (place, meta, shared, mix_again, inverse, tiles),
        [pltpu.VMEM((n_pat, rank, cols), F32), pltpu.VMEM((patients, rank), F32)], flops=5e9,
    )
    groups = [[core + 2 * i for i in range(half)] for core in (0, 1)]

    def exchange(x):
        return lax.all_to_all(x, "pat", 0, 0, axis_index_groups=groups, tiled=True)

    lanes = 2 * rank
    packed = call(
        pair_kernel, shape((half, cols // lanes + 1, rank, lanes), BF16), [VM] * 4,
        (keep, swap(send, "pat", 1), wgram, swap(wgram, "pat", 1)),
    )
    code = call(
        factor_kernel, shape((half, rank, cols), BF16), [VM, VM], (exchange(packed), mix_gram)
    )
    mine = exchange(code)
    place_scratch = [pltpu.VMEM(mine.shape, F32), pltpu.SemaphoreType.DMA((half,))]
    result = shape((rank, n_pat * cols), F32)
    came = swap(mine, "pat", 1)
    code_new = call(
        functools.partial(place_kernel, False), result, [SM, VM], (place, mine), place_scratch,
        spec=HBM,
    )
    code_new = call(
        functools.partial(place_kernel, True), result, [SM, VM, HBM], (place, came, code_new),
        place_scratch, spec=HBM, alias={2: 0},
    )
    return (code_new, mix_new, weight_new)


def solution(mesh):
    placed = (
        P("pat", "code", None, None, None),
        P("pat", "code", None, None),
        P("pat", "code"),
        P("pat"),
        P(None, "code"),
        P(),
        P("pat", None),
    )
    return jax.shard_map(
        body,
        mesh=mesh,
        in_specs=placed,
        out_specs=(P(None, "code"), P(), P(("pat", "code"), None)),
        check_vma=False,
    )
```

```python
import functools

import jax
import jax.numpy as jnp
from jax import lax
from jax.experimental import pallas as pl
from jax.experimental.pallas import tpu as pltpu
from jax.sharding import PartitionSpec as P

VBLOCKS = 2
NS_STEPS = 8
damping = 0.1
epsilon = 1e-06
F32, BF16, F16 = jnp.float32, jnp.bfloat16, jnp.float16
VM = pl.BlockSpec(memory_space=pltpu.VMEM)
HBM = pl.BlockSpec(memory_space=pl.ANY)
SM = pl.BlockSpec(memory_space=pltpu.SMEM)
MIB = 1024 * 1024


def mm(a, b, dims=((1,), (0,))):
    return lax.dot_general(
        a, b, (dims, ((), ())), precision=lax.Precision.HIGHEST, preferred_element_type=F32
    )


def mm16(a, b, dims=((1,), (0,))):
    return lax.dot_general(a, b, (dims, ((), ())), preferred_element_type=F32)


NT = ((1,), (1,))
TN = ((0,), (0,))


def split(x):
    high = x.astype(BF16)
    return high, (x - high.astype(F32)).astype(BF16)


def mm3(a, b, dims=((1,), (0,))):
    return mm16(a[0], b[0], dims) + (mm16(a[0], b[1], dims) + mm16(a[1], b[0], dims))


def fold(x):
    half = x.shape[1] // 2
    return x[:, :half] + x[:, half:]


def times2(x, y):
    return [[x[i][0] * y[0][j] + x[i][1] * y[1][j] for j in (0, 1)] for i in (0, 1)]


def dot4(x, y):
    return (x[0] * y[0] + x[1] * y[1]) + (x[2] * y[2] + x[3] * y[3])


def inverse4(p):
    a = [[p[1][1], -p[0][1]], [-p[0][1], p[0][0]]]
    det = p[0][0] * p[1][1] - p[0][1] * p[0][1]
    b = [[p[0][2], p[0][3]], [p[1][2], p[1][3]]]
    t = times2(a, b)
    s00 = det * p[2][2] - (b[0][0] * t[0][0] + b[1][0] * t[1][0])
    s01 = det * p[2][3] - (b[0][0] * t[0][1] + b[1][0] * t[1][1])
    s11 = det * p[3][3] - (b[0][1] * t[0][1] + b[1][1] * t[1][1])
    over = 1.0 / (s00 * s11 - s01 * s01)
    over_det = 1.0 / det
    flip = [[s11, -s01], [-s01, s00]]
    u = times2(t, flip)
    v = times2(u, [[t[0][0], t[1][0]], [t[0][1], t[1][1]]])
    side = [[u[i][j] * over for j in (0, 1)] for i in (0, 1)]
    last = [[flip[i][j] * (det * over) for j in (0, 1)] for i in (0, 1)]
    first = [
        [a[i][j] * over_det + v[i][j] * (over * over_det) for j in (0, 1)] for i in (0, 1)
    ]
    return [
        [first[0][0], first[0][1], -side[0][0], -side[0][1]],
        [first[0][1], first[1][1], -side[1][0], -side[1][1]],
        [-side[0][0], -side[1][0], last[0][0], last[0][1]],
        [-side[0][1], -side[1][1], last[0][1], last[1][1]],
    ]


def halves(x):
    low = x.shape[0] // 2
    return jnp.concatenate([x[:low], x[low:]], axis=1)


def damped_inverse(gram):
    size = gram.shape[0]
    eye = lax.broadcasted_iota(jnp.int32, (size, size), 0) == lax.broadcasted_iota(
        jnp.int32, (size, size), 1
    )
    scale = size / jnp.sum(jnp.where(eye, gram, 0.0), keepdims=True)
    work = jnp.concatenate(
        [gram * scale + jnp.where(eye, damping, 0.0), eye.astype(F32)], axis=1
    )
    lanes = 2 * size
    four = range(4)
    blocks = [work[i : i + 8] for i in range(0, size, 8)]
    fresh = []
    for step in range(len(blocks)):
        j = 8 * step
        rows = [blocks[step][i : i + 1] for i in range(8)]

        def entry(i, k):
            return jnp.broadcast_to(rows[i][:, j + k : j + k + 1], (1, lanes))

        a = inverse4([[entry(i, k) if k >= i else None for k in four] for i in four])
        b = [[entry(i, 4 + k) for i in four] for k in four]
        t = [[dot4(a[i], b[k]) for i in four] for k in four]
        d = inverse4(
            [
                [entry(4 + i, 4 + k) - dot4(b[i], t[k]) if k >= i else None for k in four]
                for i in four
            ]
        )
        top = [dot4(a[i], rows[:4]) for i in four]
        rest = [rows[4 + i] - dot4(b[i], top) for i in four]
        low = [dot4(d[i], rest) for i in four]
        new = [top[i] - dot4([t[k][i] for k in four], low) for i in four] + low
        fresh += new
        for m in range(step + 1, len(blocks)):
            block = blocks[m]
            part = [block[:, j + k : j + k + 1] * new[k] for k in range(8)]
            blocks[m] = block - (
                ((part[0] + part[1]) + (part[2] + part[3]))
                + ((part[4] + part[5]) + (part[6] + part[7]))
            )
    raw = jnp.concatenate(blocks, axis=0)[:, size:]
    fresh = jnp.concatenate(fresh, axis=0)[:, size:]
    return scale * mm(raw, fresh, TN)


def live_rows(t, meta_ref, tile_rows):
    k, b, g = meta_ref[0, 0, 0, t], meta_ref[0, 1, 0, t], meta_ref[0, 2, 0, t]
    kept = jnp.where(t < meta_ref[0, 3, 0, 0], meta_ref[0, 4, 0, k] - tile_rows * b, 0)
    return k, b, g, kept


def products_kernel(
    meta_hbm, tile_hbm, code_hbm, out_ref, meta_ref, tile_ref, code_ref, small_sem, sems
):
    slots, rows, cols = tile_ref.shape
    rank = code_ref.shape[0]
    parts = sems.shape[0] - 1
    each = slots // parts
    small = pltpu.make_async_copy(meta_hbm, meta_ref, small_sem)
    small.start()
    code_copy = pltpu.make_async_copy(code_hbm, code_ref, sems.at[parts])
    code_copy.start()
    copies = []
    for i in range(parts):
        at = pl.ds(i * each, each)
        copies.append(pltpu.make_async_copy(tile_hbm.at[0, 0, at], tile_ref.at[at], sems.at[i]))
        copies[-1].start()
    out_ref[...] = jnp.zeros(out_ref.shape, F32)
    lane = lax.broadcasted_iota(jnp.int32, (rank, rows), 1)
    small.wait()
    code_copy.wait()
    for t in range(slots):
        if t % each == 0:
            copies[t // each].wait()
        k, b, g, kept = live_rows(t, meta_ref, rows)
        codes = code_ref[:, pl.ds(pl.multiple_of(g * cols, cols), cols)].astype(BF16)
        part = mm16(codes, tile_ref[t], NT)
        out_ref[k * VBLOCKS + b] += jnp.where(lane < kept, part, 0.0)


def gram_kernel(code_ref, out_ref):
    high, low = split(code_ref[...])
    cross = mm16(high, low, NT)
    out_ref[...] = halves(mm16(high, high, NT) + cross + cross.T)


def polar_kernel(
    scales, at_ref, prod_ref, mix_ref, weight_ref, gram_ref, sums_ref, out_ref
):
    segs, rank, rows = prod_ref.shape
    own = segs // VBLOCKS
    eye = lax.broadcasted_iota(jnp.int32, (rank, rank), 0) == lax.broadcasted_iota(
        jnp.int32, (rank, rank), 1
    )
    prods, zs, weights = [], [], []
    for j in range(own):
        prods.append(
            split(jnp.concatenate([prod_ref[VBLOCKS * j + b] for b in range(VBLOCKS)], axis=1))
        )
        weights.append(weight_ref[pl.ds(at_ref[0] * own + j, 1), :])
        target = mm3(split(mix_ref[...] * weights[j]), prods[j])
        zs.append(target / jnp.sqrt(jnp.sum(target * target, keepdims=True) + epsilon))
    zs = [split(z) for z in zs]
    for _ in range(NS_STEPS):
        factors = [split(jnp.where(eye, 1.5, 0.0) - 0.5 * mm3(z, z, NT)) for z in zs]
        zs = [split(mm3(q, z)) for q, z in zip(factors, zs)]
    pieces = [z[0][:, b * rows : (b + 1) * rows] for z in zs for b in range(VBLOCKS)]
    numer = jnp.zeros((rank, rank), F32)
    for z, p, weight in zip(zs, prods, weights):
        projected = mm3(z, p, NT)
        numer += projected * weight
        pieces.append(jnp.concatenate(split(projected), axis=1))
    low = rank // 2
    weight = weight_ref[...]
    sums_ref[:low, :] = halves(mm(weight, weight, TN)) * scales[0]
    sums_ref[low:rank, :] = halves(numer)
    sums_ref[rank:, :] = gram_ref[...] * scales[1]
    for i, piece in enumerate(pieces):
        out_ref[i * rank : (i + 1) * rank, :] = piece


def whole(x):
    rank = x.shape[1] // 2
    return jnp.concatenate([x[:, :rank], x[:, rank:]], axis=0)


def mix_kernel(a_ref, b_ref, c_ref, d_ref, mix_ref, again_ref, mgram_ref, inverse_ref):
    sums = (a_ref[...] + b_ref[...]) + (c_ref[...] + d_ref[...])
    rank = mix_ref.shape[0]
    low = rank // 2
    weight_gram, code_gram = whole(sums[:low]), whole(sums[rank:])
    mix = mm(whole(sums[low:rank]), damped_inverse(code_gram * weight_gram))
    again_ref[...] = mix
    mix_ref[...] = mix
    mix_gram = mm(mix, mix, TN)
    mgram_ref[...] = mix_gram
    inverse_ref[...] = damped_inverse(mix_gram * code_gram)


def numer_kernel(
    place_ref, meta_ref, got_ref, mix_ref, inverse_ref, tile_ref,
    keep_ref, send_ref, wgram_ref, own_ref, acc_ref, weight_ref,
):
    acc_ref[...] = jnp.zeros(acc_ref.shape, F32)
    slots, rows, cols = tile_ref.shape
    sources = got_ref.shape[0]
    rank = mix_ref.shape[0]
    own = own_ref.shape[0]
    first = own * VBLOCKS * rank
    layers = 2
    z_at = lax.div(place_ref[0], sources // layers)

    def source(d):
        x_at, layer = lax.rem(d, sources // layers), lax.div(d, sources // layers)
        return x_at * layers + jnp.where(layer == z_at, 0, 1)

    mix = mix_ref[...]
    twice = jnp.concatenate([mix, mix], axis=1)
    terms = []
    for d in range(sources):
        for j in range(own):
            at = first + j * rank
            part = got_ref[d, at : at + rank, :].astype(F32) * twice
            terms.append(jnp.sum(part, axis=0, keepdims=True))
    weight = jnp.maximum(mm(fold(jnp.concatenate(terms, axis=0)), inverse_ref[...]), 0.0)
    weight_ref[...] = weight
    for j in range(own):
        own_ref[j : j + 1, :] = weight_ref[pl.ds(source(place_ref[0]) * own + j, 1), :]
    wgram_ref[...] = halves(mm(weight, weight, TN))
    lane = lax.broadcasted_iota(jnp.int32, (rank, rows), 1)
    for t in range(slots):
        k, b, g, kept = live_rows(t, meta_ref, rows)
        d, j = source(lax.div(k, own)), lax.rem(k, own)
        both = jnp.concatenate(split(mix * weight_ref[pl.ds(d * own + j, 1), :]), axis=0)
        at = pl.multiple_of((j * VBLOCKS + b) * rank, rank)
        polar = got_ref[d, pl.ds(at, rank), :]
        spread = mm16(both, jnp.concatenate([polar, polar], axis=0), TN)
        spread = jnp.where(lane < kept, spread, 0.0).astype(BF16)
        acc_ref[g] += mm16(spread, tile_ref[t])
    parity = place_ref[1]
    for j in range(keep_ref.shape[0]):
        keep_ref[j] = acc_ref[2 * j + parity]
        send_ref[j] = acc_ref[2 * j + 1 - parity].astype(BF16)


def pair_kernel(keep_ref, came_ref, gram_a, gram_b, out_ref):
    low, lanes = gram_a.shape
    slabs = keep_ref.shape[2] // lanes
    piece = jnp.concatenate(split(gram_a[...] + gram_b[...]), axis=0)
    for j in range(keep_ref.shape[0]):
        both = (keep_ref[j] + came_ref[j]).astype(BF16)
        for i in range(slabs):
            out_ref[j, i] = both[:, i * lanes : (i + 1) * lanes]
        out_ref[j, slabs] = piece


def factor_kernel(got_ref, mgram_ref, out_ref):
    sources, slabs = got_ref.shape[0], got_ref.shape[1] - 1
    sums = []
    for i in range(slabs + 1):
        total = got_ref[0, i].astype(F32)
        for d in range(1, sources):
            total += got_ref[d, i].astype(F32)
        sums.append(total)
    low = sums[slabs].shape[0] // 2
    gram = whole(sums[slabs][:low] + sums[slabs][low:])
    inverse = damped_inverse(mgram_ref[...] * gram)
    code = jnp.maximum(mm(inverse, jnp.concatenate(sums[:slabs], axis=1)), 0.0).astype(BF16)
    for d in range(sources):
        out_ref[d] = code


def place_kernel(flip, place_ref, from_ref, *refs):
    out_hbm, wide_ref, sems = refs[-3:]
    parity = place_ref[1] if not flip else 1 - place_ref[1]
    cols = from_ref.shape[2]
    copies = []
    for j in range(from_ref.shape[0]):
        wide_ref[j] = from_ref[j].astype(F32)
        at = pl.multiple_of((2 * j + parity) * cols, cols)
        copies.append(
            pltpu.make_async_copy(wide_ref.at[j], out_hbm.at[:, pl.ds(at, cols)], sems.at[j])
        )
        copies[-1].start()
    for copy in copies:
        copy.wait()


def call(kernel, outs, specs, args, scratch=(), flops=1e9, spec=VM, alias=None, vmem=16):
    many = isinstance(outs, tuple)
    return pl.pallas_call(
        kernel,
        out_shape=outs,
        in_specs=specs,
        out_specs=(spec,) * len(outs) if many else spec,
        input_output_aliases=alias or {},
        scratch_shapes=scratch,
        compiler_params=pltpu.CompilerParams(vmem_limit_bytes=vmem * MIB),
        cost_estimate=pl.CostEstimate(flops=int(flops), bytes_accessed=65536, transcendentals=0),
    )(*args)


def swap(x, axis, bit):
    size = lax.axis_size(axis)
    return lax.ppermute(x, axis, [(i, i ^ bit) for i in range(size)])


def swap_z(x, high, low):
    n_pat, n_code = lax.axis_size("pat"), lax.axis_size("code")
    pairs = [
        (p * n_code + c, (p ^ (high * n_pat // 2)) * n_code + (c ^ (low * n_code // 2)))
        for p in range(n_pat)
        for c in range(n_code)
    ]
    return lax.ppermute(x, ("pat", "code"), pairs)


def plus(x, parts):
    for part in parts:
        x = x + part
    return x


def body(tile_data, tile_list, tile_count, visit_counts, code_factor_t, visit_mix, patient_weight):
    tiles = tile_data[0, 0]
    slots, rows, cols = tiles.shape
    rank = visit_mix.shape[0]
    patients = visit_counts.shape[0]
    n_code, n_pat = lax.axis_size("code"), lax.axis_size("pat")
    half = n_pat // 2
    own = patients // n_code
    code_at, pat_at = lax.axis_index("code"), lax.axis_index("pat")
    meta = jnp.concatenate(
        [
            jnp.pad(
                jnp.transpose(tile_list, (0, 2, 1, 3)),
                ((0, 0), (0, 0), (0, 0), (0, patients - slots)),
            ),
            jnp.broadcast_to(tile_count[0, 0], (1, 1, 1, patients)),
            visit_counts.reshape(1, 1, 1, patients),
        ],
        axis=1,
    )
    place = jnp.stack([code_at, lax.rem(pat_at, 2)]).astype(jnp.int32)
    shape = jax.ShapeDtypeStruct
    square = shape((rank, rank), F32)

    partial = call(
        products_kernel, shape((patients * VBLOCKS, rank, rows), F32), [HBM] * 3,
        (meta, tile_data, code_factor_t),
        [
            pltpu.SMEM(meta.shape, jnp.int32), pltpu.VMEM(tiles.shape, BF16),
            pltpu.VMEM(code_factor_t.shape, F32), pltpu.SemaphoreType.DMA(()),
            pltpu.SemaphoreType.DMA((3,)),
        ],
        vmem=50,
    )
    sent = partial.astype(F16).reshape(n_code, own * VBLOCKS * rank, rows)
    got = lax.all_to_all(sent, "code", 0, 0, tiled=True)
    gram = call(gram_kernel, shape((rank // 2, 2 * rank), F32), [VM], (code_factor_t,))
    products = jnp.sum(got.astype(F32), axis=0).reshape(own * VBLOCKS, rank, rows)

    scales = (0.5, 0.5)
    length = (own * VBLOCKS + own) * rank
    sums, message = call(
        functools.partial(polar_kernel, scales),
        (shape((3 * rank // 2, 2 * rank), F32), shape((length, rows), BF16)),
        [SM, VM, VM, VM, VM], (place, products, visit_mix, patient_weight, gram), flops=5e9,
    )
    quarter = n_code // 2
    other = swap(message, "code", quarter)
    low = rank // 2
    weight_gram, sums = sums[:low], sums[low:]
    parts = [swap(sums, "code", bit) for bit in (1, 2, 3)]
    message = jnp.broadcast_to(jnp.concatenate([message, other])[None], (quarter, 2 * length, rows))
    message, *parts = lax.optimization_barrier((message, *parts))
    sums = plus(sums, parts)
    code_gram, sums = sums[low:], jnp.concatenate([weight_gram, sums[:low]])
    layers = [[z * quarter + i for i in range(quarter)] for z in (0, 1)]
    shared = lax.all_to_all(message, "code", 0, 0, axis_index_groups=layers, tiled=True)
    shared = shared.reshape(n_code, length, rows)
    sums = plus(sums, [swap(sums, "pat", bit) for bit in (2, 4, 6)])
    sums = sums + swap(sums, "pat", 1)
    sums = jnp.concatenate([sums, code_gram])
    mix_new, mix_again, mix_gram, inverse = call(
        mix_kernel, (square,) * 4, [VM] * 4,
        (sums, *(swap_z(sums, high, low) for high, low in ((0, 1), (1, 0), (1, 1)))), flops=5e9,
    )
    block = shape((half, rank, cols), F32)
    keep, send, wgram, weight_new = call(
        numer_kernel,
        (
            block, shape(block.shape, BF16), shape((rank // 2, 2 * rank), F32),
            shape((own, rank), F32),
        ),
        [SM, SM, VM, VM, VM, VM],
        (place, meta, shared, mix_again, inverse, tiles),
        [pltpu.VMEM((n_pat, rank, cols), F32), pltpu.VMEM((patients, rank), F32)], flops=5e9,
    )
    groups = [[core + 2 * i for i in range(half)] for core in (0, 1)]

    def exchange(x):
        return lax.all_to_all(x, "pat", 0, 0, axis_index_groups=groups, tiled=True)

    lanes = 2 * rank
    packed = call(
        pair_kernel, shape((half, cols // lanes + 1, rank, lanes), BF16), [VM] * 4,
        (keep, swap(send, "pat", 1), wgram, swap(wgram, "pat", 1)),
    )
    code = call(
        factor_kernel, shape((half, rank, cols), BF16), [VM, VM], (exchange(packed), mix_gram)
    )
    mine = exchange(code)
    place_scratch = [pltpu.VMEM(mine.shape, F32), pltpu.SemaphoreType.DMA((half,))]
    result = shape((rank, n_pat * cols), F32)
    came = swap(mine, "pat", 1)
    code_new = call(
        functools.partial(place_kernel, False), result, [SM, VM], (place, mine), place_scratch,
        spec=HBM,
    )
    code_new = call(
        functools.partial(place_kernel, True), result, [SM, VM, HBM], (place, came, code_new),
        place_scratch, spec=HBM, alias={2: 0},
    )
    return (code_new, mix_new, weight_new)


def solution(mesh):
    placed = (
        P("pat", "code", None, None, None),
        P("pat", "code", None, None),
        P("pat", "code"),
        P("pat"),
        P(None, "code"),
        P(),
        P("pat", None),
    )
    return jax.shard_map(
        body,
        mesh=mesh,
        in_specs=placed,
        out_specs=(P(None, "code"), P(), P(("pat", "code"), None)),
        check_vma=False,
    )
```
